32 devices in a mesh: ctx: 16 (over z, y, core), wa: 2 (over x).
Axes of the slice: x: 2, y: 2, z: 4, core: 2. Of those that a mesh axis runs over, the one named last changes fastest.
Arguments:
- ids: int32 [32768], P('ctx'), may hold values from 0 to 274
- targets: int32 [32768], P('ctx'), may hold values from 0 to 274
- doc_lengths: int32 [4], replicated, may hold values from 1 to 16384, 32768 in all
- block_of: int32 [16], replicated, may hold values from 0 to 15, each once
- embed: bfloat16 [275, 100], replicated, may hold values from -6 to 6
- w_in: bfloat16 [100, 4, 2048], P(None, None, 'wa'), may hold values from -0.625 to 0.625
- b_in: float32 [4, 2048], P(None, 'wa'), may hold values from -6.5 to 12.5
- w_out: bfloat16 [2048, 275], P('wa'), may hold values from -0.5 to 0.5
- b_out: float32 [275], replicated, may hold values from -3 to 3
Outputs:
- hidden_out: bfloat16 [32768, 2048], P('ctx', 'wa')
- loss: float32 [], replicated
- grad_embed: float32 [275, 100], replicated
- grad_w_in: float32 [100, 4, 2048], P(None, None, 'wa')
- grad_b_in: float32 [4, 2048], P(None, 'wa')
- grad_w_out: float32 [2048, 275], P('wa')
- grad_b_out: float32 [275], replicated
The draws below stay inside these ranges and needn't reach their ends.
Inputs may be any that keep to these rules, and one draw needn't show every extreme that they name: `doc_lengths`: the documents are laid end to end from position 0 and fill the stream. Device d of ctx holds stream block block_of[d]; each block once.
All inputs are finite; a program needn't handle non-finite values.
Results may differ from the reference program's by a relative error of at most 0.0019.
Values may be sent and summed in bfloat16 or wider, within the bound.
No kernel may reach another device: no remote copies, remote signals or barrier semaphores. Data moves between devices by JAX's collectives and lax.ppermute only.
A program may use at most 192 MiB of HBM per device.

```python
import math
import jax
import jax.numpy as jnp
import numpy as np
from jax import lax

EMB = 100
H = 2048
VOCAB = 275
GATES = 4
TOK_DEV = 2048
TOKENS = 32768
DOCS = 4
DOC_MOST = 16384
N_CTX = 16


def draw_b_in(key, part):
    key_slow, key_other = jax.random.split(key, 2)
    slowness = jax.random.uniform(key_slow, (H,), jnp.float32)
    others = jnp.clip(0.5 * jax.random.normal(key_other, (GATES, H), jnp.float32), -1.5, 1.5)
    forget_row = 9.0 * slowness + others[1]
    input_row = -5.0 * slowness + others[0]
    return jnp.stack([input_row, forget_row, others[2], others[3]], axis=0)


def touch_ends(result, rng, least, high):
    index_at = [jax.random.randint(jax.random.fold_in(rng, axis), (), 0, length) for axis, length in enumerate(result.shape)]
    main_axis = result.shape.index(max(result.shape))
    neighbour = index_at[:main_axis] + [(index_at[main_axis] + 1) % result.shape[main_axis]] + index_at[main_axis + 1:]
    return result.at[tuple(index_at)].set(least).at[tuple(neighbour)].set(high)


def block_levels(rng, shape, shards, smallest, top_value):
    gain, own = 1.0, jax.random.fold_in(rng, 6)
    for dim, shards_of in shards:
        steps = jnp.exp(jax.random.uniform(jax.random.fold_in(own, dim), (shards_of,), jnp.float32, smallest / len(shards), top_value / len(shards)))
        gain = gain * jnp.repeat(steps, shape[dim] // shards_of).reshape([-1 if axis == dim else 1 for axis in range(len(shape))])
    return gain


def rank_bounds(number_of, slope):
    portions = [(1 << 20) // math.isqrt(rank ** slope) + 1 for rank in range(1, number_of + 1)]
    width = 1 + sum(portions) // (1 << 30)
    return np.cumsum(np.array([max(1, weight // width) for weight in portions]))


def ranked(own_key, shape, amount, skew):
    grid = rank_bounds(amount, skew)
    pick = jax.random.randint(jax.random.fold_in(own_key, 1), shape, 0, int(grid[amount - 1]))
    standing = jnp.searchsorted(jnp.asarray(grid, jnp.int32), pick, side="right")
    return jax.random.permutation(jax.random.fold_in(own_key, 2), amount)[standing].astype(jnp.int32)


def split_up(amount, total, reach, lean):
    weights = [(1 << 20) // math.isqrt(grade ** lean) + 1 for grade in range(2, amount + 1)]
    surplus, given = total - reach - (amount - 1), [1] * (amount - 1)
    while surplus > 0:
        movable = [i for i in range(amount - 1) if given[i] < reach]
        pool, budget = sum([weights[i] for i in movable]), surplus
        for i in movable:
            more = min(reach - given[i], max(1, budget * weights[i] // pool), surplus)
            given[i] = given[i] + more
            surplus = surplus - more
    return np.array([reach] + given)


def ragged_sizes(rng, count, total, most, skew):
    if count == 2:
        one = jax.random.randint(rng, (), max(1, total - most), min(most, total - 1) + 1)
        return jnp.stack([one, total - one])
    lengths = jnp.asarray(split_up(count, total, most, skew), jnp.int32)
    pairs = (count - 1) // 2
    donor, taker = lengths[1:1 + 2 * pairs:2], lengths[2:2 + 2 * pairs:2]
    margin = jnp.minimum(donor - 1, most - taker)
    moved = jax.random.randint(jax.random.fold_in(rng, 1), (pairs,), 0, 1 << 20) % (margin + 1)
    lengths = lengths.at[1:1 + 2 * pairs:2].set(donor - moved).at[2:2 + 2 * pairs:2].set(taker + moved)
    return lengths[jax.random.permutation(jax.random.fold_in(rng, 2), count)]


def scatter_about(key, dims, spread, bound, pieces=(), held_as=jnp.bfloat16):
    drawn = spread * jax.random.normal(key, dims, jnp.float32)
    if pieces:
        drawn = drawn * block_levels(key, dims, pieces, -0.22, 0.18)
    return jnp.clip(drawn, -bound, bound).astype(held_as)


def setup_inputs(seed: int = 0) -> dict:
    key_of = jax.random.split(jax.random.key(seed), 10)
    ids = touch_ends(ranked(key_of[0], (TOKENS,), VOCAB, 2), jax.random.fold_in(key_of[0], 3), 0, VOCAB - 1).astype(jnp.int32)
    targets = touch_ends(ranked(key_of[1], (TOKENS,), VOCAB, 2), jax.random.fold_in(key_of[1], 3), 0, VOCAB - 1).astype(jnp.int32)
    doc_lengths = ragged_sizes(key_of[2], DOCS, TOKENS, DOC_MOST, 2).astype(jnp.int32)
    block_of = jax.random.permutation(key_of[3], N_CTX).astype(jnp.int32)
    embed = scatter_about(key_of[4], (VOCAB, EMB), 1.0, 6.0)
    w_in = scatter_about(key_of[5], (EMB, GATES, H), EMB ** -0.5, 0.625, ((2, 2),))
    b_in = draw_b_in(jax.random.fold_in(key_of[9], 71), 0)
    w_out = scatter_about(key_of[7], (H, VOCAB), (H // 16) ** -0.5, 0.5, ((0, 2),))
    b_out = scatter_about(key_of[8], (VOCAB,), 0.5, 3.0, (), jnp.float32)
    return {"ids": ids, "targets": targets, "doc_lengths": doc_lengths, "block_of": block_of, "embed": embed, "w_in": w_in, "b_in": b_in, "w_out": w_out, "b_out": b_out}


@jax.custom_vjp
def low(v):
    return lax.optimization_barrier(v.astype(jnp.bfloat16)).astype(jnp.float32)

@jax.custom_vjp
def low_back(v):
    return v

def low_keep(v):
    return (low(v), None)

def low_pass(kept, grad):
    return (grad,)

def back_keep(v):
    return (v, None)

def back_low(kept, grad):
    return (low(grad),)
low.defvjp(low_keep, low_pass)
low_back.defvjp(back_keep, back_low)

def combine(earlier, later):
    return (earlier[0] * later[0], later[0] * earlier[1] + later[1])

def reference(ids, targets, doc_lengths, block_of, embed, w_in, b_in, w_out, b_out):
    highest = lax.Precision.HIGHEST
    order = jnp.argsort(block_of).astype(jnp.int32)
    ids_stream = ids.reshape(N_CTX, TOK_DEV)[order]
    tgt_stream = targets.reshape(N_CTX, TOK_DEV)[order]
    starts = (jnp.cumsum(doc_lengths) - doc_lengths).astype(jnp.int32)
    resets = jnp.zeros((TOKENS,), jnp.float32).at[starts].set(1.0).reshape(N_CTX, TOK_DEV)
    params = (embed.astype(jnp.float32), w_in.astype(jnp.float32), b_in, w_out.astype(jnp.float32), b_out)

    def forward(embed_f, w_in_f, b_in_f, w_out_f, b_out_f):

        def step(cell_prev, inputs):
            ids_blk, tgt_blk, reset_blk = inputs
            feats = embed_f[ids_blk]
            gates = jnp.einsum('te,egh->tgh', feats, w_in_f, precision=highest) + b_in_f[None]
            gates = low_back(gates)
            in_gate = jax.nn.sigmoid(gates[:, 0])
            forget = jax.nn.sigmoid(gates[:, 1] + 3.0)
            candidate = jnp.tanh(gates[:, 2])
            out_gate = jax.nn.sigmoid(gates[:, 3])
            decay = forget * (1.0 - reset_blk)[:, None]
            prods, sums = lax.associative_scan(combine, (decay, in_gate * candidate), axis=0)
            cells = sums + prods * cell_prev[None]
            hidden_low = low(out_gate * jnp.tanh(cells))
            logits = low_back(jnp.dot(hidden_low, w_out_f, precision=highest) + b_out_f)
            log_total = jax.nn.logsumexp(logits, axis=1)
            picked = jnp.take_along_axis(logits, tgt_blk[:, None], axis=1)[:, 0]
            return (cells[-1], (jnp.sum(log_total - picked), hidden_low))
        start_cell = jnp.zeros((H,), jnp.float32)
        last_cell, (losses, hiddens) = lax.scan(jax.checkpoint(step), start_cell, (ids_stream, tgt_stream, resets))
        return (jnp.sum(losses) / TOKENS, hiddens)
    loss, back_fn, hiddens = jax.vjp(forward, *params, has_aux=True)
    grads = back_fn(jnp.ones((), jnp.float32))
    hidden_out = hiddens[block_of].reshape(TOKENS, H).astype(jnp.bfloat16)
    return (hidden_out, loss, grads[0], grads[1], grads[2], grads[3], grads[4])
```

```python
import functools

import jax
import jax.numpy as jnp
from jax import lax
from jax.experimental import pallas as pl
from jax.experimental.pallas import tpu as pltpu
from jax.sharding import PartitionSpec as P

SUB = 8
LANE = 128
WBLK = 256
VMEM = 52 * 1024 * 1024
RESET_PULL = -30000.0
F32 = jnp.float32
BF16 = jnp.bfloat16


def ceil_to(value, step):
    return -(-value // step) * step


def params(steps=1):
    return pltpu.CompilerParams(dimension_semantics=("arbitrary",) * steps, vmem_limit_bytes=VMEM)


def whole(shape):
    zeros = (0,) * len(shape)
    return pl.BlockSpec(shape, lambda *_: zeros)


def smem():
    return pl.BlockSpec(memory_space=pltpu.SMEM)


def stages_of(count):
    stages, bit, number = [], 1, 0
    while bit < count:
        if number >= 2 and bit * 2 < count:
            stages.append([bit, 2 * bit, 3 * bit])
            bit *= 4
        else:
            stages.append([bit])
            bit *= 2
        number += 1
    return stages


def swap(value, axis, mask):
    count = lax.axis_size(axis)
    return lax.ppermute(value, axis, [(k, k ^ mask) for k in range(count)])


def gather_xor(value, axis):
    out = value[None]
    for masks in stages_of(lax.axis_size(axis)):
        out = jnp.concatenate([out] + [swap(out, axis, mask) for mask in masks], axis=0)
    return out


def slot_of(xor_index, count):
    place, size, bit = 0, count, 1
    for masks in stages_of(count):
        ways = len(masks) + 1
        size = size // ways
        place = place + ((xor_index // bit) % ways) * size
        bit = bit * ways
    return place


def scatter_sum(chunks, axis):
    count = lax.axis_size(axis)
    value = chunks
    for masks in stages_of(count):
        ways = len(masks) + 1
        value = value.reshape((ways, value.shape[0] // ways) + value.shape[1:])
        moved = [swap(value[k + 1], axis, mask) for k, mask in enumerate(masks)]
        total = value[0]
        for part in moved:
            total = total + part
        value = total
    return value[0]


def gather_chunks(chunk, axis):
    value = chunk[None]
    for masks in reversed(stages_of(lax.axis_size(axis))):
        value = jnp.concatenate([value] + [swap(value, axis, mask) for mask in masks], axis=0)
    return value


def feats_kernel(starts, base, ids, table, feats, onehot):
    vocab, toks = onehot.shape
    seg = toks // SUB
    hits = lax.broadcasted_iota(jnp.int32, (vocab, toks), 0) == ids[...]
    table_t = hits.astype(F32).astype(BF16)
    onehot[...] = table_t
    rows = lax.dot_general(table_t, table[...], (((0,), (0,)), ((), ())), preferred_element_type=F32)
    width = rows.shape[1]
    row = lax.broadcasted_iota(jnp.int32, (toks, width), 0)
    col = lax.broadcasted_iota(jnp.int32, (toks, width), 1)
    position = base[0] + (row % SUB) * seg + row // SUB
    hit = position == starts[0]
    for k in range(1, starts.shape[0]):
        hit = hit | (position == starts[k])
    mark = jnp.where(hit & (col == 103), 1.0, 0.0)
    feats[...] = (rows + mark).astype(BF16)


def gate_kernel(feats, w, decay, source, out, seg_p, seg_s, block_ps):
    toks = feats.shape[0]
    rows = 128
    width = decay.shape[1]

    def chunk(k, carry):
        prod, total = carry
        at = pl.multiple_of(k * rows, rows)
        fe = feats[pl.ds(at, rows), :]
        gate = [jnp.dot(fe, w[g], preferred_element_type=F32) for g in range(4)]
        in_gate = 0.5 * jnp.tanh(gate[0]) + 0.5
        forget = 0.5 * jnp.tanh(gate[1]) + 0.5
        cand = jnp.tanh(gate[2])
        src = in_gate * cand
        decay[pl.ds(at, rows), :] = forget
        source[pl.ds(at, rows), :] = src
        out[pl.ds(at, rows), :] = 0.5 * jnp.tanh(gate[3]) + 0.5
        for r in range(rows // SUB):
            d = forget[r * SUB:(r + 1) * SUB]
            total = d * total + src[r * SUB:(r + 1) * SUB]
            prod = prod * d
        return prod, total

    prod, total = lax.fori_loop(
        0, toks // rows, chunk, (jnp.ones((SUB, width), F32), jnp.zeros((SUB, width), F32))
    )
    seg_p[...] = prod
    seg_s[...] = total
    p_all, s_all = prod[0:1], total[0:1]
    for s in range(1, SUB):
        s_all = prod[s:s + 1] * s_all + total[s:s + 1]
        p_all = prod[s:s + 1] * p_all
    block_ps[0:1, :] = p_all
    block_ps[1:2, :] = s_all


def cell_kernel(
    order, meta, d_o, x_o, o_o, d_x, x_x, o_x, ps_all, sp_o, ss_o, sp_x, ss_x, wt_o, wt_x, bias, tgt,
    prev, hid, lgrad, src, go, h_seg, h_blk, b_grad, loss,
    c_o, c_x, pcum, hs_o, hs_x, hb_o, hb_x, q, u, hg, gacc, *, total_tokens,
):
    k = pl.program_id(0)
    steps = hid.shape[1]
    rows = steps * SUB
    width = d_o.shape[1]
    vocab = wt_o.shape[0]

    @pl.when(k == 0)
    def _():
        me, own = meta[0], meta[1]

        def earlier(b, c):
            pair = ps_all[order[b] ^ me]
            return pair[0:1] * c + pair[1:2]

        c = lax.fori_loop(0, own, earlier, jnp.zeros((1, ps_all.shape[2]), F32))
        for ref, sp, ss, at in ((c_o, sp_o, ss_o, 0), (c_x, sp_x, ss_x, width)):
            one = c[:, at:at + ref.shape[1]]
            for s in range(SUB):
                ref[s:s + 1, :] = one
                one = sp[s:s + 1, :] * one + ss[s:s + 1, :]
        pcum[...] = jnp.ones_like(pcum)
        h_seg[...] = jnp.zeros_like(h_seg)
        gacc[...] = jnp.zeros_like(gacc)
        loss[...] = jnp.zeros_like(loss)

    def spread(ref, r, value):
        for b in range(ref.shape[0]):
            ref[b, pl.ds(r, SUB, stride=steps), :] = value[:, b * LANE:(b + 1) * LANE]

    def own_step(r, c):
        at = pl.multiple_of(r * SUB, SUB)
        prev[pl.ds(at, SUB), :] = c
        c = d_o[pl.ds(at, SUB), :] * c + x_o[pl.ds(at, SUB), :]
        t = jnp.tanh(c)
        o = o_o[pl.ds(at, SUB), :]
        h = o * t
        q[pl.ds(at, SUB), :] = o - h * t
        u[pl.ds(at, SUB), :] = h - h * o
        spread(hs_o, r, h)
        return c

    def other_step(r, c):
        at = pl.multiple_of(r * SUB, SUB)
        c = d_x[pl.ds(at, SUB), :] * c + x_x[pl.ds(at, SUB), :]
        spread(hs_x, r, o_x[pl.ds(at, SUB), :] * jnp.tanh(c))
        return c

    c_o[...] = lax.fori_loop(0, steps, own_step, c_o[...], unroll=4)
    c_x[...] = lax.fori_loop(0, steps, other_step, c_x[...], unroll=4)
    for low, high in ((hb_o, hs_o), (hb_x, hs_x)):
        for b in range(high.shape[0]):
            low[:, b * LANE:(b + 1) * LANE] = high[b].astype(BF16)
    hid[...] = hb_o[...].reshape(SUB, steps, width)
    nt = (((1,), (1,)), ((), ()))
    logits = lax.dot_general(hb_o[...], wt_o[...], nt, preferred_element_type=F32)
    logits = logits + lax.dot_general(hb_x[...], wt_x[...], nt, preferred_element_type=F32)
    logits = logits + bias[...]
    target = lax.broadcasted_iota(jnp.int32, (rows, vocab), 1) == tgt[...].reshape(rows, 1)
    top = jnp.max(logits, axis=1, keepdims=True)
    power = jnp.exp(logits - top)
    norm = jnp.sum(power, axis=1, keepdims=True)
    picked = jnp.sum(jnp.where(target, logits, 0.0), axis=1, keepdims=True)
    loss[...] += jnp.sum(top + jnp.log(norm) - picked, keepdims=True)
    probs = power / norm
    grad = ((probs - jnp.where(target, 1.0, 0.0)) * (1.0 / total_tokens)).astype(BF16)
    lgrad[...] = grad.reshape(SUB, steps, vocab)
    gacc[...] += jnp.sum(grad.astype(F32).reshape(rows // SUB, SUB, vocab), axis=0)
    back = jnp.dot(grad, wt_o[...], preferred_element_type=F32)
    for b in range(hg.shape[0]):
        hg[b] = back[:, b * LANE:(b + 1) * LANE]

    def back_step(pair, carry):
        pc, acc = carry
        outs = []
        for half in range(2):
            r = pair * 2 + half
            at = pl.multiple_of(r * SUB, SUB)
            g = jnp.concatenate([hg[b, pl.ds(r, SUB, stride=steps), :] for b in range(hg.shape[0])], axis=1)
            s = g * q[pl.ds(at, SUB), :]
            src[pl.ds(at, SUB), :] = s
            outs.append(g * u[pl.ds(at, SUB), :])
            pc = pc * d_o[pl.ds(at, SUB), :]
            acc = acc + pc * s
        at = pl.multiple_of(pair * 2 * SUB, 2 * SUB)
        go[pl.ds(at, 2 * SUB), :] = jnp.concatenate(outs, axis=0).astype(BF16)
        return pc, acc

    pc, acc = lax.fori_loop(0, steps // 2, back_step, (pcum[...], h_seg[...]), unroll=2)
    pcum[...] = pc
    h_seg[...] = acc

    @pl.when(k == pl.num_programs(0) - 1)
    def _():
        b_grad[...] = jnp.sum(gacc[...], axis=0, keepdims=True)
        head = h_seg[SUB - 1:SUB, :]
        for s in range(SUB - 2, -1, -1):
            head = h_seg[s:s + 1, :] + sp_o[s:s + 1, :] * head
        h_blk[...] = head


def decoder_grad_kernel(meta, lgrad, hid, out, *, count):
    j = pl.program_id(0)
    tn = (((0,), (0,)), ((), ()))
    grad = lax.dot_general(lgrad[...], hid[...], tn, preferred_element_type=F32)
    vocab = grad.shape[0]
    cols = grad.shape[1] // LANE
    part = out.shape[1]
    splits = count // (pl.num_programs(0) * cols)
    for c in range(cols):
        for e in range(splits):
            if e * part >= vocab:
                continue
            size = min(part, vocab - e * part)
            slot = slot_of(((j * cols + c) * splits + e) ^ meta[0], count)
            piece = grad[e * part:e * part + size, c * LANE:(c + 1) * LANE]
            if size < part:
                piece = jnp.concatenate([piece, jnp.zeros((part - size, LANE), F32)], axis=0)
            out[slot] = piece


def input_grad_kernel(
    order, meta, feats, w, prev, src, go, onehot, table_t, h_all, ps_all, seg_p, h_seg, b_grad, loss,
    out, out_e,
    gg, hn, eacc, *, count, part,
):
    j = pl.program_id(0)
    toks = feats.shape[0]
    rows = 128
    width = prev.shape[1]
    vocab = onehot.shape[0]
    me, own = meta[0], meta[1]

    def later(i, g):
        slot = order[count - 1 - i] ^ me
        return h_all[slot] + ps_all[slot][0:1] * g

    one = lax.fori_loop(0, count - 1 - own, later, jnp.zeros((1, width), F32))
    for s in range(SUB - 1, -1, -1):
        hn[s:s + 1, :] = one
        one = h_seg[s:s + 1, :] + seg_p[s:s + 1, :] * one

    def chunk(i, later_grad):
        at = pl.multiple_of((toks // rows - 1 - i) * rows, rows)
        fe = feats[pl.ds(at, rows), :]
        gate = [jnp.dot(fe, w[g], preferred_element_type=F32) for g in range(3)]
        in_gate = 0.5 * jnp.tanh(gate[0]) + 0.5
        decay = 0.5 * jnp.tanh(gate[1]) + 0.5
        cand = jnp.tanh(gate[2])
        source = in_gate * cand
        given = src[pl.ds(at, rows), :]
        cell, carried = [], []
        for r in range(rows // SUB - 1, -1, -1):
            g = given[r * SUB:(r + 1) * SUB] + later_grad
            later_grad = decay[r * SUB:(r + 1) * SUB] * g
            cell.append(g)
            carried.append(later_grad)
        g = jnp.concatenate(cell[::-1], axis=0)
        h = jnp.concatenate(carried[::-1], axis=0)
        gg[pl.ds(at, rows), 0:width] = (g * (source - source * in_gate)).astype(BF16)
        gg[pl.ds(at, rows), width:2 * width] = (h * prev[pl.ds(at, rows), :] * (1.0 - decay)).astype(BF16)
        gg[pl.ds(at, rows), 2 * width:3 * width] = (g * (in_gate - source * cand)).astype(BF16)
        return later_grad

    lax.fori_loop(0, toks // rows, chunk, hn[...])
    gg[:, 3 * width:4 * width] = go[...]
    both = (((1,), (1,)), ((), ()))
    cols = width // LANE
    splits = count // (pl.num_programs(0) * cols)
    part_e = jnp.zeros((vocab, feats.shape[1]), F32)
    for gate in range(4):
        total = jnp.dot(onehot[...], gg[:, gate * width:(gate + 1) * width], preferred_element_type=F32)
        high = total.astype(BF16)
        low = (total - high.astype(F32)).astype(BF16)
        wide = jnp.dot(table_t[...], high, preferred_element_type=F32)
        wide = wide + jnp.dot(table_t[...], low, preferred_element_type=F32)
        for c in range(cols):
            for e in range(splits):
                if e * part >= wide.shape[0]:
                    continue
                size = min(part, wide.shape[0] - e * part)
                slot = slot_of(((j * cols + c) * splits + e) ^ me, count)
                out[slot, gate * part:gate * part + size, :] = wide[
                    e * part:e * part + size, c * LANE:(c + 1) * LANE
                ]
        back = lax.dot_general(high, w[gate], both, preferred_element_type=F32)
        back = back + lax.dot_general(low, w[gate], both, preferred_element_type=F32)
        part_e = part_e + (back if gate == 2 else 2.0 * back)

    @pl.when(j == 0)
    def _():
        eacc[...] = jnp.zeros_like(eacc)

    eacc[0:vocab, 0:feats.shape[1]] += part_e

    @pl.when(j == pl.num_programs(0) - 1)
    def _():
        for k in range(3):
            size = min(LANE, vocab - k * LANE)
            eacc[vocab + k:vocab + k + 1, 0:size] = b_grad[:, k * LANE:k * LANE + size]
        eacc[vocab + 3:vocab + 4, 0:1] = loss[...]
        per = out_e.shape[1]
        for p in range(count):
            out_e[slot_of(p ^ me, count)] = eacc[p * per:(p + 1) * per, :]


def finish_kernel(meta, chunks, w_grad, b_grad, e_grad, o_grad, loss, eacc, *, part, vocab, emb, shards, total_tokens):
    count = chunks.shape[0]
    me = meta[0]
    width = w_grad.shape[2]
    cols = width // LANE
    splits = count // cols
    per = chunks.shape[1] - 4 * part
    for c in range(cols):
        lanes = slice(c * LANE, (c + 1) * LANE)
        for e in range(splits):
            slot = slot_of((c * splits + e) ^ me, count)
            size = max(0, min(part, emb - e * part))
            for gate in range(4):
                if size:
                    w_grad[gate, e * part:e * part + size, lanes] = chunks[slot, gate * part:gate * part + size, :]
                if e * part <= emb < (e + 1) * part:
                    at = gate * part + emb - e * part
                    b_grad[gate:gate + 1, lanes] = chunks[slot, at:at + 1, :]
    for p in range(count):
        eacc[p * per:(p + 1) * per, :] = chunks[slot_of(p ^ me, count), 4 * part:4 * part + per, :]
    e_grad[...] = eacc[0:e_grad.shape[0], 0:emb]
    for k in range(3):
        size = min(LANE, o_grad.shape[1] - k * LANE)
        o_grad[:, k * LANE:k * LANE + size] = eacc[vocab + k:vocab + k + 1, 0:size] * (1.0 / shards)
    loss[...] = eacc[vocab + 3:vocab + 4, 0:1] * (1.0 / (shards * total_tokens))


def decoder_finish_kernel(meta, chunks, out):
    count = chunks.shape[0]
    me = meta[0]
    cols = out.shape[1] // LANE
    splits = count // cols
    part = chunks.shape[1]
    for c in range(cols):
        for e in range(splits):
            size = max(0, min(part, out.shape[0] - e * part))
            if size:
                slot = slot_of((c * splits + e) ^ me, count)
                out[e * part:e * part + size, c * LANE:(c + 1) * LANE] = chunks[slot, 0:size, :]


def fetch_others(value, wa, own_core):
    half = value.shape[0] // 2
    mine = lax.dynamic_slice_in_dim(value, own_core * half, half, 0)
    fetched = []
    for shift in range(1, wa):
        got = lax.ppermute(mine, "wa", [(k, (k - shift) % wa) for k in range(wa)])
        other = swap(got, "ctx", 1)
        first = jnp.where(own_core == 0, got, other)
        second = jnp.where(own_core == 0, other, got)
        fetched.append(jnp.concatenate([first, second], axis=0))
    return fetched


def body(ids, targets, doc_lengths, block_of, embed, w_in, b_in, w_out, b_out):
    count = lax.axis_size("ctx")
    wa = lax.axis_size("wa")
    me = lax.axis_index("ctx").astype(jnp.int32)
    toks = ids.shape[0]
    seg = toks // SUB
    emb, gates, width = w_in.shape
    other = width * (wa - 1)
    vocab = embed.shape[0]
    vpad = ceil_to(vocab, 32)
    total_tokens = toks * count
    block_ids = jnp.arange(count, dtype=jnp.int32)
    own_block = jnp.sum(jnp.where(block_ids == me, block_of, 0))
    order = jnp.sum(jnp.where(block_of[None, :] == block_ids[:, None], block_ids[None, :], 0), axis=1)
    meta = jnp.stack([me, own_block])
    base = (own_block * toks)[None]
    starts = jnp.cumsum(doc_lengths) - doc_lengths

    kdim = ceil_to(emb + 4, 16)
    scale = jnp.array([0.5, 0.5, 1.0, 0.5], F32)
    shift = jnp.array([0.0, 3.0, 0.0, 0.0], F32)
    b_eff = (b_in + shift[:, None]) * scale[:, None]
    b_hi = lax.reduce_precision(b_eff, 8, 7)
    b_mid = lax.reduce_precision(b_eff - b_hi, 8, 7)
    b_lo = b_eff - b_hi - b_mid
    pull = jnp.broadcast_to(jnp.array([0.0, RESET_PULL, 0.0, 0.0], F32)[:, None], (gates, width))
    extra = jnp.stack([b_hi, b_mid, b_lo, pull], axis=1)
    main = jnp.transpose(w_in, (1, 0, 2)).astype(F32) * scale[:, None, None]
    fill = jnp.zeros((gates, kdim - emb - 4, width), F32)
    w_own = jnp.concatenate([main, extra, fill], axis=1).astype(BF16)
    table = jnp.pad(embed, ((0, vpad - vocab), (0, kdim - emb)))
    table = jnp.where((jnp.arange(kdim) >= emb) & (jnp.arange(kdim) < emb + 3), jnp.ones((), BF16), table)
    wt_own = jnp.pad(w_out.T, ((0, vpad - vocab), (0, 0)))
    core = me % 2
    w_oth = jnp.concatenate(fetch_others(w_own, wa, core), axis=2)
    wt_oth = jnp.concatenate(fetch_others(wt_own, wa, core), axis=1)
    bias_out = jnp.pad(b_out, (0, vpad - vocab), constant_values=-1e30)[None]
    ids_p = ids.reshape(SUB, seg).T.reshape(1, toks)
    tgt = targets.reshape(SUB, seg, 1)

    feats, onehot = pl.pallas_call(
        feats_kernel,
        in_specs=[smem(), smem(), whole((1, toks)), whole((vpad, kdim))],
        out_specs=[whole((toks, kdim)), whole((vpad, toks))],
        out_shape=[jax.ShapeDtypeStruct((toks, kdim), BF16), jax.ShapeDtypeStruct((vpad, toks), BF16)],
        compiler_params=pltpu.CompilerParams(vmem_limit_bytes=VMEM),
        name="feats",
    )(starts, base, ids_p, table)

    def gate_call(w, name):
        wide = w.shape[2]
        column = lambda rows: pl.BlockSpec((rows, WBLK), lambda j: (0, j))
        shape = lambda rows: jax.ShapeDtypeStruct((rows, wide), F32)
        return pl.pallas_call(
            gate_kernel,
            grid=(wide // WBLK,),
            in_specs=[whole((toks, kdim)), pl.BlockSpec((gates, kdim, WBLK), lambda j: (0, 0, j))],
            out_specs=[column(toks)] * 3 + [column(SUB)] * 2 + [column(2)],
            out_shape=[shape(toks)] * 3 + [shape(SUB)] * 2 + [shape(2)],
            compiler_params=params(),
            cost_estimate=pl.CostEstimate(
                flops=8 * toks * kdim * wide, bytes_accessed=12 * toks * wide, transcendentals=4 * toks * wide
            ),
            name=name,
        )(feats, w)

    d_o, x_o, o_o, sp_o, ss_o, ps = gate_call(w_own, "gates_own")
    ps_x = [ps] + [
        lax.ppermute(ps, "wa", [(k, (k - s) % wa) for k in range(wa)]) for s in range(1, wa)
    ]
    ps_all = gather_xor(jnp.concatenate(ps_x, axis=1), "ctx")
    d_x, x_x, o_x, sp_x, ss_x, _ = gate_call(w_oth, "gates_other")

    steps = 32
    rows = steps * SUB
    row_block = lambda wide: pl.BlockSpec((rows, wide), lambda k: (k, 0))
    nat_block = lambda wide: pl.BlockSpec((SUB, steps, wide), lambda k: (0, k, 0))
    prev, hid, lgrad, src, go, h_seg, h_blk, b_grad, loss = pl.pallas_call(
        functools.partial(cell_kernel, total_tokens=total_tokens),
        grid=(seg // steps,),
        in_specs=[smem(), smem()]
        + [row_block(width)] * 3
        + [row_block(other)] * 3
        + [whole(ps_all.shape)]
        + [whole((SUB, width))] * 2
        + [whole((SUB, other))] * 2
        + [whole((vpad, width)), whole((vpad, other)), whole((1, vpad)), nat_block(1)],
        out_specs=[
            row_block(width), nat_block(width), nat_block(vpad), row_block(width), row_block(width),
            whole((SUB, width)), whole((1, width)), whole((1, vpad)), whole((1, 1)),
        ],
        out_shape=[
            jax.ShapeDtypeStruct((toks, width), F32),
            jax.ShapeDtypeStruct((SUB, seg, width), BF16),
            jax.ShapeDtypeStruct((SUB, seg, vpad), BF16),
            jax.ShapeDtypeStruct((toks, width), F32),
            jax.ShapeDtypeStruct((toks, width), BF16),
            jax.ShapeDtypeStruct((SUB, width), F32),
            jax.ShapeDtypeStruct((1, width), F32),
            jax.ShapeDtypeStruct((1, vpad), F32),
            jax.ShapeDtypeStruct((1, 1), F32),
        ],
        scratch_shapes=[
            pltpu.VMEM((SUB, width), F32), pltpu.VMEM((SUB, other), F32), pltpu.VMEM((SUB, width), F32),
            pltpu.VMEM((width // LANE, rows, LANE), F32), pltpu.VMEM((other // LANE, rows, LANE), F32),
            pltpu.VMEM((rows, width), BF16), pltpu.VMEM((rows, other), BF16),
            pltpu.VMEM((rows, width), F32), pltpu.VMEM((rows, width), F32),
            pltpu.VMEM((width // LANE, rows, LANE), F32),
            pltpu.VMEM((SUB, vpad), F32),
        ],
        compiler_params=params(),
        name="cells",
    )(order, meta, d_o, x_o, o_o, d_x, x_x, o_x, ps_all, sp_o, ss_o, sp_x, ss_x, wt_own, wt_oth, bias_out, tgt)

    hidden = hid.reshape(toks, width)
    h_all = gather_xor(h_blk, "ctx")

    cols = width // LANE
    splits = count // cols
    vpart = ceil_to(-(-vpad // splits), 8)
    w_out_chunks = pl.pallas_call(
        functools.partial(decoder_grad_kernel, count=count),
        grid=(width // WBLK,),
        in_specs=[smem(), whole((toks, vpad)), pl.BlockSpec((toks, WBLK), lambda j: (0, j))],
        out_specs=whole((count, vpart, LANE)),
        out_shape=jax.ShapeDtypeStruct((count, vpart, LANE), F32),
        compiler_params=params(),
        cost_estimate=pl.CostEstimate(
            flops=2 * toks * vpad * width, bytes_accessed=2 * toks * (width + vpad), transcendentals=0
        ),
        name="decoder_grad",
    )(meta, lgrad.reshape(toks, vpad), hidden)

    part = ceil_to(-(-kdim // splits), 8)
    per = ceil_to(-(-(vpad + 4) // count), 8)
    column = lambda size: pl.BlockSpec((size, WBLK), lambda j: (0, j))
    lead = lambda *size: pl.BlockSpec(size + (WBLK,), lambda j: (0, 0, j))
    w_chunks, e_chunks = pl.pallas_call(
        functools.partial(input_grad_kernel, count=count, part=part),
        grid=(width // WBLK,),
        in_specs=[
            smem(), smem(), whole((toks, kdim)), lead(gates, kdim), column(toks), column(toks), column(toks),
            whole((vpad, toks)), whole((kdim, vpad)), lead(count, 1), lead(count, 2), column(SUB), column(SUB),
            whole((1, vpad)), whole((1, 1)),
        ],
        out_specs=[whole((count, 4 * part, LANE)), whole((count, per, LANE))],
        out_shape=[
            jax.ShapeDtypeStruct((count, 4 * part, LANE), F32),
            jax.ShapeDtypeStruct((count, per, LANE), F32),
        ],
        scratch_shapes=[
            pltpu.VMEM((toks, 4 * WBLK), BF16), pltpu.VMEM((SUB, WBLK), F32), pltpu.VMEM((count * per, LANE), F32)
        ],
        compiler_params=params(),
        name="input_grad",
    )(order, meta, feats, w_own, prev, src, go, onehot, table.T, h_all, ps_all, sp_o, h_seg, b_grad, loss)

    bit = 1
    while bit < wa:
        e_chunks = e_chunks + swap(e_chunks, "wa", bit)
        bit *= 2
    out_chunk = gather_chunks(scatter_sum(w_out_chunks, "ctx"), "ctx")
    w_out_grad = pl.pallas_call(
        decoder_finish_kernel,
        in_specs=[smem(), whole(out_chunk.shape)],
        out_specs=whole((vpad, width)),
        out_shape=jax.ShapeDtypeStruct((vpad, width), F32),
        compiler_params=pltpu.CompilerParams(vmem_limit_bytes=VMEM),
        name="decoder_finish",
    )(meta, out_chunk)
    in_chunk = gather_chunks(scatter_sum(jnp.concatenate([w_chunks, e_chunks], axis=1), "ctx"), "ctx")
    w_grad, bi_grad, e_grad, bo_grad, loss_all = pl.pallas_call(
        functools.partial(
            finish_kernel, part=part, vocab=vpad, emb=emb, shards=wa, total_tokens=total_tokens
        ),
        in_specs=[smem(), whole(in_chunk.shape)],
        out_specs=[
            whole((gates, emb, width)), whole((gates, width)), whole((vocab, emb)), whole((1, vocab)), whole((1, 1))
        ],
        out_shape=[
            jax.ShapeDtypeStruct((gates, emb, width), F32),
            jax.ShapeDtypeStruct((gates, width), F32),
            jax.ShapeDtypeStruct((vocab, emb), F32),
            jax.ShapeDtypeStruct((1, vocab), F32),
            jax.ShapeDtypeStruct((1, 1), F32),
        ],
        scratch_shapes=[pltpu.VMEM((count * per, LANE), F32)],
        compiler_params=pltpu.CompilerParams(vmem_limit_bytes=VMEM),
        name="finish",
    )(meta, in_chunk)
    return (
        hidden,
        loss_all[0, 0],
        e_grad,
        jnp.transpose(w_grad, (1, 0, 2)),
        bi_grad,
        w_out_grad[:vocab].T,
        bo_grad[0],
    )


def solution(mesh):
    placed = (
        P("ctx"),
        P("ctx"),
        P(),
        P(),
        P(),
        P(None, None, "wa"),
        P(None, "wa"),
        P("wa", None),
        P(),
    )
    return jax.shard_map(
        body,
        mesh=mesh,
        in_specs=placed,
        out_specs=(
            P("ctx", "wa"),
            P(),
            P(),
            P(None, None, "wa"),
            P(None, "wa"),
            P("wa", None),
            P(),
        ),
        check_vma=False,
    )
```

```python
import functools

import jax
import jax.numpy as jnp
from jax import lax
from jax.experimental import pallas as pl
from jax.experimental.pallas import tpu as pltpu
from jax.sharding import PartitionSpec as P

CHAINS = 16
LANE = 128
F32 = jnp.float32
BF16 = jnp.bfloat16


def ceil_to(value, step):
    return -(-value // step) * step


def call(kernel, name, scalars, arrays, outs, scratch=(), limit=16, in_spaces=None, out_spaces=None, micros=1):
    spec = lambda m: m if isinstance(m, pl.BlockSpec) else pl.BlockSpec(memory_space=m)
    blocked = [m for m in in_spaces or [] if isinstance(m, pl.BlockSpec)]
    steps = micros[1] if blocked else None
    return pl.pallas_call(
        kernel,
        grid=(steps,) if blocked else (),
        in_specs=[spec(pltpu.SMEM)] * len(scalars) + [spec(m) for m in in_spaces or [pltpu.VMEM] * len(arrays)],
        out_specs=[spec(m) for m in out_spaces or [pltpu.VMEM] * len(outs)],
        out_shape=list(outs),
        scratch_shapes=list(scratch),
        compiler_params=pltpu.CompilerParams(vmem_limit_bytes=limit * 1024 * 1024),
        cost_estimate=pl.CostEstimate(
            flops=0, transcendentals=0, bytes_accessed=3000000 * (micros[0] if blocked else micros)
        ),
        name=name,
    )(*scalars, *arrays)


def near(value):
    return pltpu.with_memory_space_constraint(value, pltpu.VMEM)


def stages_of(count):
    stages, bit = [[1]], 2
    while bit < count:
        ways = min(8 if bit == 2 else 4, count // bit)
        stages.append([k * bit for k in range(1, ways)])
        bit *= ways
    return stages


def swap(value, axis, mask):
    count = lax.axis_size(axis)
    return lax.ppermute(value, axis, [(k, k ^ mask) for k in range(count)])


def all_of(value, axes):
    count = lax.axis_size(axes)
    return lax.all_to_all(jnp.broadcast_to(value[None], (count,) + value.shape), axes, 0, 0, tiled=True)


def slot_of(xor_index, count):
    place, size, bit = 0, count, 1
    for masks in stages_of(count):
        ways = len(masks) + 1
        size = size // ways
        place = place + ((xor_index // bit) % ways) * size
        bit = bit * ways
    return place


STEPS = 32766.0
BIAS = 90


def power_of_two(exponent):
    value = jnp.full(exponent.shape, 2.0 ** -BIAS, F32)
    for bit in range(7):
        on = ((exponent + BIAS) // (1 << bit)) % 2 == 1
        value = value * jnp.where(on, 2.0 ** (1 << bit), 1.0)
    return value


def coded_rows(groups):
    return ceil_to(sum(groups) + len(groups), 16)


def encode(value, groups):
    parts, exponents, at = [], [], 0
    for size in groups:
        part = value[at:at + size]
        most = jnp.max(jnp.abs(part), axis=0, keepdims=True)
        exponent = jnp.ceil(jnp.log2(jnp.maximum(most, 2.0 ** (1 - BIAS)))).astype(jnp.int32)
        exponent = jnp.clip(exponent, -BIAS, 127 - BIAS)
        parts.append(jnp.round(part * (STEPS / power_of_two(exponent))).astype(jnp.int32))
        exponents.append(exponent)
        at += size
    fill = coded_rows(groups) - at - len(groups)
    if fill:
        exponents.append(jnp.zeros((fill, value.shape[1]), jnp.int32))
    return jnp.concatenate(parts + exponents, axis=0).astype(jnp.int16)


def decode(code, groups):
    code = code.astype(jnp.int32)
    parts, at, total = [], 0, sum(groups)
    for k, size in enumerate(groups):
        unit = power_of_two(code[total + k:total + k + 1]) * (1.0 / STEPS)
        parts.append(code[at:at + size].astype(F32) * unit)
        at += size
    return jnp.concatenate(parts, axis=0)


def reduce_chunks(keeps, moved, groups, axis):
    stages = stages_of(lax.axis_size(axis))[1:]
    number = len(keeps)
    sizes = [k.shape[1] for k in keeps]
    rows, coded = sum(sizes), coded_rows(groups)
    half = keeps[0].shape[0]
    ways = len(stages[0]) + 1 if stages else 1
    code_shape = lambda size: jax.ShapeDtypeStruct((size, coded, LANE), jnp.int16)

    def first(*refs):
        ins, outs = refs[:2 * number], refs[2 * number:]
        for place in range(half):
            way, slot = place // (half // ways), place % (half // ways)
            parts = [ins[k][place] + ins[number + k][place] for k in range(number)]
            value = jnp.concatenate(parts, axis=0)
            outs[way][slot] = value if way == 0 else encode(value, groups)

    keep, *sends = call(
        first,
        "core_sum",
        [],
        list(keeps) + list(moved),
        [jax.ShapeDtypeStruct((half // ways, rows, LANE), F32)] + [code_shape(half // ways)] * (ways - 1),
        limit=24,
    )
    for k, masks in enumerate(stages):
        got = [swap(part, axis, mask) for part, mask in zip(sends, masks)]
        ways = len(stages[k + 1]) + 1 if k + 1 < len(stages) else 1
        size = keep.shape[0] // ways
        last = k + 1 == len(stages)

        def later(*refs):
            ins, outs = refs[:len(got) + 1], refs[len(got) + 1:]
            for way in range(ways):
                for slot in range(size):
                    value = ins[0][way * size + slot]
                    for ref in ins[1:]:
                        value = value + decode(ref[way * size + slot], groups)
                    outs[way][slot] = value if way == 0 and not last else encode(value, groups)

        kept = code_shape(size) if last else jax.ShapeDtypeStruct((size, rows, LANE), F32)
        keep, *sends = call(
            later, "chip_sum" + str(k), [], [keep] + got, [kept] + [code_shape(size)] * (ways - 1), limit=24
        )
    return keep


def gather_chunks(chunk, axis):
    value = chunk
    stages = stages_of(lax.axis_size(axis))
    for number, masks in enumerate(reversed(stages[1:])):
        parts = [value] + [swap(value, axis, mask) for mask in masks]
        size = value.shape[0]

        def kernel(*refs):
            for k, ref in enumerate(refs[:-1]):
                refs[-1][k * size:(k + 1) * size] = ref[...]

        shape = (size * len(parts),) + value.shape[1:]
        value = call(kernel, "chunk_join" + str(number), [], parts, [jax.ShapeDtypeStruct(shape, value.dtype)])[0]
    return value, swap(value, axis, 1)


def padded(value, rows, lanes, size):
    count = rows.stop - rows.start
    if count == 0:
        return jnp.zeros((size, LANE), F32)
    piece = value[rows, lanes]
    return piece if count == size else jnp.concatenate([piece, jnp.zeros((size - count, LANE), F32)], axis=0)


def store_pairs(keep, send, me, value_of, count, rows):
    first = me % 2 == 0
    for pair in range(count // 2):
        a, b = value_of(2 * pair), value_of(2 * pair + 1)
        slot = slot_of((2 * pair) ^ (me - me % 2), count)
        keep[slot, rows, :] = jnp.where(first, a, b)
        send[slot, rows, :] = jnp.where(first, b, a)


def tile(ref, index, blocks, kind=0, kinds=1):
    return ref.at[pl.ds(pl.multiple_of((index * kinds + kind) * blocks, blocks), blocks), :]


def spread(ref, value, first, blocks, kind=0, kinds=1):
    rows = value.shape[0]
    for b in range(blocks):
        place = pl.ds((first * kinds + kind) * blocks + b, rows, stride=kinds * blocks)
        ref[place, :] = value[:, b * LANE:(b + 1) * LANE]


def gathered(ref, first, rows, blocks, b, kind=0, kinds=1):
    return ref[pl.ds((first * kinds + kind) * blocks + b, rows, stride=kinds * blocks), :]


def stream_order(order, block_of):
    def place(d, carry):
        order[block_of[d]] = d
        return carry

    lax.fori_loop(0, block_of.shape[0], place, 0)
    return block_of[lax.axis_index("ctx")]


def segment_ends(ids, tab, toks, blocks, kinds):
    length = toks // CHAINS

    def step(r, carry):
        prod, total = list(carry[:CHAINS]), list(carry[CHAINS:])
        for s in range(CHAINS):
            at = ids[s * length + r]
            d = tile(tab, at, blocks, 0, kinds)[...]
            total[s] = d * total[s] + tile(tab, at, blocks, 1, kinds)[...]
            prod[s] = prod[s] * d
        return tuple(prod + total)

    first = [jnp.ones((blocks, LANE), F32)] * CHAINS + [jnp.zeros((blocks, LANE), F32)] * CHAINS
    carry = lax.fori_loop(0, length, step, tuple(first), unroll=2)
    return carry[:CHAINS], carry[CHAINS:]


def own_table_kernel(doc_lengths, block_of, ids, embed, w, marked, spots, tab, seg, ends, sem, *, vocab, blocks):
    toks = ids.shape[0]
    copy = pltpu.make_async_copy(ids, marked, sem)
    copy.start()
    gate = [jnp.dot(embed[...], w[g], preferred_element_type=F32) for g in range(3)]
    spread(tab, jax.nn.sigmoid(gate[1] + 3.0), 0, blocks, 0, 2)
    spread(tab, jax.nn.sigmoid(gate[0]) * jnp.tanh(gate[2]), 0, blocks, 1, 2)
    copy.wait()
    start = -block_of[lax.axis_index("ctx")] * toks
    for k in range(doc_lengths.shape[0]):
        inside = (start >= 0) & (start < toks)
        at = jnp.clip(start, 0, toks - 1)
        spot = jnp.where(inside, marked[at], 0)
        spots[k] = spot
        marked[at] = jnp.where(inside, vocab + k, marked[at])
        tile(tab, vocab + k, blocks, 0, 2)[...] = jnp.zeros((blocks, LANE), F32)
        tile(tab, vocab + k, blocks, 1, 2)[...] = tile(tab, spot, blocks, 1, 2)[...]
        start = start + doc_lengths[k]
    prod, total = segment_ends(marked, tab, toks, blocks, 2)
    p_all, s_all = prod[0], total[0]
    for s in range(CHAINS):
        seg[s, 0] = prod[s]
        seg[s, 1] = total[s]
        if s:
            s_all = prod[s] * s_all + total[s]
            p_all = prod[s] * p_all
    ends[0] = p_all
    ends[1] = s_all


def rest_table_kernel(ids, spots, embed, w, *refs, vocab, blocks, others):
    fetched = refs[:2 * others]
    outs = refs[2 * others:]
    o_tab, coef = outs[:2]
    toks = ids.shape[0]
    gate = [jnp.dot(embed[...], w[g], preferred_element_type=F32) for g in (0, 2, 3)]
    in_gate, cand = jax.nn.sigmoid(gate[0]), jnp.tanh(gate[1])
    source = in_gate * cand
    spread(o_tab, jax.nn.sigmoid(gate[2]), 0, blocks)
    spread(coef, source - source * in_gate, 0, blocks, 0, 2)
    spread(coef, in_gate - source * cand, 0, blocks, 1, 2)
    docs = spots.shape[0]
    for k in range(docs):
        tile(o_tab, vocab + k, blocks)[...] = tile(o_tab, spots[k], blocks)[...]
    first = lax.axis_index("ctx") % 2 == 0
    for p in range(others):
        direct, passed = fetched[2 * p:2 * p + 2]
        tab, seg = outs[2 + 2 * p:4 + 2 * p]

        def weights(g):
            mine, theirs = direct[g % 2], passed[g % 2]
            return jnp.where(first, mine, theirs) if g < 2 else jnp.where(first, theirs, mine)

        gate = [jnp.dot(embed[...], weights(g), preferred_element_type=F32) for g in range(4)]
        spread(tab, jax.nn.sigmoid(gate[1] + 3.0), 0, blocks, 0, 3)
        spread(tab, jax.nn.sigmoid(gate[0]) * jnp.tanh(gate[2]), 0, blocks, 1, 3)
        spread(tab, jax.nn.sigmoid(gate[3]), 0, blocks, 2, 3)
        for k in range(docs):
            tile(tab, vocab + k, blocks, 0, 3)[...] = jnp.zeros((blocks, LANE), F32)
            for kind in (1, 2):
                tile(tab, vocab + k, blocks, kind, 3)[...] = tile(tab, spots[k], blocks, kind, 3)[...]
        prod, total = segment_ends(ids, tab, toks, blocks, 3)
        for s in range(CHAINS):
            seg[s, 0] = prod[s]
            seg[s, 1] = total[s]


def cell_kernel(*refs, others, total_tokens, blocks):
    ids, block_of, ps_all, tab_o, o_tab, seg_o, wt_o, bias, tgt, ids_row = refs[:10]
    refs = refs[10:]
    tab_x, seg_x = refs[:others], refs[others:2 * others]
    halves = refs[2 * others:4 * others]
    refs = refs[4 * others:]
    hid, prev_out, src_out, lgrad, heads, head, o_sum, sums = refs[:8]
    order, prev, src, hs, low, low_x, wt_x, logits, pcum, sem, src_sems = refs[8:]
    toks = ids.shape[0]
    length = toks // CHAINS
    width = blocks * LANE
    vocab = wt_o.shape[0]
    own = stream_order(order, block_of)
    shards, mine = lax.axis_size("wa"), lax.axis_index("wa")
    nt = (((1,), (1,)), ((), ()))
    tn = (((0,), (0,)), ((), ()))

    def starts(piece, seg):
        def earlier(b, c):
            slot = order[b] * shards + (mine + piece) % shards
            return ps_all[slot, 0] * c + ps_all[slot, 1]

        c = lax.fori_loop(0, own, earlier, jnp.zeros((blocks, LANE), F32))
        out = []
        for s in range(CHAINS):
            out.append(c)
            c = seg[s, 0] * c + seg[s, 1]
        return tuple(out)

    def flatten(low):
        rows = 256

        def part(k, carry):
            at = pl.multiple_of(k * rows, rows)
            value = hs[pl.ds(at * blocks, rows * blocks), :]
            low[pl.ds(at, rows), :] = value.reshape(rows, width).astype(BF16)
            return carry

        lax.fori_loop(0, toks // rows, part, 0)

    def own_step(r, carry):
        cells, prods = list(carry[:CHAINS]), list(carry[CHAINS:])
        for s in range(CHAINS):
            t = s * length + r
            at = ids[t]
            d = tile(tab_o, at, blocks, 0, 2)[...]
            o = tile(o_tab, at, blocks)[...]
            tile(prev, t, blocks)[...] = cells[s]
            cells[s] = d * cells[s] + tile(tab_o, at, blocks, 1, 2)[...]
            prods[s] = prods[s] * d
            tile(pcum, t, blocks)[...] = prods[s]
            th = jnp.tanh(cells[s])
            h = o * th
            tile(hs, t, blocks)[...] = h
            tile(src, t, blocks)[...] = o - h * th
        return tuple(cells + prods)

    lax.fori_loop(0, length, own_step, starts(0, seg_o) + (jnp.ones((blocks, LANE), F32),) * CHAINS)
    save_prev = pltpu.make_async_copy(prev, prev_out, sem.at[1])
    save_prev.start()
    flatten(low)
    save = pltpu.make_async_copy(low, hid, sem.at[0])
    save.start()
    logits[...] = lax.dot_general(wt_o[...], low[...], nt, preferred_element_type=F32) + bias[...]
    first = lax.axis_index("ctx") % 2 == 0
    half = vocab // 2
    for p in range(others):
        tab = tab_x[p]
        direct, passed = halves[2 * p:2 * p + 2]
        wt_x[0:half, :] = jnp.where(first, direct[...], passed[...])
        wt_x[half:vocab, :] = jnp.where(first, passed[...], direct[...])

        def other_step(r, carry):
            cells = list(carry)
            for s in range(CHAINS):
                t = s * length + r
                at = ids[t]
                cells[s] = tile(tab, at, blocks, 0, 3)[...] * cells[s] + tile(tab, at, blocks, 1, 3)[...]
                tile(hs, t, blocks)[...] = tile(tab, at, blocks, 2, 3)[...] * jnp.tanh(cells[s])
            return tuple(cells)

        lax.fori_loop(0, length, other_step, starts(p + 1, seg_x[p]))
        flatten(low_x)
        logits[...] += lax.dot_general(wt_x[...], low_x[...], nt, preferred_element_type=F32)

    rows = 512

    def save_src(k):
        place = pl.ds(pl.multiple_of(k * rows * blocks, rows * blocks), rows * blocks)
        return pltpu.make_async_copy(src.at[place, :], src_out.at[place, :], src_sems.at[k])

    o_sum[...] = jnp.zeros_like(o_sum)

    def back(k, carry):
        loss, b_grad = carry
        at = pl.multiple_of(k * rows, rows)
        part = logits[:, pl.ds(at, rows)]
        target = lax.broadcasted_iota(jnp.int32, (vocab, rows), 0) == tgt[:, pl.ds(at, rows)]
        top = jnp.max(part, axis=0, keepdims=True)
        power = jnp.exp(part - top)
        norm = jnp.sum(power, axis=0, keepdims=True)
        picked = jnp.sum(jnp.where(target, part, 0.0), axis=0, keepdims=True)
        loss = loss + (top + jnp.log(norm) - picked)
        grad = ((power / norm - jnp.where(target, 1.0, 0.0)) * (1.0 / total_tokens)).astype(BF16)
        lgrad[:, pl.ds(at, rows)] = grad
        b_grad = b_grad + jnp.sum(grad.astype(F32).reshape(vocab, rows // LANE, LANE), axis=1)
        hg = lax.dot_general(grad, wt_o[...], tn, preferred_element_type=F32)
        chars = lax.broadcasted_iota(jnp.int32, (vocab, rows), 0) == ids_row[:, pl.ds(at, rows)]
        moment = (hg * low[pl.ds(at, rows), :].astype(F32)).astype(BF16)
        o_sum[...] += jnp.dot(chars.astype(F32).astype(BF16), moment, preferred_element_type=F32)
        for b in range(blocks):
            hs[pl.ds(at * blocks + b, rows, stride=blocks), :] = hg[:, b * LANE:(b + 1) * LANE]
        for q in range(rows // length):
            place = pl.ds((at + q * length) * blocks, length * blocks)
            grad_src = src[place, :] * hs[place, :]
            src[place, :] = grad_src
            ends = (pcum[place, :] * grad_src).reshape(length, blocks, LANE)
            tile(heads, k * (rows // length) + q, blocks)[...] = jnp.sum(ends, axis=0)
        save_src(k).start()
        return loss, b_grad

    loss, b_grad = lax.fori_loop(
        0, toks // rows, back, (jnp.zeros((1, rows), F32), jnp.zeros((vocab, LANE), F32))
    )
    lane = lax.broadcasted_iota(jnp.int32, (vocab, LANE), 1)
    row = lax.broadcasted_iota(jnp.int32, (vocab, LANE), 0)
    sums[...] = jnp.where(lane == LANE - 1, jnp.sum(b_grad, axis=1, keepdims=True), 0.0) + jnp.where(
        (lane == LANE - 2) & (row == 0), jnp.sum(loss, axis=1, keepdims=True), 0.0
    )
    save.wait()
    save_prev.wait()
    for k in range(toks // rows):
        save_src(k).wait()
    total = tile(heads, CHAINS - 1, blocks)[...]
    for s in range(CHAINS - 2, -1, -1):
        total = tile(heads, s, blocks)[...] + seg_o[s, 0] * total
    head[...] = total


def decoder_grad_kernel(lgrad, hid, keep, send, *, count, blocks):
    grad = jnp.dot(lgrad[...], hid[...], preferred_element_type=F32)
    vocab = grad.shape[0]
    part = keep.shape[1]
    splits = count // blocks

    def piece(q):
        c, e = q // splits, q % splits
        size = max(0, min(part, vocab - e * part))
        return padded(grad, slice(e * part, e * part + size), slice(c * LANE, (c + 1) * LANE), part)

    store_pairs(keep, send, lax.axis_index("ctx"), piece, count, slice(0, part))


def char_sum_kernel(
    ids, block_of, tab, seg, heads, h_all, ps_all, prev, src, sums, order, carry, *refs, copies, blocks
):
    number = pl.program_id(0)
    length = ids.shape[0] // CHAINS
    span = prev.shape[1] // blocks
    sets = [refs[2 * k:2 * k + 2] for k in range(copies)]

    @pl.when(number == 0)
    def _():
        for ref in refs:
            ref[...] = jnp.zeros_like(ref)
        own = stream_order(order, block_of)
        count = block_of.shape[0]
        shards, mine = lax.axis_size("wa"), lax.axis_index("wa")

        def from_later(i, g):
            slot = order[count - 1 - i]
            return h_all[slot] + ps_all[slot * shards + mine, 0] * g

        later = lax.fori_loop(0, count - 1 - own, from_later, jnp.zeros((blocks, LANE), F32))
        for s in range(CHAINS - 1, -1, -1):
            carry[s] = later
            later = tile(heads, s, blocks)[...] + seg[s, 0] * later

    def step(i, later):
        h = list(later)
        r = span - 1 - i
        for s in range(CHAINS):
            at = ids[s * length + (pl.num_programs(0) - 1 - number) * span + r]
            here = pl.ds(pl.multiple_of(r * blocks, blocks), blocks)
            g = src[s, here, :] + h[s]
            h[s] = tile(tab, at, blocks, 0, 2)[...] * g
            cell, forget = sets[s % copies]
            tile(cell, at, blocks)[...] += g
            tile(forget, at, blocks)[...] += g * prev[s, here, :]
        return tuple(h)

    ends = lax.fori_loop(0, span, step, tuple(carry[s] for s in range(CHAINS)))
    for s in range(CHAINS):
        carry[s] = ends[s]

    @pl.when(number == pl.num_programs(0) - 1)
    def _():
        for k in range(2):
            value = refs[k][...]
            for more in sets[1:]:
                value = value + more[k][...]
            sums[k] = value


def input_grad_kernel(
    spots, sums, o_sum, tab, o_tab, coef, w, table, extra, keep, send, keep_e, send_e, merged,
    *, count, part, vocab, blocks,
):
    rows = table.shape[0]
    width = blocks * LANE
    me = lax.axis_index("ctx")
    merged[...] = sums[...]
    for k in range(spots.shape[0]):
        tile(merged.at[0], spots[k], blocks)[...] += tile(merged.at[0], vocab + k, blocks)[...]
    pad = (rows - vocab) * blocks
    for q in range(2):
        merged[q, vocab * blocks:, :] = jnp.zeros((pad, LANE), F32)

    def units(value_of):
        return jnp.concatenate([value_of(b) for b in range(blocks)], axis=1)

    def column(q, b):
        return merged[q, pl.ds(b, rows, stride=blocks), :]

    def square(ref, b, kinds):
        value = gathered(ref, 0, rows, blocks, b, 0, kinds)
        return value - value * value

    parts = [
        units(lambda b: column(0, b) * gathered(coef, 0, rows, blocks, b, 0, 2)),
        units(lambda b: column(1, b) * square(tab, b, 2)),
        units(lambda b: column(0, b) * gathered(coef, 0, rows, blocks, b, 1, 2)),
        o_sum[...] * (1.0 - units(lambda b: gathered(o_tab, 0, rows, blocks, b))),
    ]
    both = (((1,), (1,)), ((), ()))
    tn = (((0,), (0,)), ((), ()))
    splits = count // blocks
    part_e = jnp.zeros((rows, w.shape[1]), F32)
    for gate in range(4):
        total = parts[gate]
        high = total.astype(BF16)
        low = (total - high.astype(F32)).astype(BF16)
        wide = lax.dot_general(table[...], high, tn, preferred_element_type=F32)
        wide = wide + lax.dot_general(table[...], low, tn, preferred_element_type=F32)

        def piece(q):
            c, e = q // splits, q % splits
            size = max(0, min(part, wide.shape[0] - e * part))
            return padded(wide, slice(e * part, e * part + size), slice(c * LANE, (c + 1) * LANE), part)

        store_pairs(keep, send, me, piece, count, slice(gate * part, (gate + 1) * part))
        part_e = part_e + lax.dot_general(high, w[gate], both, preferred_element_type=F32)
        part_e = part_e + lax.dot_general(low, w[gate], both, preferred_element_type=F32)
    per = keep_e.shape[1]
    wide_e = jnp.concatenate([part_e, jnp.zeros((rows, LANE - part_e.shape[1]), F32)], axis=1) + extra[...]
    wide_e = jnp.concatenate([wide_e, jnp.zeros((count * per - rows, LANE), F32)], axis=0)
    store_pairs(keep_e, send_e, me, lambda q: wide_e[q * per:(q + 1) * per, :], count, slice(0, per))


def finish_kernel(
    mine, theirs, w_grad, b_grad, e_grad, out_grad, o_grad, loss, eacc, *, groups, part, per, emb, shards, total_tokens
):
    count = 2 * mine.shape[0]
    me = lax.axis_index("ctx")
    first = me % 2 == 0
    pairs = {}

    def chunk(q, rows):
        pair = q - q % 2
        if pair not in pairs:
            slot = slot_of(pair ^ (me - me % 2), count)
            own, other = mine[slot].astype(jnp.int32), theirs[slot].astype(jnp.int32)
            pairs[pair] = [
                decode(jnp.where(first, own, other), groups), decode(jnp.where(first, other, own), groups)
            ]
        return pairs[pair][q % 2][rows]

    cols = w_grad.shape[2] // LANE
    splits = count // cols
    vpart = groups[-1]
    vocab = out_grad.shape[0]
    for c in range(cols):
        lanes = slice(c * LANE, (c + 1) * LANE)
        for e in range(splits):
            q = c * splits + e
            size = max(0, min(part, emb - e * part))
            for gate in range(4):
                if size:
                    w_grad[gate, e * part:e * part + size, lanes] = chunk(q, slice(gate * part, gate * part + size))
                if e * part <= emb < (e + 1) * part:
                    at = gate * part + emb - e * part
                    b_grad[gate:gate + 1, lanes] = chunk(q, slice(at, at + 1))
            size = max(0, min(vpart, vocab - e * vpart))
            if size:
                at = 4 * part + per
                out_grad[e * vpart:e * vpart + size, lanes] = chunk(q, slice(at, at + size))
    for p in range(count):
        eacc[p * per:(p + 1) * per, :] = chunk(p, slice(4 * part, 4 * part + per))
    e_grad[...] = eacc[0:vocab, 0:emb]
    for k in range(eacc.shape[0] // LANE):
        size = max(0, min(LANE, vocab - k * LANE))
        if size:
            flipped = jnp.transpose(eacc[k * LANE:(k + 1) * LANE, :], (1, 0))
            o_grad[:, k * LANE:k * LANE + size] = flipped[LANE - 1:LANE, 0:size] * (1.0 / shards)
    loss[...] = eacc[0:1, LANE - 2:LANE - 1] * (1.0 / (shards * total_tokens))


def half_of(value, core):
    half = value.shape[0] // 2
    return lax.dynamic_slice_in_dim(value, core * half, half, 0)


def from_others(value, wa):
    return [lax.ppermute(value, "wa", [(k, (k - s) % wa) for k in range(wa)]) for s in range(1, wa)]


def after(value, earlier):
    return lax.optimization_barrier((value, earlier))[0]


def body(ids, targets, doc_lengths, block_of, embed, w_in, b_in, w_out, b_out):
    count = lax.axis_size("ctx")
    wa = lax.axis_size("wa")
    toks = ids.shape[0]
    emb, gates, width = w_in.shape
    blocks = width // LANE
    vocab = embed.shape[0]
    docs = doc_lengths.shape[0]
    vpad = ceil_to(vocab + docs, 32)
    kdim = ceil_to(emb + 3, 16)
    total_tokens = toks * count
    core = lax.axis_index("ctx") % 2

    b_hi = lax.reduce_precision(b_in, 8, 7)
    b_mid = lax.reduce_precision(b_in - b_hi, 8, 7)
    extra_rows = jnp.stack([b_hi, b_mid, b_in - b_hi - b_mid], axis=1).astype(BF16)
    fill = jnp.zeros((gates, kdim - emb - 3, width), BF16)
    w_own = jnp.concatenate([jnp.transpose(w_in, (1, 0, 2)), extra_rows, fill], axis=1)
    ones_col = (jnp.arange(kdim) >= emb) & (jnp.arange(kdim) < emb + 3)
    ones_row = jnp.arange(vpad) < vocab
    table = jnp.pad(embed, ((0, vpad - vocab), (0, kdim - emb)))
    table = jnp.where(ones_col[None, :] & ones_row[:, None], jnp.ones((), BF16), table)

    chip = lambda *shape: pltpu.VMEM(shape, F32)
    hbm = lambda shape, kind: jax.ShapeDtypeStruct(shape, kind)
    smem = lambda shape: jax.ShapeDtypeStruct(shape, jnp.int32)
    tokens = (toks * blocks, LANE)

    marked, spots, tab, seg, ends = call(
        functools.partial(own_table_kernel, vocab=vocab, blocks=blocks),
        "tables_own",
        [doc_lengths, block_of],
        [ids, table, w_own],
        [smem((toks,)), smem((docs,)), chip(vpad * 2 * blocks, LANE), chip(CHAINS, 2, blocks, LANE),
         hbm((2, blocks, LANE), F32)],
        [pltpu.SemaphoreType.DMA],
        in_spaces=[pl.ANY, pltpu.VMEM, pltpu.VMEM],
        out_spaces=[pltpu.SMEM, pltpu.SMEM, pltpu.VMEM, pltpu.VMEM, pltpu.VMEM],
    )
    tab, seg = near(tab), near(seg)
    w_far = from_others(half_of(after(w_own, ends), core), wa)
    ps_all = all_of(ends, ("ctx", "wa"))
    w_far = [after(w, ps_all) for w in w_far]
    w_oth = [v for w in w_far for v in (w, swap(w, "ctx", 1))]
    wt_own = jnp.pad(after(w_out, ps_all).T, ((0, vpad - vocab), (0, 0)))
    wt_far = from_others(half_of(wt_own, core), wa)
    wt_oth = [v for w in wt_far for v in (w, swap(w, "ctx", 1))]
    bias_out = jnp.pad(b_out, (0, vpad - vocab), constant_values=-1e30)[:, None]
    others = wa - 1
    rest = call(
        functools.partial(rest_table_kernel, vocab=vocab, blocks=blocks, others=others),
        "tables_rest",
        [marked, spots],
        [table, w_own] + w_oth,
        [chip(vpad * blocks, LANE), chip(vpad * 2 * blocks, LANE)]
        + [chip(vpad * 3 * blocks, LANE), chip(CHAINS, 2, blocks, LANE)] * others,
        micros=6,
    )
    rest = [near(r) for r in rest]
    o_tab, coef = rest[:2]

    hid, prev, src, lgrad, heads, head, o_sum, extra = call(
        functools.partial(cell_kernel, others=others, total_tokens=total_tokens, blocks=blocks),
        "cells",
        [marked, block_of],
        [ps_all, tab, o_tab, seg, wt_own, bias_out, targets[None], ids[None]] + rest[2::2] + rest[3::2] + wt_oth,
        [
            hbm((toks, width), BF16), hbm(tokens, F32), hbm(tokens, F32),
            pltpu.VMEM((vpad, toks), BF16), chip(CHAINS * blocks, LANE), hbm((blocks, LANE), F32),
            chip(vpad, width), hbm((vpad, LANE), F32),
        ],
        [
            pltpu.SMEM((count,), jnp.int32), pltpu.VMEM(tokens, F32), pltpu.VMEM(tokens, F32),
            pltpu.VMEM(tokens, F32), pltpu.VMEM((toks, width), BF16),
            pltpu.VMEM((toks, width), BF16), pltpu.VMEM((vpad, width), BF16), pltpu.VMEM((vpad, toks), F32), pltpu.VMEM(tokens, F32),
            pltpu.SemaphoreType.DMA((2,)), pltpu.SemaphoreType.DMA((toks // 512,)),
        ],
        limit=48,
        out_spaces=[pl.ANY] * 3 + [pltpu.VMEM] * 5,
        micros=26,
    )
    lgrad, heads, o_sum = map(near, (lgrad, heads, o_sum))
    splits = count // blocks
    vpart = ceil_to(-(-vpad // splits), 8)
    half_chunks = lambda rows: [hbm((count // 2, rows, LANE), F32)] * 2
    copies = 4

    part = ceil_to(-(-kdim // splits), 8)
    per = ceil_to(-(-vpad // count), 8)
    h_all = all_of(head, "ctx")
    keep_o, send_o = call(
        functools.partial(decoder_grad_kernel, count=count, blocks=blocks),
        "decoder_grad",
        [],
        [lgrad, after(hid, h_all)],
        half_chunks(vpart),
        limit=20,
    )
    got_o = swap(send_o, "ctx", 1)
    length = toks // CHAINS
    span = 16
    block = pl.BlockSpec((CHAINS, span * blocks, LANE), lambda i: (0, length // span - 1 - i, 0))
    (sums,) = call(
        functools.partial(char_sum_kernel, copies=copies, blocks=blocks),
        "char_sums",
        [marked, block_of],
        [tab, seg, heads, h_all, ps_all] + [v.reshape(CHAINS, length * blocks, LANE) for v in (prev, src)],
        [chip(2, vpad * blocks, LANE)],
        [pltpu.SMEM((count,), jnp.int32), pltpu.VMEM((CHAINS, blocks, LANE), F32)]
        + [pltpu.VMEM((vpad * blocks, LANE), F32)] * (2 * copies),
        limit=24,
        in_spaces=[pltpu.VMEM] * 5 + [block] * 2,
        micros=(9, length // span),
    )
    keep, send, keep_e, send_e = call(
        functools.partial(input_grad_kernel, count=count, part=part, vocab=vocab, blocks=blocks),
        "input_grad",
        [spots],
        [near(sums), o_sum, tab, o_tab, coef, w_own, table, extra],
        half_chunks(4 * part) + half_chunks(per),
        [pltpu.VMEM((2, vpad * blocks, LANE), F32)],
        limit=24,
        micros=5,
    )
    bit = 1
    while bit < wa:
        keep_e, send_e = keep_e + swap(keep_e, "wa", bit), send_e + swap(send_e, "wa", bit)
        bit *= 2
    groups = [part] * gates + [per, vpart]
    chunk = reduce_chunks(
        [keep, keep_e, keep_o], [swap(send, "ctx", 1), swap(send_e, "ctx", 1), got_o], groups, "ctx"
    )
    mine, theirs = gather_chunks(chunk, "ctx")
    w_grad, bi_grad, e_grad, w_out_grad, bo_grad, loss = call(
        functools.partial(finish_kernel, groups=groups, part=part, per=per, emb=emb, shards=wa, total_tokens=total_tokens),
        "finish",
        [],
        [mine, theirs],
        [
            hbm((gates, emb, width), F32), hbm((gates, width), F32), hbm((vocab, emb), F32),
            hbm((vocab, width), F32), hbm((1, vocab), F32), hbm((1, 1), F32),
        ],
        [pltpu.VMEM((ceil_to(count * per, LANE), LANE), F32)],
    )
    return (
        hid,
        loss[0, 0],
        e_grad,
        jnp.transpose(w_grad, (1, 0, 2)),
        bi_grad,
        w_out_grad.T,
        bo_grad[0],
    )


def solution(mesh):
    placed = (
        P("ctx"),
        P("ctx"),
        P(),
        P(),
        P(),
        P(None, None, "wa"),
        P(None, "wa"),
        P("wa", None),
        P(),
    )
    return jax.shard_map(
        body,
        mesh=mesh,
        in_specs=placed,
        out_specs=(
            P("ctx", "wa"),
            P(),
            P(),
            P(None, None, "wa"),
            P(None, "wa"),
            P("wa", None),
            P(),
        ),
        check_vma=False,
    )
```

```python
import functools

import jax
import jax.numpy as jnp
from jax import lax
from jax.experimental import pallas as pl
from jax.experimental.pallas import tpu as pltpu
from jax.sharding import PartitionSpec as P

CHAINS = 16
LANE = 128
F32 = jnp.float32
BF16 = jnp.bfloat16


def ceil_to(value, step):
    return -(-value // step) * step


def call(kernel, name, scalars, arrays, outs, scratch=(), limit=16, in_spaces=None, out_spaces=None, micros=1):
    spec = lambda m: m if isinstance(m, pl.BlockSpec) else pl.BlockSpec(memory_space=m)
    blocked = [m for m in in_spaces or [] if isinstance(m, pl.BlockSpec)]
    steps = micros[1] if blocked else None
    return pl.pallas_call(
        kernel,
        grid=(steps,) if blocked else (),
        in_specs=[spec(pltpu.SMEM)] * len(scalars) + [spec(m) for m in in_spaces or [pltpu.VMEM] * len(arrays)],
        out_specs=[spec(m) for m in out_spaces or [pltpu.VMEM] * len(outs)],
        out_shape=list(outs),
        scratch_shapes=list(scratch),
        compiler_params=pltpu.CompilerParams(vmem_limit_bytes=limit * 1024 * 1024),
        cost_estimate=pl.CostEstimate(
            flops=0, transcendentals=0, bytes_accessed=3000000 * (micros[0] if blocked else micros)
        ),
        name=name,
    )(*scalars, *arrays)


def near(value):
    return pltpu.with_memory_space_constraint(value, pltpu.VMEM)


def far(value):
    return pltpu.with_memory_space_constraint(value, pltpu.HBM)


def stages_of(count):
    stages, bit = [[1]], 2
    while bit < count:
        ways = min(8 if bit == 2 else 4, count // bit)
        stages.append([k * bit for k in range(1, ways)])
        bit *= ways
    return stages


def swap(value, axis, mask):
    count = lax.axis_size(axis)
    return lax.ppermute(value, axis, [(k, k ^ mask) for k in range(count)])


def exchange(copies, axis):
    return lax.all_to_all(copies, axis, 0, 0, tiled=True)


def slot_of(xor_index, count):
    place, size, bit = 0, count, 1
    for masks in stages_of(count):
        ways = len(masks) + 1
        size = size // ways
        place = place + ((xor_index // bit) % ways) * size
        bit = bit * ways
    return place


STEPS = 32766.0
BIAS = 90


def power_of_two(exponent):
    value = jnp.full(exponent.shape, 2.0 ** -BIAS, F32)
    for bit in range(7):
        on = ((exponent + BIAS) // (1 << bit)) % 2 == 1
        value = value * jnp.where(on, 2.0 ** (1 << bit), 1.0)
    return value


def coded_rows(groups):
    return ceil_to(sum(groups) + len(groups), 16)


def encode(value, groups):
    parts, exponents, at = [], [], 0
    for size in groups:
        part = value[at:at + size]
        most = jnp.max(jnp.abs(part), axis=0, keepdims=True)
        exponent = jnp.ceil(jnp.log2(jnp.maximum(most, 2.0 ** (1 - BIAS)))).astype(jnp.int32)
        exponent = jnp.clip(exponent, -BIAS, 127 - BIAS)
        parts.append(jnp.round(part * (STEPS / power_of_two(exponent))).astype(jnp.int32))
        exponents.append(exponent)
        at += size
    fill = coded_rows(groups) - at - len(groups)
    if fill:
        exponents.append(jnp.zeros((fill, value.shape[1]), jnp.int32))
    return jnp.concatenate(parts + exponents, axis=0).astype(jnp.int16)


def decode(code, groups):
    code = code.astype(jnp.int32)
    parts, at, total = [], 0, sum(groups)
    for k, size in enumerate(groups):
        unit = power_of_two(code[total + k:total + k + 1]) * (1.0 / STEPS)
        parts.append(code[at:at + size].astype(F32) * unit)
        at += size
    return jnp.concatenate(parts, axis=0)


def reduce_chunks(keeps, moved, groups, axis):
    stages = stages_of(lax.axis_size(axis))[1:]
    number = len(keeps)
    sizes = [k.shape[1] for k in keeps]
    rows, coded = sum(sizes), coded_rows(groups)
    half = keeps[0].shape[0]
    ways = len(stages[0]) + 1 if stages else 1
    code_shape = lambda size: jax.ShapeDtypeStruct((size, coded, LANE), jnp.int16)

    def first(*refs):
        ins, outs = refs[:2 * number], refs[2 * number:]
        for place in range(half):
            way, slot = place // (half // ways), place % (half // ways)
            parts = [ins[k][place] + ins[number + k][place] for k in range(number)]
            value = jnp.concatenate(parts, axis=0)
            outs[way][slot] = value if way == 0 else encode(value, groups)

    keep, *sends = call(
        first,
        "core_sum",
        [],
        list(keeps) + list(moved),
        [jax.ShapeDtypeStruct((half // ways, rows, LANE), F32)] + [code_shape(half // ways)] * (ways - 1),
        limit=24,
    )
    for k, masks in enumerate(stages):
        got = [swap(part, axis, mask) for part, mask in zip(sends, masks)]
        ways = len(stages[k + 1]) + 1 if k + 1 < len(stages) else 1
        size = keep.shape[0] // ways
        last = k + 1 == len(stages)

        def later(*refs):
            ins, outs = refs[:len(got) + 1], refs[len(got) + 1:]
            for way in range(ways):
                for slot in range(size):
                    value = ins[0][way * size + slot]
                    for ref in ins[1:]:
                        value = value + decode(ref[way * size + slot], groups)
                    outs[way][slot] = value if way == 0 and not last else encode(value, groups)

        kept = code_shape(size) if last else jax.ShapeDtypeStruct((size, rows, LANE), F32)
        keep, *sends = call(
            later, "chip_sum" + str(k), [], [keep] + got, [kept] + [code_shape(size)] * (ways - 1), limit=24
        )
    return keep


def gather_chunks(chunk, axis):
    value = chunk
    stages = stages_of(lax.axis_size(axis))
    for number, masks in enumerate(reversed(stages[1:])):
        parts = [value] + [swap(value, axis, mask) for mask in masks]
        size = value.shape[0]

        def kernel(*refs):
            for k, ref in enumerate(refs[:-1]):
                refs[-1][k * size:(k + 1) * size] = ref[...]

        shape = (size * len(parts),) + value.shape[1:]
        value = call(kernel, "chunk_join" + str(number), [], parts, [jax.ShapeDtypeStruct(shape, value.dtype)])[0]
    return value, swap(value, axis, 1)


def padded(value, rows, lanes, size):
    count = rows.stop - rows.start
    if count == 0:
        return jnp.zeros((size, LANE), F32)
    piece = value[rows, lanes]
    return piece if count == size else jnp.concatenate([piece, jnp.zeros((size - count, LANE), F32)], axis=0)


def store_pairs(keep, send, me, value_of, count, rows):
    first = me % 2 == 0
    for pair in range(count // 2):
        a, b = value_of(2 * pair), value_of(2 * pair + 1)
        slot = slot_of((2 * pair) ^ (me - me % 2), count)
        keep[slot, rows, :] = jnp.where(first, a, b)
        send[slot, rows, :] = jnp.where(first, b, a)


def tile(ref, index, blocks, kind=0, kinds=1):
    return ref.at[pl.ds(pl.multiple_of((index * kinds + kind) * blocks, blocks), blocks), :]


def spread(ref, value, first, blocks, kind=0, kinds=1):
    rows = value.shape[0]
    for b in range(blocks):
        place = pl.ds((first * kinds + kind) * blocks + b, rows, stride=kinds * blocks)
        ref[place, :] = value[:, b * LANE:(b + 1) * LANE]


def gathered(ref, first, rows, blocks, b, kind=0, kinds=1):
    return ref[pl.ds((first * kinds + kind) * blocks + b, rows, stride=kinds * blocks), :]


def stream_order(order, block_of):
    def place(d, carry):
        order[block_of[d]] = d
        return carry

    lax.fori_loop(0, block_of.shape[0], place, 0)
    return block_of[lax.axis_index("ctx")]


def segment_ends(ids, tab, toks, blocks, kinds):
    length = toks // CHAINS

    def step(r, carry):
        prod, total = list(carry[:CHAINS]), list(carry[CHAINS:])
        for s in range(CHAINS):
            at = ids[s * length + r]
            d = tile(tab, at, blocks, 0, kinds)[...]
            total[s] = d * total[s] + tile(tab, at, blocks, 1, kinds)[...]
            prod[s] = prod[s] * d
        return tuple(prod + total)

    first = [jnp.ones((blocks, LANE), F32)] * CHAINS + [jnp.zeros((blocks, LANE), F32)] * CHAINS
    carry = lax.fori_loop(0, length, step, tuple(first), unroll=2)
    return carry[:CHAINS], carry[CHAINS:]


def own_table_kernel(
    doc_lengths, block_of, ids, embed, w, w_out, marked, spots, tab, seg, ends, w_far, wt, wt_far, sem, *, vocab, blocks
):
    toks = ids.shape[0]
    copy = pltpu.make_async_copy(ids, marked, sem)
    copy.start()
    core = lax.axis_index("ctx") % 2
    shape = (wt.shape[0], w_out.shape[0])
    same = lax.broadcasted_iota(jnp.int32, shape, 0) == lax.broadcasted_iota(jnp.int32, shape, 1)
    turned = jnp.dot(same.astype(F32).astype(BF16), w_out[...], preferred_element_type=F32).astype(BF16)
    wt[...] = turned
    half = wt_far.shape[0]
    wt_far[...] = jnp.where(core == 0, turned[0:half], turned[half:2 * half])
    for g in range(w_far.shape[0]):
        w_far[g] = w[core * w_far.shape[0] + g]
    gate = [jnp.dot(embed[...], w[g], preferred_element_type=F32) for g in range(3)]
    spread(tab, jax.nn.sigmoid(gate[1] + 3.0), 0, blocks, 0, 2)
    spread(tab, jax.nn.sigmoid(gate[0]) * jnp.tanh(gate[2]), 0, blocks, 1, 2)
    copy.wait()
    start = -block_of[lax.axis_index("ctx")] * toks
    for k in range(doc_lengths.shape[0]):
        inside = (start >= 0) & (start < toks)
        at = jnp.clip(start, 0, toks - 1)
        spot = jnp.where(inside, marked[at], 0)
        spots[k] = spot
        marked[at] = jnp.where(inside, vocab + k, marked[at])
        tile(tab, vocab + k, blocks, 0, 2)[...] = jnp.zeros((blocks, LANE), F32)
        tile(tab, vocab + k, blocks, 1, 2)[...] = tile(tab, spot, blocks, 1, 2)[...]
        start = start + doc_lengths[k]
    prod, total = segment_ends(marked, tab, toks, blocks, 2)
    p_all, s_all = prod[0], total[0]
    for s in range(CHAINS):
        seg[s, 0] = prod[s]
        seg[s, 1] = total[s]
        if s:
            s_all = prod[s] * s_all + total[s]
            p_all = prod[s] * p_all
    for d in range(ends.shape[0]):
        ends[d, 0] = p_all
        ends[d, 1] = s_all


def carry_kernel(block_of, ps_all, _, bias, carry, order):
    own = stream_order(order, block_of)

    def earlier(b, c):
        return ps_all[order[b], 0] * c + ps_all[order[b], 1]

    carry[...] = lax.fori_loop(0, own, earlier, jnp.zeros(carry.shape, F32))


def rest_table_kernel(spots, embed, w, o_tab, *, vocab, blocks):
    spread(o_tab, jax.nn.sigmoid(jnp.dot(embed[...], w[3], preferred_element_type=F32)), 0, blocks)
    for k in range(spots.shape[0]):
        tile(o_tab, vocab + k, blocks)[...] = tile(o_tab, spots[k], blocks)[...]


def other_table_kernel(spots, embed, direct, passed, tab, *, vocab, blocks):
    first = lax.axis_index("ctx") % 2 == 0

    def weights(g):
        mine, theirs = direct[g % 2], passed[g % 2]
        return jnp.where(first, mine, theirs) if g < 2 else jnp.where(first, theirs, mine)

    gate = [jnp.dot(embed[...], weights(g), preferred_element_type=F32) for g in range(4)]
    spread(tab, jax.nn.sigmoid(gate[1] + 3.0), 0, blocks, 0, 3)
    spread(tab, jax.nn.sigmoid(gate[0]) * jnp.tanh(gate[2]), 0, blocks, 1, 3)
    spread(tab, jax.nn.sigmoid(gate[3]), 0, blocks, 2, 3)
    for k in range(spots.shape[0]):
        tile(tab, vocab + k, blocks, 0, 3)[...] = jnp.zeros((blocks, LANE), F32)
        for kind in (1, 2):
            tile(tab, vocab + k, blocks, kind, 3)[...] = tile(tab, spots[k], blocks, kind, 3)[...]


def cell_kernel(*refs, others, total_tokens, blocks):
    ids, tab_o, o_tab, seg_o, wt_o, bias, tgt, ids_row = refs[:8]
    carries = refs[8:9 + others]
    refs = refs[9 + others:]
    tab_x, seg_x = refs[:others], refs[others:2 * others]
    halves = refs[2 * others:4 * others]
    refs = refs[4 * others:]
    hid, prev_out, src_out, keep_o, send_o, heads, head, o_sum, sums = refs[:9]
    prev, src, hs, low, low_x, wt_x, logits, pcum, lgrad, sem, src_sems = refs[9:]
    toks = ids.shape[0]
    length = toks // CHAINS
    width = blocks * LANE
    vocab = wt_o.shape[0]
    nt = (((1,), (1,)), ((), ()))
    tn = (((0,), (0,)), ((), ()))

    def starts(piece, seg):
        c = carries[piece][...]
        out = []
        for s in range(CHAINS):
            out.append(c)
            c = seg[s, 0] * c + seg[s, 1]
        return tuple(out)

    def flatten(low):
        rows = 256

        def part(k, carry):
            at = pl.multiple_of(k * rows, rows)
            value = hs[pl.ds(at * blocks, rows * blocks), :]
            low[pl.ds(at, rows), :] = value.reshape(rows, width).astype(BF16)
            return carry

        lax.fori_loop(0, toks // rows, part, 0)

    def own_step(r, carry):
        cells, prods = list(carry[:CHAINS]), list(carry[CHAINS:])
        for s in range(CHAINS):
            t = s * length + r
            at = ids[t]
            d = tile(tab_o, at, blocks, 0, 2)[...]
            o = tile(o_tab, at, blocks)[...]
            tile(prev, t, blocks)[...] = cells[s]
            cells[s] = d * cells[s] + tile(tab_o, at, blocks, 1, 2)[...]
            prods[s] = prods[s] * d
            tile(pcum, t, blocks)[...] = prods[s]
            th = jnp.tanh(cells[s])
            h = o * th
            tile(hs, t, blocks)[...] = h
            tile(src, t, blocks)[...] = o - h * th
        return tuple(cells + prods)

    lax.fori_loop(0, length, own_step, starts(0, seg_o) + (jnp.ones((blocks, LANE), F32),) * CHAINS, unroll=2)
    save_prev = pltpu.make_async_copy(prev, prev_out, sem.at[1])
    save_prev.start()
    flatten(low)
    save = pltpu.make_async_copy(low, hid, sem.at[0])
    save.start()
    logits[...] = lax.dot_general(wt_o[...], low[...], nt, preferred_element_type=F32) + bias[...]
    first = lax.axis_index("ctx") % 2 == 0
    half = vocab // 2
    for p in range(others):
        tab = tab_x[p]
        direct, passed = halves[2 * p:2 * p + 2]
        wt_x[0:half, :] = jnp.where(first, direct[...], passed[...])
        wt_x[half:vocab, :] = jnp.where(first, passed[...], direct[...])

        def other_step(r, carry):
            cells = list(carry)
            for s in range(CHAINS):
                t = s * length + r
                at = ids[t]
                cells[s] = tile(tab, at, blocks, 0, 3)[...] * cells[s] + tile(tab, at, blocks, 1, 3)[...]
                tile(hs, t, blocks)[...] = tile(tab, at, blocks, 2, 3)[...] * jnp.tanh(cells[s])
            return tuple(cells)

        lax.fori_loop(0, length, other_step, starts(p + 1, seg_x[p]))
        flatten(low_x)
        logits[...] += lax.dot_general(wt_x[...], low_x[...], nt, preferred_element_type=F32)

    rows = 512

    def save_src(k):
        place = pl.ds(pl.multiple_of(k * rows * blocks, rows * blocks), rows * blocks)
        return pltpu.make_async_copy(src.at[place, :], src_out.at[place, :], src_sems.at[k])


    def back(k, carry):
        loss, b_grad = carry
        at = pl.multiple_of(k * rows, rows)
        part = logits[:, pl.ds(at, rows)]
        target = lax.broadcasted_iota(jnp.int32, (vocab, rows), 0) == tgt[:, pl.ds(at, rows)]
        top = jnp.max(part, axis=0, keepdims=True)
        power = jnp.exp(part - top)
        norm = jnp.sum(power, axis=0, keepdims=True)
        picked = jnp.sum(jnp.where(target, part, 0.0), axis=0, keepdims=True)
        loss = loss + (top + jnp.log(norm) - picked)
        grad = ((power / norm - jnp.where(target, 1.0, 0.0)) * (1.0 / total_tokens)).astype(BF16)
        lgrad[:, pl.ds(at, rows)] = grad
        b_grad = b_grad + jnp.sum(grad.astype(F32).reshape(vocab, rows // LANE, LANE), axis=1)
        hg = lax.dot_general(grad, wt_o[...], tn, preferred_element_type=F32)
        low_x[pl.ds(at, rows), :] = (hg * low[pl.ds(at, rows), :].astype(F32)).astype(BF16)
        for b in range(blocks):
            hs[pl.ds(at * blocks + b, rows, stride=blocks), :] = hg[:, b * LANE:(b + 1) * LANE]
        for q in range(rows // length):
            place = pl.ds((at + q * length) * blocks, length * blocks)
            grad_src = src[place, :] * hs[place, :]
            src[place, :] = grad_src
            ends = (pcum[place, :] * grad_src).reshape(length, blocks, LANE)
            tile(heads, k * (rows // length) + q, blocks)[...] = jnp.sum(ends, axis=0)
        save_src(k).start()
        return loss, b_grad

    loss, b_grad = lax.fori_loop(
        0, toks // rows, back, (jnp.zeros((1, rows), F32), jnp.zeros((vocab, LANE), F32))
    )
    lane = lax.broadcasted_iota(jnp.int32, (vocab, LANE), 1)
    row = lax.broadcasted_iota(jnp.int32, (vocab, LANE), 0)
    sums[...] = jnp.where(lane == LANE - 1, jnp.sum(b_grad, axis=1, keepdims=True), 0.0) + jnp.where(
        (lane == LANE - 2) & (row == 0), jnp.sum(loss, axis=1, keepdims=True), 0.0
    )
    grad_out = jnp.dot(lgrad[...], low[...], preferred_element_type=F32)
    part = keep_o.shape[1]
    count = head.shape[0]
    splits = count // blocks

    def piece(q):
        c, e = q // splits, q % splits
        size = max(0, min(part, vocab - e * part))
        return padded(grad_out, slice(e * part, e * part + size), slice(c * LANE, (c + 1) * LANE), part)

    store_pairs(keep_o, send_o, lax.axis_index("ctx"), piece, count, slice(0, part))
    chars = lax.broadcasted_iota(jnp.int32, (vocab, toks), 0) == ids_row[...]
    o_sum[...] = jnp.dot(chars.astype(F32).astype(BF16), low_x[...], preferred_element_type=F32)
    save.wait()
    save_prev.wait()
    for k in range(toks // rows):
        save_src(k).wait()
    total = tile(heads, CHAINS - 1, blocks)[...]
    for s in range(CHAINS - 2, -1, -1):
        total = tile(heads, s, blocks)[...] + seg_o[s, 0] * total
    for d in range(head.shape[0]):
        head[d] = total


def char_sum_kernel(
    ids, block_of, tab, seg, heads, h_all, ps_all, prev, src, sums, order, carry, *refs, copies, blocks
):
    number = pl.program_id(0)
    length = ids.shape[0] // CHAINS
    span = prev.shape[1] // blocks
    sets = [refs[2 * k:2 * k + 2] for k in range(copies)]

    @pl.when(number == 0)
    def _():
        for ref in refs:
            ref[...] = jnp.zeros_like(ref)
        own = stream_order(order, block_of)
        count = block_of.shape[0]

        def from_later(i, g):
            slot = order[count - 1 - i]
            return h_all[slot] + ps_all[slot, 0] * g

        later = lax.fori_loop(0, count - 1 - own, from_later, jnp.zeros((blocks, LANE), F32))
        for s in range(CHAINS - 1, -1, -1):
            carry[s] = later
            later = tile(heads, s, blocks)[...] + seg[s, 0] * later

    def step(i, later):
        h = list(later)
        r = span - 1 - i
        for s in range(CHAINS):
            at = ids[s * length + (pl.num_programs(0) - 1 - number) * span + r]
            here = pl.ds(pl.multiple_of(r * blocks, blocks), blocks)
            g = src[s, here, :] + h[s]
            h[s] = tile(tab, at, blocks, 0, 2)[...] * g
            cell, forget = sets[s % copies]
            tile(cell, at, blocks)[...] += g
            tile(forget, at, blocks)[...] += g * prev[s, here, :]
        return tuple(h)

    ends = lax.fori_loop(0, span, step, tuple(carry[s] for s in range(CHAINS)))
    for s in range(CHAINS):
        carry[s] = ends[s]

    @pl.when(number == pl.num_programs(0) - 1)
    def _():
        for k in range(2):
            value = refs[k][...]
            for more in sets[1:]:
                value = value + more[k][...]
            sums[k] = value


def gate_sum_kernel(spots, sums, o_sum, embed, w, extra, high, low, keep_e, send_e, merged, *, count, vocab, blocks):
    rows = high.shape[1]
    merged[...] = sums[...]
    for k in range(spots.shape[0]):
        tile(merged.at[0], spots[k], blocks)[...] += tile(merged.at[0], vocab + k, blocks)[...]
    pad = (rows - vocab) * blocks
    for q in range(2):
        merged[q, vocab * blocks:, :] = jnp.zeros((pad, LANE), F32)

    def units(value_of):
        return jnp.concatenate([value_of(b) for b in range(blocks)], axis=1)

    def column(q, b):
        return merged[q, pl.ds(b, rows, stride=blocks), :]

    def gate_of(g):
        return jnp.dot(embed[...], w[g], preferred_element_type=F32)

    both = (((1,), (1,)), ((), ()))
    in_gate, cand = jax.nn.sigmoid(gate_of(0)), jnp.tanh(gate_of(2))
    forget = jax.nn.sigmoid(gate_of(1) + 3.0)
    cell = units(lambda b: column(0, b))
    source = in_gate * cand
    parts = [
        lambda: cell * (source - source * in_gate),
        lambda: units(lambda b: column(1, b)) * (forget - forget * forget),
        lambda: cell * (in_gate - source * cand),
        lambda: o_sum[...] * (1.0 - jax.nn.sigmoid(gate_of(3))),
    ]
    part_e = jnp.zeros((rows, w.shape[1]), F32)
    for gate in range(4):
        total = parts[gate]()
        high[gate] = total.astype(BF16)
        low[gate] = (total - high[gate].astype(F32)).astype(BF16)
        part_e = part_e + lax.dot_general(high[gate], w[gate], both, preferred_element_type=F32)
        part_e = part_e + lax.dot_general(low[gate], w[gate], both, preferred_element_type=F32)
    per = keep_e.shape[1]
    wide_e = jnp.concatenate([part_e, jnp.zeros((rows, LANE - part_e.shape[1]), F32)], axis=1) + extra[...]
    wide_e = jnp.concatenate([wide_e, jnp.zeros((count * per - rows, LANE), F32)], axis=0)
    me = lax.axis_index("ctx")
    store_pairs(keep_e, send_e, me, lambda q: wide_e[q * per:(q + 1) * per, :], count, slice(0, per))


def input_grad_kernel(high, low, table, keep, send, *, count, part, blocks):
    tn = (((0,), (0,)), ((), ()))
    splits = count // blocks
    for gate in range(4):
        wide = lax.dot_general(table[...], high[gate], tn, preferred_element_type=F32)
        wide = wide + lax.dot_general(table[...], low[gate], tn, preferred_element_type=F32)

        def piece(q):
            c, e = q // splits, q % splits
            size = max(0, min(part, wide.shape[0] - e * part))
            return padded(wide, slice(e * part, e * part + size), slice(c * LANE, (c + 1) * LANE), part)

        store_pairs(keep, send, lax.axis_index("ctx"), piece, count, slice(gate * part, (gate + 1) * part))


def finish_kernel(
    mine, theirs, w_grad, b_grad, e_grad, out_grad, o_grad, loss, eacc, *, groups, part, per, emb, shards, total_tokens
):
    count = 2 * mine.shape[0]
    me = lax.axis_index("ctx")
    first = me % 2 == 0
    pairs = {}

    def chunk(q, rows):
        pair = q - q % 2
        if pair not in pairs:
            slot = slot_of(pair ^ (me - me % 2), count)
            own, other = mine[slot].astype(jnp.int32), theirs[slot].astype(jnp.int32)
            pairs[pair] = [
                decode(jnp.where(first, own, other), groups), decode(jnp.where(first, other, own), groups)
            ]
        return pairs[pair][q % 2][rows]

    cols = w_grad.shape[2] // LANE
    splits = count // cols
    vpart = groups[-1]
    vocab = out_grad.shape[0]
    for c in range(cols):
        lanes = slice(c * LANE, (c + 1) * LANE)
        for e in range(splits):
            q = c * splits + e
            size = max(0, min(part, emb - e * part))
            for gate in range(4):
                if size:
                    w_grad[e * part:e * part + size, gate, lanes] = chunk(q, slice(gate * part, gate * part + size))
                if e * part <= emb < (e + 1) * part:
                    at = gate * part + emb - e * part
                    b_grad[gate:gate + 1, lanes] = chunk(q, slice(at, at + 1))
            size = max(0, min(vpart, vocab - e * vpart))
            if size:
                at = 4 * part + per
                out_grad[e * vpart:e * vpart + size, lanes] = chunk(q, slice(at, at + size))
    for p in range(count):
        eacc[p * per:(p + 1) * per, :] = chunk(p, slice(4 * part, 4 * part + per))
    e_grad[...] = eacc[0:vocab, 0:emb]
    for k in range(eacc.shape[0] // LANE):
        size = max(0, min(LANE, vocab - k * LANE))
        if size:
            flipped = jnp.transpose(eacc[k * LANE:(k + 1) * LANE, :], (1, 0))
            o_grad[:, k * LANE:k * LANE + size] = flipped[LANE - 1:LANE, 0:size] * (1.0 / shards)
    loss[...] = eacc[0:1, LANE - 2:LANE - 1] * (1.0 / (shards * total_tokens))


def half_of(value, core):
    half = value.shape[0] // 2
    return lax.dynamic_slice_in_dim(value, core * half, half, 0)


def from_others(value, wa):
    return [lax.ppermute(value, "wa", [(k, (k - s) % wa) for k in range(wa)]) for s in range(1, wa)]


def after(value, earlier):
    return lax.optimization_barrier((value, earlier))[0]


def body(ids, targets, doc_lengths, block_of, embed, w_in, b_in, w_out, b_out):
    count = lax.axis_size("ctx")
    wa = lax.axis_size("wa")
    toks = ids.shape[0]
    emb, gates, width = w_in.shape
    blocks = width // LANE
    vocab = embed.shape[0]
    docs = doc_lengths.shape[0]
    vpad = ceil_to(vocab + docs, 32)
    kdim = ceil_to(emb + 3, 16)
    total_tokens = toks * count
    core = lax.axis_index("ctx") % 2

    b_hi = lax.reduce_precision(b_in, 8, 7)
    b_mid = lax.reduce_precision(b_in - b_hi, 8, 7)
    extra_rows = jnp.stack([b_hi, b_mid, b_in - b_hi - b_mid], axis=1).astype(BF16)
    fill = jnp.zeros((gates, kdim - emb - 3, width), BF16)
    w_own = jnp.concatenate([jnp.transpose(w_in, (1, 0, 2)), extra_rows, fill], axis=1)
    ones_col = (jnp.arange(kdim) >= emb) & (jnp.arange(kdim) < emb + 3)
    ones_row = jnp.arange(vpad) < vocab
    table = jnp.pad(embed, ((0, vpad - vocab), (0, kdim - emb)))
    table = jnp.where(ones_col[None, :] & ones_row[:, None], jnp.ones((), BF16), table)

    chip = lambda *shape: pltpu.VMEM(shape, F32)
    hbm = lambda shape, kind: jax.ShapeDtypeStruct(shape, kind)
    smem = lambda shape: jax.ShapeDtypeStruct(shape, jnp.int32)
    tokens = (toks * blocks, LANE)

    bf = lambda *shape: pltpu.HBM(shape, BF16)
    marked, spots, tab, seg, ends, w_far, wt_own, wt_far = call(
        functools.partial(own_table_kernel, vocab=vocab, blocks=blocks),
        "tables_own",
        [doc_lengths, block_of],
        [ids, table, w_own, w_out.T],
        [smem((toks,)), smem((docs,)), chip(vpad * 2 * blocks, LANE), pltpu.HBM((CHAINS, 2, blocks, LANE), F32),
         pltpu.HBM((count, 2, blocks, LANE), F32), bf(gates // 2, kdim, width), bf(vpad, width), bf(vpad // 2, width)],
        [pltpu.SemaphoreType.DMA],
        in_spaces=[pl.ANY, pltpu.VMEM, pltpu.VMEM, pltpu.VMEM],
        out_spaces=[pltpu.SMEM, pltpu.SMEM] + [pltpu.VMEM] * 6,
        micros=6,
    )
    tab = near(tab)
    w_far, seg_x, wt_far = from_others(w_far, wa), from_others(seg, wa), from_others(wt_far, wa)
    ps_all = exchange(ends, "ctx")
    bias_out = jnp.pad(b_out, (0, vpad - vocab), constant_values=-1e30)[:, None]
    (o_tab,) = call(
        functools.partial(rest_table_kernel, vocab=vocab, blocks=blocks),
        "tables_rest",
        [spots],
        [table, w_own],
        [chip(vpad * blocks, LANE)],
        micros=3,
    )
    o_tab = near(o_tab)
    (carry,) = call(
        carry_kernel, "carry", [block_of], [ps_all, o_tab, bias_out], [hbm((blocks, LANE), F32)],
        [pltpu.SMEM((count,), jnp.int32)], in_spaces=[pltpu.VMEM, pltpu.VMEM, pl.ANY],
    )
    carries = [carry] + from_others(carry, wa)
    w_far = [after(w, ps_all) for w in w_far]
    w_oth = [v for w in w_far for v in (w, swap(w, "ctx", 1))]
    wt_far = [after(w, carry) for w in wt_far]
    wt_oth = [v for w in wt_far for v in (w, swap(w, "ctx", 1))]
    others = wa - 1
    tab_x = [
        near(call(
            functools.partial(other_table_kernel, vocab=vocab, blocks=blocks),
            "tables_other",
            [spots],
            [table] + w_oth[2 * p:2 * p + 2],
            [chip(vpad * 3 * blocks, LANE)],
            micros=3,
        )[0])
        for p in range(others)
    ]

    splits = count // blocks
    vpart = ceil_to(-(-vpad // splits), 8)
    half_chunks = lambda rows: [hbm((count // 2, rows, LANE), F32)] * 2
    copies = 4
    hid, prev, src, keep_o, send_o, heads, head, o_sum, extra = call(
        functools.partial(cell_kernel, others=others, total_tokens=total_tokens, blocks=blocks),
        "cells",
        [marked],
        [tab, o_tab, seg, wt_own, bias_out, targets[None], ids[None]] + carries + tab_x + seg_x + wt_oth,
        [
            hbm((toks, width), BF16), hbm(tokens, F32), hbm(tokens, F32),
            *half_chunks(vpart), chip(CHAINS * blocks, LANE), hbm((count, blocks, LANE), F32),
            chip(vpad, width), hbm((vpad, LANE), F32),
        ],
        [
            pltpu.VMEM(tokens, F32), pltpu.VMEM(tokens, F32), pltpu.VMEM(tokens, F32),
            pltpu.VMEM((toks, width), BF16),
            pltpu.VMEM((toks, width), BF16), pltpu.VMEM((vpad, width), BF16), pltpu.VMEM((vpad, toks), F32), pltpu.VMEM(tokens, F32),
            pltpu.VMEM((vpad, toks), BF16), pltpu.SemaphoreType.DMA((2,)), pltpu.SemaphoreType.DMA((toks // 512,)),
        ],
        limit=52,
        out_spaces=[pl.ANY] * 3 + [pltpu.VMEM] * 6,
        micros=26,
    )
    heads, o_sum = near(heads), near(o_sum)
    part = ceil_to(-(-kdim // splits), 8)
    per = ceil_to(-(-vpad // count), 8)
    h_all = exchange(head, "ctx")
    got_o = swap(send_o, "ctx", 1)
    length = toks // CHAINS
    span = 16
    block = pl.BlockSpec((CHAINS, span * blocks, LANE), lambda i: (0, length // span - 1 - i, 0))
    (sums,) = call(
        functools.partial(char_sum_kernel, copies=copies, blocks=blocks),
        "char_sums",
        [marked, block_of],
        [tab, seg, heads, h_all, ps_all] + [far(v.reshape(CHAINS, length * blocks, LANE)) for v in (prev, src)],
        [chip(2, vpad * blocks, LANE)],
        [pltpu.SMEM((count,), jnp.int32), pltpu.VMEM((CHAINS, blocks, LANE), F32)]
        + [pltpu.VMEM((vpad * blocks, LANE), F32)] * (2 * copies),
        limit=24,
        in_spaces=[pltpu.VMEM] * 5 + [block] * 2,
        micros=(9, length // span),
    )
    high, low, keep_e, send_e = call(
        functools.partial(gate_sum_kernel, count=count, vocab=vocab, blocks=blocks),
        "gate_sums",
        [spots],
        [near(sums), o_sum, table, w_own, extra],
        [pltpu.VMEM((gates, vpad, width), BF16)] * 2 + half_chunks(per),
        [pltpu.VMEM((2, vpad * blocks, LANE), F32)],
        limit=24,
        micros=3,
    )
    keep, send = call(
        functools.partial(input_grad_kernel, count=count, part=part, blocks=blocks),
        "input_grad",
        [],
        [near(high), near(low), table],
        half_chunks(4 * part),
        limit=24,
        micros=3,
    )
    bit = 1
    while bit < wa:
        keep_e, send_e = keep_e + swap(keep_e, "wa", bit), send_e + swap(send_e, "wa", bit)
        bit *= 2
    groups = [part] * gates + [per, vpart]
    chunk = reduce_chunks(
        [keep, keep_e, keep_o], [swap(send, "ctx", 1), swap(send_e, "ctx", 1), got_o], groups, "ctx"
    )
    mine, theirs = gather_chunks(chunk, "ctx")
    w_grad, bi_grad, e_grad, w_out_grad, bo_grad, loss = call(
        functools.partial(finish_kernel, groups=groups, part=part, per=per, emb=emb, shards=wa, total_tokens=total_tokens),
        "finish",
        [],
        [mine, theirs],
        [
            hbm((emb, gates, width), F32), hbm((gates, width), F32), hbm((vocab, emb), F32),
            hbm((vocab, width), F32), hbm((1, vocab), F32), hbm((1, 1), F32),
        ],
        [pltpu.VMEM((ceil_to(count * per, LANE), LANE), F32)],
    )
    return (
        hid,
        loss[0, 0],
        e_grad,
        w_grad,
        bi_grad,
        w_out_grad.T,
        bo_grad[0],
    )


def solution(mesh):
    placed = (
        P("ctx"),
        P("ctx"),
        P(),
        P(),
        P(),
        P(None, None, "wa"),
        P(None, "wa"),
        P("wa", None),
        P(),
    )
    return jax.shard_map(
        body,
        mesh=mesh,
        in_specs=placed,
        out_specs=(
            P("ctx", "wa"),
            P(),
            P(),
            P(None, None, "wa"),
            P(None, "wa"),
            P("wa", None),
            P(),
        ),
        check_vma=False,
    )
```

```python
import functools

import jax
import jax.numpy as jnp
from jax import lax
from jax.experimental import pallas as pl
from jax.experimental.pallas import tpu as pltpu
from jax.sharding import PartitionSpec as P

CHAINS = 16
LANE = 128
F32 = jnp.float32
BF16 = jnp.bfloat16


def ceil_to(value, step):
    return -(-value // step) * step


def call(kernel, name, scalars, arrays, outs, scratch=(), limit=16, in_spaces=None, out_spaces=None, micros=1):
    spec = lambda m: m if isinstance(m, pl.BlockSpec) else pl.BlockSpec(memory_space=m)
    blocked = [m for m in in_spaces or [] if isinstance(m, pl.BlockSpec)]
    steps = micros[1] if blocked else None
    return pl.pallas_call(
        kernel,
        grid=(steps,) if blocked else (),
        in_specs=[spec(pltpu.SMEM)] * len(scalars) + [spec(m) for m in in_spaces or [pltpu.VMEM] * len(arrays)],
        out_specs=[spec(m) for m in out_spaces or [pltpu.VMEM] * len(outs)],
        out_shape=list(outs),
        scratch_shapes=list(scratch),
        compiler_params=pltpu.CompilerParams(vmem_limit_bytes=limit * 1024 * 1024),
        cost_estimate=pl.CostEstimate(
            flops=0, transcendentals=0, bytes_accessed=3000000 * (micros[0] if blocked else micros)
        ),
        name=name,
    )(*scalars, *arrays)


def near(value):
    return pltpu.with_memory_space_constraint(value, pltpu.VMEM)


def far(value):
    return pltpu.with_memory_space_constraint(value, pltpu.HBM)


def stages_of(count):
    stages, bit = [[1]], 2
    while bit < count:
        ways = min(8 if bit == 2 else 4, count // bit)
        stages.append([k * bit for k in range(1, ways)])
        bit *= ways
    return stages


def gather_stages_of(count):
    stages, bit = [[1]], 2
    while bit < count:
        ways = min(2 if bit == 2 else 4, count // bit)
        stages.append([k * bit for k in range(1, ways)])
        bit *= ways
    return stages


def swap(value, axis, mask):
    count = lax.axis_size(axis)
    return lax.ppermute(value, axis, [(k, k ^ mask) for k in range(count)])


def exchange(copies, axis):
    return lax.all_to_all(copies, axis, 0, 0, tiled=True)


def slot_of(xor_index, count, stages=None):
    place, size, bit = 0, count, 1
    for masks in stages or stages_of(count):
        ways = len(masks) + 1
        size = size // ways
        place = place + ((xor_index // bit) % ways) * size
        bit = bit * ways
    return place


STEPS = 32766.0
BIAS = 90


def power_of_two(exponent):
    value = jnp.full(exponent.shape, 2.0 ** -BIAS, F32)
    for bit in range(7):
        on = ((exponent + BIAS) // (1 << bit)) % 2 == 1
        value = value * jnp.where(on, 2.0 ** (1 << bit), 1.0)
    return value


def coded_rows(groups):
    return ceil_to(sum(groups) + len(groups), 16)


def encode(value, groups):
    parts, exponents, at = [], [], 0
    for size in groups:
        part = value[at:at + size]
        most = jnp.max(jnp.abs(part), axis=0, keepdims=True)
        exponent = jnp.ceil(jnp.log2(jnp.maximum(most, 2.0 ** (1 - BIAS)))).astype(jnp.int32)
        exponent = jnp.clip(exponent, -BIAS, 127 - BIAS)
        parts.append(jnp.round(part * (STEPS / power_of_two(exponent))).astype(jnp.int32))
        exponents.append(exponent)
        at += size
    fill = coded_rows(groups) - at - len(groups)
    if fill:
        exponents.append(jnp.zeros((fill, value.shape[1]), jnp.int32))
    return jnp.concatenate(parts + exponents, axis=0).astype(jnp.int16)


def decode(code, groups):
    code = code.astype(jnp.int32)
    parts, at, total = [], 0, sum(groups)
    for k, size in enumerate(groups):
        unit = power_of_two(code[total + k:total + k + 1]) * (1.0 / STEPS)
        parts.append(code[at:at + size].astype(F32) * unit)
        at += size
    return jnp.concatenate(parts, axis=0)


def reduce_chunks(keeps, moved, groups, axis):
    stages = stages_of(lax.axis_size(axis))[1:]
    number = len(keeps)
    sizes = [k.shape[1] for k in keeps]
    rows, coded = sum(sizes), coded_rows(groups)
    half = keeps[0].shape[0]
    ways = len(stages[0]) + 1 if stages else 1
    code_shape = lambda size: jax.ShapeDtypeStruct((size, coded, LANE), jnp.int16)

    def first(*refs):
        ins, outs = refs[:2 * number], refs[2 * number:]
        for place in range(half):
            way, slot = place // (half // ways), place % (half // ways)
            parts = [ins[k][place] + ins[number + k][place] for k in range(number)]
            value = jnp.concatenate(parts, axis=0)
            outs[way][slot] = value if way == 0 else encode(value, groups)

    keep, *sends = call(
        first,
        "core_sum",
        [],
        list(keeps) + list(moved),
        [jax.ShapeDtypeStruct((half // ways, rows, LANE), F32)] + [code_shape(half // ways)] * (ways - 1),
        limit=24,
    )
    for k, masks in enumerate(stages):
        got = [swap(part, axis, mask) for part, mask in zip(sends, masks)]
        ways = len(stages[k + 1]) + 1 if k + 1 < len(stages) else 1
        size = keep.shape[0] // ways
        last = k + 1 == len(stages)

        def later(*refs):
            ins, outs = refs[:len(got) + 1], refs[len(got) + 1:]
            for way in range(ways):
                for slot in range(size):
                    value = ins[0][way * size + slot]
                    for ref in ins[1:]:
                        value = value + decode(ref[way * size + slot], groups)
                    outs[way][slot] = value if way == 0 and not last else encode(value, groups)

        kept = code_shape(size) if last else jax.ShapeDtypeStruct((size, rows, LANE), F32)
        keep, *sends = call(
            later, "chip_sum" + str(k), [], [keep] + got, [kept] + [code_shape(size)] * (ways - 1), limit=24
        )
    return keep


def gather_chunks(chunk, axis):
    stages = gather_stages_of(lax.axis_size(axis))
    middle = ceil_to(chunk.shape[1] // 2, 16)
    halves = [chunk[:, :middle], chunk[:, middle:]]
    for number, masks in enumerate(reversed(stages[1:])):
        for h in range(2):
            value = halves[h]
            parts = [value] + [swap(value, axis, mask) for mask in masks]
            size = value.shape[0]

            def kernel(*refs):
                for k, ref in enumerate(refs[:-1]):
                    refs[-1][k * size:(k + 1) * size] = ref[...]

            shape = (size * len(parts),) + value.shape[1:]
            out = jax.ShapeDtypeStruct(shape, value.dtype)
            halves[h] = call(kernel, "chunk_join" + str(number), [], parts, [out])[0]
    return halves + [swap(h, axis, 1) for h in halves]


def padded(value, rows, lanes, size):
    count = rows.stop - rows.start
    if count == 0:
        return jnp.zeros((size, LANE), F32)
    piece = value[rows, lanes]
    return piece if count == size else jnp.concatenate([piece, jnp.zeros((size - count, LANE), F32)], axis=0)


def store_pairs(keep, send, me, value_of, count, rows):
    first = me % 2 == 0
    for pair in range(count // 2):
        a, b = value_of(2 * pair), value_of(2 * pair + 1)
        slot = slot_of((2 * pair) ^ (me - me % 2), count)
        keep[slot, rows, :] = jnp.where(first, a, b)
        send[slot, rows, :] = jnp.where(first, b, a)


def tile(ref, index, blocks, kind=0, kinds=1):
    return ref.at[pl.ds(pl.multiple_of((index * kinds + kind) * blocks, blocks), blocks), :]


def spread(ref, value, first, blocks, kind=0, kinds=1):
    rows = value.shape[0]
    for b in range(blocks):
        place = pl.ds((first * kinds + kind) * blocks + b, rows, stride=kinds * blocks)
        ref[place, :] = value[:, b * LANE:(b + 1) * LANE]


def gathered(ref, first, rows, blocks, b, kind=0, kinds=1):
    return ref[pl.ds((first * kinds + kind) * blocks + b, rows, stride=kinds * blocks), :]


def stream_order(order, block_of):
    def place(d, carry):
        order[block_of[d]] = d
        return carry

    lax.fori_loop(0, block_of.shape[0], place, 0)
    return block_of[lax.axis_index("ctx")]


def segment_ends(ids, tab, toks, blocks, kinds):
    length = toks // CHAINS

    def step(r, carry):
        prod, total = list(carry[:CHAINS]), list(carry[CHAINS:])
        for s in range(CHAINS):
            at = ids[s * length + r]
            d = tile(tab, at, blocks, 0, kinds)[...]
            total[s] = d * total[s] + tile(tab, at, blocks, 1, kinds)[...]
            prod[s] = prod[s] * d
        return tuple(prod + total)

    first = [jnp.ones((blocks, LANE), F32)] * CHAINS + [jnp.zeros((blocks, LANE), F32)] * CHAINS
    carry = lax.fori_loop(0, length, step, tuple(first), unroll=2)
    return carry[:CHAINS], carry[CHAINS:]


def own_table_kernel(
    doc_lengths, block_of, ids, embed, w, w_out, marked, spots, tab, seg, ends, w_far, wt, wt_far, sem, *, vocab, blocks
):
    toks = ids.shape[0]
    copy = pltpu.make_async_copy(ids, marked, sem)
    copy.start()
    core = lax.axis_index("ctx") % 2
    shape = (wt.shape[0], w_out.shape[0])
    same = lax.broadcasted_iota(jnp.int32, shape, 0) == lax.broadcasted_iota(jnp.int32, shape, 1)
    turned = jnp.dot(same.astype(F32).astype(BF16), w_out[...], preferred_element_type=F32).astype(BF16)
    wt[...] = turned
    half = wt_far.shape[0]
    wt_far[...] = jnp.where(core == 0, turned[0:half], turned[half:2 * half])
    for g in range(w_far.shape[0]):
        w_far[g] = w[core * w_far.shape[0] + g]
    gate = [jnp.dot(embed[...], w[g], preferred_element_type=F32) for g in range(3)]
    spread(tab, jax.nn.sigmoid(gate[1] + 3.0), 0, blocks, 0, 2)
    spread(tab, jax.nn.sigmoid(gate[0]) * jnp.tanh(gate[2]), 0, blocks, 1, 2)
    copy.wait()
    start = -block_of[lax.axis_index("ctx")] * toks
    for k in range(doc_lengths.shape[0]):
        inside = (start >= 0) & (start < toks)
        at = jnp.clip(start, 0, toks - 1)
        spot = jnp.where(inside, marked[at], 0)
        spots[k] = spot
        marked[at] = jnp.where(inside, vocab + k, marked[at])
        tile(tab, vocab + k, blocks, 0, 2)[...] = jnp.zeros((blocks, LANE), F32)
        tile(tab, vocab + k, blocks, 1, 2)[...] = tile(tab, spot, blocks, 1, 2)[...]
        start = start + doc_lengths[k]
    prod, total = segment_ends(marked, tab, toks, blocks, 2)
    p_all, s_all = prod[0], total[0]
    for s in range(CHAINS):
        seg[s, 0] = prod[s]
        seg[s, 1] = total[s]
        if s:
            s_all = prod[s] * s_all + total[s]
            p_all = prod[s] * p_all
    for d in range(ends.shape[0]):
        ends[d, 0] = p_all
        ends[d, 1] = s_all


def carry_kernel(block_of, ps_all, _, bias, carry, order):
    own = stream_order(order, block_of)

    def earlier(b, c):
        return ps_all[order[b], 0] * c + ps_all[order[b], 1]

    carry[...] = lax.fori_loop(0, own, earlier, jnp.zeros(carry.shape, F32))


def rest_table_kernel(spots, embed, w, o_tab, *, vocab, blocks):
    spread(o_tab, jax.nn.sigmoid(jnp.dot(embed[...], w[3], preferred_element_type=F32)), 0, blocks)
    for k in range(spots.shape[0]):
        tile(o_tab, vocab + k, blocks)[...] = tile(o_tab, spots[k], blocks)[...]


def other_table_kernel(spots, embed, direct, passed, tab, *, vocab, blocks):
    first = lax.axis_index("ctx") % 2 == 0

    def weights(g):
        mine, theirs = direct[g % 2], passed[g % 2]
        return jnp.where(first, mine, theirs) if g < 2 else jnp.where(first, theirs, mine)

    gate = [jnp.dot(embed[...], weights(g), preferred_element_type=F32) for g in range(4)]
    spread(tab, jax.nn.sigmoid(gate[1] + 3.0), 0, blocks, 0, 3)
    spread(tab, jax.nn.sigmoid(gate[0]) * jnp.tanh(gate[2]), 0, blocks, 1, 3)
    spread(tab, jax.nn.sigmoid(gate[3]), 0, blocks, 2, 3)
    for k in range(spots.shape[0]):
        tile(tab, vocab + k, blocks, 0, 3)[...] = jnp.zeros((blocks, LANE), F32)
        for kind in (1, 2):
            tile(tab, vocab + k, blocks, kind, 3)[...] = tile(tab, spots[k], blocks, kind, 3)[...]


def cell_kernel(*refs, others, total_tokens, blocks):
    ids, tab_o, o_tab, seg_o, wt_o, bias, tgt, ids_row = refs[:8]
    carries = refs[8:9 + others]
    refs = refs[9 + others:]
    tab_x, seg_x = refs[:others], refs[others:2 * others]
    halves = refs[2 * others:4 * others]
    refs = refs[4 * others:]
    hid, prev, src_out, keep_o, send_o, heads, head, o_sum, sums = refs[:9]
    src, hs, low, low_x, wt_x, logits, pcum, lgrad, sem, src_sems = refs[9:]
    toks = ids.shape[0]
    length = toks // CHAINS
    width = blocks * LANE
    vocab = wt_o.shape[0]
    nt = (((1,), (1,)), ((), ()))
    tn = (((0,), (0,)), ((), ()))

    def starts(piece, seg):
        c = carries[piece][...]
        out = []
        for s in range(CHAINS):
            out.append(c)
            c = seg[s, 0] * c + seg[s, 1]
        return tuple(out)

    def flatten(low):
        rows = 256

        def part(k, carry):
            at = pl.multiple_of(k * rows, rows)
            value = hs[pl.ds(at * blocks, rows * blocks), :]
            low[pl.ds(at, rows), :] = value.reshape(rows, width).astype(BF16)
            return carry

        lax.fori_loop(0, toks // rows, part, 0)

    def own_step(r, carry):
        cells, prods = list(carry[:CHAINS]), list(carry[CHAINS:])
        for s in range(CHAINS):
            t = s * length + r
            at = ids[t]
            d = tile(tab_o, at, blocks, 0, 2)[...]
            o = tile(o_tab, at, blocks)[...]
            tile(prev, t, blocks)[...] = cells[s]
            cells[s] = d * cells[s] + tile(tab_o, at, blocks, 1, 2)[...]
            prods[s] = prods[s] * d
            tile(pcum, t, blocks)[...] = prods[s]
            th = jnp.tanh(cells[s])
            h = o * th
            tile(hs, t, blocks)[...] = h
            tile(src, t, blocks)[...] = o - h * th
        return tuple(cells + prods)

    lax.fori_loop(0, length, own_step, starts(0, seg_o) + (jnp.ones((blocks, LANE), F32),) * CHAINS, unroll=2)
    flatten(low)
    save = pltpu.make_async_copy(low, hid, sem)
    save.start()
    logits[...] = lax.dot_general(wt_o[...], low[...], nt, preferred_element_type=F32) + bias[...]
    first = lax.axis_index("ctx") % 2 == 0
    half = vocab // 2
    for p in range(others):
        tab = tab_x[p]
        direct, passed = halves[2 * p:2 * p + 2]
        wt_x[0:half, :] = jnp.where(first, direct[...], passed[...])
        wt_x[half:vocab, :] = jnp.where(first, passed[...], direct[...])

        def other_step(r, carry):
            cells = list(carry)
            for s in range(CHAINS):
                t = s * length + r
                at = ids[t]
                cells[s] = tile(tab, at, blocks, 0, 3)[...] * cells[s] + tile(tab, at, blocks, 1, 3)[...]
                tile(hs, t, blocks)[...] = tile(tab, at, blocks, 2, 3)[...] * jnp.tanh(cells[s])
            return tuple(cells)

        lax.fori_loop(0, length, other_step, starts(p + 1, seg_x[p]), unroll=2)
        flatten(low_x)
        logits[...] += lax.dot_general(wt_x[...], low_x[...], nt, preferred_element_type=F32)

    rows = 512

    def save_src(k):
        place = pl.ds(pl.multiple_of(k * rows * blocks, rows * blocks), rows * blocks)
        return pltpu.make_async_copy(src.at[place, :], src_out.at[place, :], src_sems.at[k])


    def back(k, carry):
        loss, b_grad = carry
        at = pl.multiple_of(k * rows, rows)
        part = logits[:, pl.ds(at, rows)]
        target = lax.broadcasted_iota(jnp.int32, (vocab, rows), 0) == tgt[:, pl.ds(at, rows)]
        top = jnp.max(part, axis=0, keepdims=True)
        power = jnp.exp(part - top)
        norm = jnp.sum(power, axis=0, keepdims=True)
        picked = jnp.sum(jnp.where(target, part, 0.0), axis=0, keepdims=True)
        loss = loss + (top + jnp.log(norm) - picked)
        share = power * ((1.0 / norm) * (1.0 / total_tokens))
        grad = (share - jnp.where(target, 1.0 / total_tokens, 0.0)).astype(BF16)
        lgrad[:, pl.ds(at, rows)] = grad
        b_grad = b_grad + jnp.sum(grad.astype(F32).reshape(vocab, rows // LANE, LANE), axis=1)
        hg = lax.dot_general(grad, wt_o[...], tn, preferred_element_type=F32)
        low_x[pl.ds(at, rows), :] = (hg * low[pl.ds(at, rows), :].astype(F32)).astype(BF16)
        for b in range(blocks):
            hs[pl.ds(at * blocks + b, rows, stride=blocks), :] = hg[:, b * LANE:(b + 1) * LANE]
        for q in range(rows // length):
            place = pl.ds((at + q * length) * blocks, length * blocks)
            grad_src = src[place, :] * hs[place, :]
            src[place, :] = grad_src
            ends = (pcum[place, :] * grad_src).reshape(length, blocks, LANE)
            tile(heads, k * (rows // length) + q, blocks)[...] = jnp.sum(ends, axis=0)
        save_src(k).start()
        return loss, b_grad

    loss, b_grad = lax.fori_loop(
        0, toks // rows, back, (jnp.zeros((1, rows), F32), jnp.zeros((vocab, LANE), F32))
    )
    lane = lax.broadcasted_iota(jnp.int32, (vocab, LANE), 1)
    row = lax.broadcasted_iota(jnp.int32, (vocab, LANE), 0)
    sums[...] = jnp.where(lane == LANE - 1, jnp.sum(b_grad, axis=1, keepdims=True), 0.0) + jnp.where(
        (lane == LANE - 2) & (row == 0), jnp.sum(loss, axis=1, keepdims=True), 0.0
    )
    grad_out = jnp.dot(lgrad[...], low[...], preferred_element_type=F32)
    part = keep_o.shape[1]
    count = head.shape[0]
    splits = count // blocks

    def piece(q):
        c, e = q // splits, q % splits
        size = max(0, min(part, vocab - e * part))
        return padded(grad_out, slice(e * part, e * part + size), slice(c * LANE, (c + 1) * LANE), part)

    store_pairs(keep_o, send_o, lax.axis_index("ctx"), piece, count, slice(0, part))
    chars = lax.broadcasted_iota(jnp.int32, (vocab, toks), 0) == ids_row[...]
    o_sum[...] = jnp.dot(chars.astype(F32).astype(BF16), low_x[...], preferred_element_type=F32)
    save.wait()
    for k in range(toks // rows):
        save_src(k).wait()
    total = tile(heads, CHAINS - 1, blocks)[...]
    for s in range(CHAINS - 2, -1, -1):
        total = tile(heads, s, blocks)[...] + seg_o[s, 0] * total
    for d in range(head.shape[0]):
        head[d] = total


def char_sum_kernel(
    ids, block_of, tab, seg, heads, h_all, ps_all, prev, src, sums, order, carry, *refs, copies, blocks
):
    number = pl.program_id(0)
    length = ids.shape[0] // CHAINS
    span = src.shape[1] // blocks
    sets = [refs[2 * k:2 * k + 2] for k in range(copies)]

    @pl.when(number == 0)
    def _():
        for ref in refs:
            ref[...] = jnp.zeros_like(ref)
        own = stream_order(order, block_of)
        count = block_of.shape[0]

        def from_later(i, g):
            slot = order[count - 1 - i]
            return h_all[slot] + ps_all[slot, 0] * g

        later = lax.fori_loop(0, count - 1 - own, from_later, jnp.zeros((blocks, LANE), F32))
        for s in range(CHAINS - 1, -1, -1):
            carry[s] = later
            later = tile(heads, s, blocks)[...] + seg[s, 0] * later

    def step(i, later):
        h = list(later)
        r = span - 1 - i
        for s in range(CHAINS):
            token = s * length + (pl.num_programs(0) - 1 - number) * span + r
            at = ids[token]
            here = pl.ds(pl.multiple_of(r * blocks, blocks), blocks)
            g = src[s, here, :] + h[s]
            h[s] = tile(tab, at, blocks, 0, 2)[...] * g
            cell, forget = sets[s % copies]
            tile(cell, at, blocks)[...] += g
            tile(forget, at, blocks)[...] += g * tile(prev, token, blocks)[...]
        return tuple(h)

    ends = lax.fori_loop(0, span, step, tuple(carry[s] for s in range(CHAINS)))
    for s in range(CHAINS):
        carry[s] = ends[s]

    @pl.when(number == pl.num_programs(0) - 1)
    def _():
        for k in range(2):
            value = refs[k][...]
            for more in sets[1:]:
                value = value + more[k][...]
            sums[k] = value


def gate_sum_kernel(spots, sums, o_sum, embed, w, extra, high, low, keep_e, send_e, merged, *, count, vocab, blocks):
    rows = high.shape[1]
    merged[...] = sums[...]
    for k in range(spots.shape[0]):
        tile(merged.at[0], spots[k], blocks)[...] += tile(merged.at[0], vocab + k, blocks)[...]
    pad = (rows - vocab) * blocks
    for q in range(2):
        merged[q, vocab * blocks:, :] = jnp.zeros((pad, LANE), F32)

    def units(value_of):
        return jnp.concatenate([value_of(b) for b in range(blocks)], axis=1)

    def column(q, b):
        return merged[q, pl.ds(b, rows, stride=blocks), :]

    def gate_of(g):
        return jnp.dot(embed[...], w[g], preferred_element_type=F32)

    both = (((1,), (1,)), ((), ()))
    in_gate, cand = jax.nn.sigmoid(gate_of(0)), jnp.tanh(gate_of(2))
    forget = jax.nn.sigmoid(gate_of(1) + 3.0)
    cell = units(lambda b: column(0, b))
    source = in_gate * cand
    parts = [
        lambda: cell * (source - source * in_gate),
        lambda: units(lambda b: column(1, b)) * (forget - forget * forget),
        lambda: cell * (in_gate - source * cand),
        lambda: o_sum[...] * (1.0 - jax.nn.sigmoid(gate_of(3))),
    ]
    part_e = jnp.zeros((rows, w.shape[1]), F32)
    for gate in range(4):
        total = parts[gate]()
        high[gate] = total.astype(BF16)
        low[gate] = (total - high[gate].astype(F32)).astype(BF16)
        part_e = part_e + lax.dot_general(high[gate], w[gate], both, preferred_element_type=F32)
        part_e = part_e + lax.dot_general(low[gate], w[gate], both, preferred_element_type=F32)
    per = keep_e.shape[1]
    wide_e = jnp.concatenate([part_e, jnp.zeros((rows, LANE - part_e.shape[1]), F32)], axis=1) + extra[...]
    wide_e = jnp.concatenate([wide_e, jnp.zeros((count * per - rows, LANE), F32)], axis=0)
    me = lax.axis_index("ctx")
    store_pairs(keep_e, send_e, me, lambda q: wide_e[q * per:(q + 1) * per, :], count, slice(0, per))


def input_grad_kernel(high, low, table, keep, send, *, count, part, blocks):
    tn = (((0,), (0,)), ((), ()))
    splits = count // blocks
    for gate in range(4):
        wide = lax.dot_general(table[...], high[gate], tn, preferred_element_type=F32)
        wide = wide + lax.dot_general(table[...], low[gate], tn, preferred_element_type=F32)

        def piece(q):
            c, e = q // splits, q % splits
            size = max(0, min(part, wide.shape[0] - e * part))
            return padded(wide, slice(e * part, e * part + size), slice(c * LANE, (c + 1) * LANE), part)

        store_pairs(keep, send, lax.axis_index("ctx"), piece, count, slice(gate * part, (gate + 1) * part))


def finish_kernel(
    mine_a, mine_b, theirs_a, theirs_b, w_grad, b_grad, e_grad, out_grad, o_grad, loss, eacc, *, groups, part, per, emb, shards, total_tokens
):
    count = 2 * mine_a.shape[0]
    me = lax.axis_index("ctx")
    first = me % 2 == 0
    pairs = {}
    stages = gather_stages_of(count)

    def chunk(q, rows):
        pair = q - q % 2
        if pair not in pairs:
            slot = slot_of(pair ^ (me - me % 2), count, stages)
            own, other = (
                jnp.concatenate([a[slot].astype(jnp.int32), b[slot].astype(jnp.int32)], axis=0)
                for a, b in ((mine_a, mine_b), (theirs_a, theirs_b))
            )
            pairs[pair] = [
                decode(jnp.where(first, own, other), groups), decode(jnp.where(first, other, own), groups)
            ]
        return pairs[pair][q % 2][rows]

    cols = w_grad.shape[2] // LANE
    splits = count // cols
    vpart = groups[-1]
    vocab = out_grad.shape[0]
    for c in range(cols):
        lanes = slice(c * LANE, (c + 1) * LANE)
        for e in range(splits):
            q = c * splits + e
            size = max(0, min(part, emb - e * part))
            for gate in range(4):
                if size:
                    w_grad[e * part:e * part + size, gate, lanes] = chunk(q, slice(gate * part, gate * part + size))
                if e * part <= emb < (e + 1) * part:
                    at = gate * part + emb - e * part
                    b_grad[gate:gate + 1, lanes] = chunk(q, slice(at, at + 1))
            size = max(0, min(vpart, vocab - e * vpart))
            if size:
                at = 4 * part + per
                out_grad[e * vpart:e * vpart + size, lanes] = chunk(q, slice(at, at + size))
    for p in range(count):
        eacc[p * per:(p + 1) * per, :] = chunk(p, slice(4 * part, 4 * part + per))
    e_grad[...] = eacc[0:vocab, 0:emb]
    for k in range(eacc.shape[0] // LANE):
        size = max(0, min(LANE, vocab - k * LANE))
        if size:
            flipped = jnp.transpose(eacc[k * LANE:(k + 1) * LANE, :], (1, 0))
            o_grad[:, k * LANE:k * LANE + size] = flipped[LANE - 1:LANE, 0:size] * (1.0 / shards)
    loss[...] = eacc[0:1, LANE - 2:LANE - 1] * (1.0 / (shards * total_tokens))


def half_of(value, core):
    half = value.shape[0] // 2
    return lax.dynamic_slice_in_dim(value, core * half, half, 0)


def from_others(value, wa):
    return [lax.ppermute(value, "wa", [(k, (k - s) % wa) for k in range(wa)]) for s in range(1, wa)]


def after(value, earlier):
    return lax.optimization_barrier((value, earlier))[0]


def body(ids, targets, doc_lengths, block_of, embed, w_in, b_in, w_out, b_out):
    count = lax.axis_size("ctx")
    wa = lax.axis_size("wa")
    toks = ids.shape[0]
    emb, gates, width = w_in.shape
    blocks = width // LANE
    vocab = embed.shape[0]
    docs = doc_lengths.shape[0]
    vpad = ceil_to(vocab + docs, 32)
    kdim = ceil_to(emb + 3, 16)
    total_tokens = toks * count
    core = lax.axis_index("ctx") % 2

    b_hi = lax.reduce_precision(b_in, 8, 7)
    b_mid = lax.reduce_precision(b_in - b_hi, 8, 7)
    extra_rows = jnp.stack([b_hi, b_mid, b_in - b_hi - b_mid], axis=1).astype(BF16)
    fill = jnp.zeros((gates, kdim - emb - 3, width), BF16)
    w_own = jnp.concatenate([jnp.transpose(w_in, (1, 0, 2)), extra_rows, fill], axis=1)
    ones_col = (jnp.arange(kdim) >= emb) & (jnp.arange(kdim) < emb + 3)
    ones_row = jnp.arange(vpad) < vocab
    table = jnp.pad(embed, ((0, vpad - vocab), (0, kdim - emb)))
    table = jnp.where(ones_col[None, :] & ones_row[:, None], jnp.ones((), BF16), table)

    chip = lambda *shape: pltpu.VMEM(shape, F32)
    hbm = lambda shape, kind: jax.ShapeDtypeStruct(shape, kind)
    smem = lambda shape: jax.ShapeDtypeStruct(shape, jnp.int32)
    tokens = (toks * blocks, LANE)

    bf = lambda *shape: pltpu.HBM(shape, BF16)
    marked, spots, tab, seg, ends, w_far, wt_own, wt_far = call(
        functools.partial(own_table_kernel, vocab=vocab, blocks=blocks),
        "tables_own",
        [doc_lengths, block_of],
        [ids, table, w_own, w_out.T],
        [smem((toks,)), smem((docs,)), chip(vpad * 2 * blocks, LANE), pltpu.HBM((CHAINS, 2, blocks, LANE), F32),
         pltpu.HBM((count, 2, blocks, LANE), F32), bf(gates // 2, kdim, width), bf(vpad, width), bf(vpad // 2, width)],
        [pltpu.SemaphoreType.DMA],
        in_spaces=[pl.ANY, pltpu.VMEM, pltpu.VMEM, pltpu.VMEM],
        out_spaces=[pltpu.SMEM, pltpu.SMEM] + [pltpu.VMEM] * 6,
        micros=6,
    )
    tab = near(tab)
    w_far, seg_x, wt_far = from_others(w_far, wa), from_others(seg, wa), from_others(wt_far, wa)
    ps_all = exchange(ends, "ctx")
    bias_out = jnp.pad(b_out, (0, vpad - vocab), constant_values=-1e30)[:, None]
    (o_tab,) = call(
        functools.partial(rest_table_kernel, vocab=vocab, blocks=blocks),
        "tables_rest",
        [spots],
        [table, w_own],
        [chip(vpad * blocks, LANE)],
        micros=3,
    )
    o_tab = near(o_tab)
    (carry,) = call(
        carry_kernel, "carry", [block_of], [ps_all, o_tab, bias_out], [hbm((blocks, LANE), F32)],
        [pltpu.SMEM((count,), jnp.int32)], in_spaces=[pltpu.VMEM, pltpu.VMEM, pl.ANY],
    )
    carries = [carry] + from_others(carry, wa)
    w_far = [after(w, ps_all) for w in w_far]
    w_oth = [v for w in w_far for v in (w, swap(w, "ctx", 1))]
    wt_far = [after(w, carry) for w in wt_far]
    wt_oth = [v for w in wt_far for v in (w, swap(w, "ctx", 1))]
    others = wa - 1
    tab_x = [
        near(call(
            functools.partial(other_table_kernel, vocab=vocab, blocks=blocks),
            "tables_other",
            [spots],
            [table] + w_oth[2 * p:2 * p + 2],
            [chip(vpad * 3 * blocks, LANE)],
            micros=3,
        )[0])
        for p in range(others)
    ]

    splits = count // blocks
    vpart = ceil_to(-(-vpad // splits), 8)
    half_chunks = lambda rows: [hbm((count // 2, rows, LANE), F32)] * 2
    copies = 4
    hid, prev, src, keep_o, send_o, heads, head, o_sum, extra = call(
        functools.partial(cell_kernel, others=others, total_tokens=total_tokens, blocks=blocks),
        "cells",
        [marked],
        [tab, o_tab, seg, wt_own, bias_out, targets[None], ids[None]] + carries + tab_x + seg_x + wt_oth,
        [
            hbm((toks, width), BF16), chip(*tokens), hbm(tokens, F32),
            *half_chunks(vpart), chip(CHAINS * blocks, LANE), hbm((count, blocks, LANE), F32),
            chip(vpad, width), hbm((vpad, LANE), F32),
        ],
        [
            pltpu.VMEM(tokens, F32), pltpu.VMEM(tokens, F32), pltpu.VMEM((toks, width), BF16),
            pltpu.VMEM((toks, width), BF16), pltpu.VMEM((vpad, width), BF16), pltpu.VMEM((vpad, toks), F32), pltpu.VMEM(tokens, F32),
            pltpu.VMEM((vpad, toks), BF16), pltpu.SemaphoreType.DMA, pltpu.SemaphoreType.DMA((toks // 512,)),
        ],
        limit=44,
        out_spaces=[pl.ANY, pltpu.VMEM, pl.ANY] + [pltpu.VMEM] * 6,
        micros=26,
    )
    prev, heads, o_sum = near(prev), near(heads), near(o_sum)
    part = ceil_to(-(-kdim // splits), 8)
    per = ceil_to(-(-vpad // count), 8)
    h_all = exchange(head, "ctx")
    got_o = swap(send_o, "ctx", 1)
    length = toks // CHAINS
    span = 32
    block = pl.BlockSpec((CHAINS, span * blocks, LANE), lambda i: (0, length // span - 1 - i, 0))
    (sums,) = call(
        functools.partial(char_sum_kernel, copies=copies, blocks=blocks),
        "char_sums",
        [marked, block_of],
        [tab, seg, heads, h_all, ps_all, prev, far(src.reshape(CHAINS, length * blocks, LANE))],
        [chip(2, vpad * blocks, LANE)],
        [pltpu.SMEM((count,), jnp.int32), pltpu.VMEM((CHAINS, blocks, LANE), F32)]
        + [pltpu.VMEM((vpad * blocks, LANE), F32)] * (2 * copies),
        limit=24,
        in_spaces=[pltpu.VMEM] * 6 + [block],
        micros=(9, length // span),
    )
    high, low, keep_e, send_e = call(
        functools.partial(gate_sum_kernel, count=count, vocab=vocab, blocks=blocks),
        "gate_sums",
        [spots],
        [near(sums), o_sum, table, w_own, extra],
        [pltpu.VMEM((gates, vpad, width), BF16)] * 2 + half_chunks(per),
        [pltpu.VMEM((2, vpad * blocks, LANE), F32)],
        limit=24,
        micros=3,
    )
    keep, send = call(
        functools.partial(input_grad_kernel, count=count, part=part, blocks=blocks),
        "input_grad",
        [],
        [near(high), near(low), table],
        half_chunks(4 * part),
        limit=24,
        micros=3,
    )
    bit = 1
    while bit < wa:
        keep_e, send_e = keep_e + swap(keep_e, "wa", bit), send_e + swap(send_e, "wa", bit)
        bit *= 2
    groups = [part] * gates + [per, vpart]
    chunk = reduce_chunks(
        [keep, keep_e, keep_o], [swap(send, "ctx", 1), swap(send_e, "ctx", 1), got_o], groups, "ctx"
    )
    halves = gather_chunks(chunk, "ctx")
    w_grad, bi_grad, e_grad, w_out_grad, bo_grad, loss = call(
        functools.partial(finish_kernel, groups=groups, part=part, per=per, emb=emb, shards=wa, total_tokens=total_tokens),
        "finish",
        [],
        halves,
        [
            hbm((emb, gates, width), F32), hbm((gates, width), F32), hbm((vocab, emb), F32),
            hbm((vocab, width), F32), hbm((1, vocab), F32), hbm((1, 1), F32),
        ],
        [pltpu.VMEM((ceil_to(count * per, LANE), LANE), F32)],
    )
    return (
        hid,
        loss[0, 0],
        e_grad,
        w_grad,
        bi_grad,
        w_out_grad.T,
        bo_grad[0],
    )


def solution(mesh):
    placed = (
        P("ctx"),
        P("ctx"),
        P(),
        P(),
        P(),
        P(None, None, "wa"),
        P(None, "wa"),
        P("wa", None),
        P(),
    )
    return jax.shard_map(
        body,
        mesh=mesh,
        in_specs=placed,
        out_specs=(
            P("ctx", "wa"),
            P(),
            P(),
            P(None, None, "wa"),
            P(None, "wa"),
            P("wa", None),
            P(),
        ),
        check_vma=False,
    )
```

```python
import functools

import jax
import jax.numpy as jnp
from jax import lax
from jax.experimental import pallas as pl
from jax.experimental.pallas import tpu as pltpu
from jax.sharding import PartitionSpec as P

CHAINS = 16
LANE = 128
F32 = jnp.float32
BF16 = jnp.bfloat16


def ceil_to(value, step):
    return -(-value // step) * step


def call(kernel, name, scalars, arrays, outs, scratch=(), limit=16, in_spaces=None, out_spaces=None, micros=1):
    spec = lambda m: m if isinstance(m, pl.BlockSpec) else pl.BlockSpec(memory_space=m)
    blocked = [m for m in in_spaces or [] if isinstance(m, pl.BlockSpec)]
    steps = micros[1] if blocked else None
    return pl.pallas_call(
        kernel,
        grid=(steps,) if blocked else (),
        in_specs=[spec(pltpu.SMEM)] * len(scalars) + [spec(m) for m in in_spaces or [pltpu.VMEM] * len(arrays)],
        out_specs=[spec(m) for m in out_spaces or [pltpu.VMEM] * len(outs)],
        out_shape=list(outs),
        scratch_shapes=list(scratch),
        compiler_params=pltpu.CompilerParams(vmem_limit_bytes=limit * 1024 * 1024),
        cost_estimate=pl.CostEstimate(
            flops=0, transcendentals=0, bytes_accessed=3000000 * (micros[0] if blocked else micros)
        ),
        name=name,
    )(*scalars, *arrays)


def near(value):
    return pltpu.with_memory_space_constraint(value, pltpu.VMEM)


def far(value):
    return pltpu.with_memory_space_constraint(value, pltpu.HBM)


def stages_of(count):
    stages, bit = [[1]], 2
    while bit < count:
        ways = min(8 if bit == 2 else 4, count // bit)
        stages.append([k * bit for k in range(1, ways)])
        bit *= ways
    return stages


def gather_stages_of(count):
    stages, bit = [[1]], 2
    while bit < count:
        ways = min(2 if bit == 2 else 4, count // bit)
        stages.append([k * bit for k in range(1, ways)])
        bit *= ways
    return stages


def swap(value, axis, mask):
    count = lax.axis_size(axis)
    return lax.ppermute(value, axis, [(k, k ^ mask) for k in range(count)])


def exchange(copies, axis):
    return lax.all_to_all(copies, axis, 0, 0, tiled=True)


def slot_of(xor_index, count, stages=None):
    place, size, bit = 0, count, 1
    for masks in stages or stages_of(count):
        ways = len(masks) + 1
        size = size // ways
        place = place + ((xor_index // bit) % ways) * size
        bit = bit * ways
    return place


STEPS = 32766.0
BIAS = 90


def power_of_two(exponent):
    value = jnp.full(exponent.shape, 2.0 ** -BIAS, F32)
    for bit in range(7):
        on = ((exponent + BIAS) // (1 << bit)) % 2 == 1
        value = value * jnp.where(on, 2.0 ** (1 << bit), 1.0)
    return value


def section_rows(groups):
    return ceil_to(sum(groups) + len(groups), 16)


def coded_rows(sections):
    return sum(section_rows(groups) for groups in sections)


def encode_all(value, sections):
    parts, at = [], 0
    for groups in sections:
        parts.append(encode(value[at:at + sum(groups)], groups))
        at += sum(groups)
    return jnp.concatenate(parts, axis=0)


def decode_all(code, sections):
    parts, at = [], 0
    for groups in sections:
        parts.append(decode(code[at:at + section_rows(groups)], groups))
        at += section_rows(groups)
    return jnp.concatenate(parts, axis=0)


def encode(value, groups):
    parts, exponents, at = [], [], 0
    for size in groups:
        part = value[at:at + size]
        most = jnp.max(jnp.abs(part), axis=0, keepdims=True)
        exponent = jnp.ceil(jnp.log2(jnp.maximum(most, 2.0 ** (1 - BIAS)))).astype(jnp.int32)
        exponent = jnp.clip(exponent, -BIAS, 127 - BIAS)
        parts.append(jnp.round(part * (STEPS / power_of_two(exponent))).astype(jnp.int32))
        exponents.append(exponent)
        at += size
    fill = section_rows(groups) - at - len(groups)
    if fill:
        exponents.append(jnp.zeros((fill, value.shape[1]), jnp.int32))
    return jnp.concatenate(parts + exponents, axis=0).astype(jnp.int16)


def decode(code, groups):
    code = code.astype(jnp.int32)
    parts, at, total = [], 0, sum(groups)
    for k, size in enumerate(groups):
        unit = power_of_two(code[total + k:total + k + 1]) * (1.0 / STEPS)
        parts.append(code[at:at + size].astype(F32) * unit)
        at += size
    return jnp.concatenate(parts, axis=0)


def reduce_chunks(keeps, moved, sections, axis):
    stages = stages_of(lax.axis_size(axis))[1:]
    number = len(keeps)
    sizes = [k.shape[1] for k in keeps]
    rows, coded = sum(sizes), coded_rows(sections)
    half = keeps[0].shape[0]
    ways = len(stages[0]) + 1 if stages else 1
    code_shape = lambda size: jax.ShapeDtypeStruct((size, coded, LANE), jnp.int16)

    def first(*refs):
        ins, outs = refs[:2 * number], refs[2 * number:]
        for place in range(half):
            way, slot = place // (half // ways), place % (half // ways)
            parts = [ins[k][place] + ins[number + k][place] for k in range(number)]
            value = jnp.concatenate(parts, axis=0)
            outs[way][slot] = value if way == 0 else encode_all(value, sections)

    keep, *sends = call(
        first,
        "core_sum",
        [],
        list(keeps) + list(moved),
        [jax.ShapeDtypeStruct((half // ways, rows, LANE), F32)] + [code_shape(half // ways)] * (ways - 1),
        limit=24,
    )
    for k, masks in enumerate(stages):
        got = [swap(part, axis, mask) for part, mask in zip(sends, masks)]
        ways = len(stages[k + 1]) + 1 if k + 1 < len(stages) else 1
        size = keep.shape[0] // ways
        last = k + 1 == len(stages)

        def later(*refs):
            ins, outs = refs[:len(got) + 1], refs[len(got) + 1:]
            for way in range(ways):
                for slot in range(size):
                    value = ins[0][way * size + slot]
                    for ref in ins[1:]:
                        value = value + decode_all(ref[way * size + slot], sections)
                    outs[way][slot] = value if way == 0 and not last else encode_all(value, sections)

        kept = code_shape(size) if last else jax.ShapeDtypeStruct((size, rows, LANE), F32)
        keep, *sends = call(
            later, "chip_sum" + str(k), [], [keep] + got, [kept] + [code_shape(size)] * (ways - 1), limit=24
        )
    return keep


def gather_chunks(chunk, axis, apart):
    stages = gather_stages_of(lax.axis_size(axis))
    middle = ceil_to(chunk.shape[1] // 2, 16)
    halves, tail = [chunk[:, :middle], chunk[:, middle:]], None
    for number, masks in enumerate(reversed(stages[1:])):
        for h in range(2):
            value = halves[h]
            parts = [value] + [swap(value, axis, mask) for mask in masks]
            size, rows = value.shape[0], value.shape[1]
            outs = [jax.ShapeDtypeStruct((size * len(parts), rows, LANE), value.dtype)]
            if h == 1 and number == len(stages) - 2:
                outs.append(jax.ShapeDtypeStruct((size * len(parts), apart, LANE), value.dtype))

            def kernel(*refs):
                for k in range(len(parts)):
                    for out in refs[len(parts):]:
                        out[k * size:(k + 1) * size] = refs[k][:, rows - out.shape[1]:, :]

            got = call(kernel, "chunk_join" + str(number), [], parts, outs)
            halves[h], tail = got[0], got[-1]
    return halves + [swap(h, axis, 1) for h in halves], tail


def padded(value, rows, lanes, size):
    count = rows.stop - rows.start
    if count == 0:
        return jnp.zeros((size, LANE), F32)
    piece = value[rows, lanes]
    return piece if count == size else jnp.concatenate([piece, jnp.zeros((size - count, LANE), F32)], axis=0)


def store_pairs(keep, send, me, value_of, count, rows):
    first = me % 2 == 0
    for pair in range(count // 2):
        a, b = value_of(2 * pair), value_of(2 * pair + 1)
        slot = slot_of((2 * pair) ^ (me - me % 2), count)
        keep[slot, rows, :] = jnp.where(first, a, b)
        send[slot, rows, :] = jnp.where(first, b, a)


def tile(ref, index, blocks, kind=0, kinds=1):
    return ref.at[pl.ds(pl.multiple_of((index * kinds + kind) * blocks, blocks), blocks), :]


def spread(ref, value, first, blocks, kind=0, kinds=1):
    rows = value.shape[0]
    for b in range(blocks):
        place = pl.ds((first * kinds + kind) * blocks + b, rows, stride=kinds * blocks)
        ref[place, :] = value[:, b * LANE:(b + 1) * LANE]


def gathered(ref, first, rows, blocks, b, kind=0, kinds=1):
    return ref[pl.ds((first * kinds + kind) * blocks + b, rows, stride=kinds * blocks), :]


def stream_order(order, block_of):
    def place(d, carry):
        order[block_of[d]] = d
        return carry

    lax.fori_loop(0, block_of.shape[0], place, 0)
    return block_of[lax.axis_index("ctx")]


def segment_ends(ids, tab, toks, blocks, kinds):
    length = toks // CHAINS

    def step(r, carry):
        prod, total = list(carry[:CHAINS]), list(carry[CHAINS:])
        for s in range(CHAINS):
            at = ids[s * length + r]
            d = tile(tab, at, blocks, 0, kinds)[...]
            total[s] = d * total[s] + tile(tab, at, blocks, 1, kinds)[...]
            prod[s] = prod[s] * d
        return tuple(prod + total)

    first = [jnp.ones((blocks, LANE), F32)] * CHAINS + [jnp.zeros((blocks, LANE), F32)] * CHAINS
    carry = lax.fori_loop(0, length, step, tuple(first), unroll=2)
    return carry[:CHAINS], carry[CHAINS:]


def own_table_kernel(
    doc_lengths, block_of, ids, embed, w, w_out, marked, spots, tab, seg, ends, w_far, wt, wt_far, sem, *, vocab, blocks
):
    toks = ids.shape[0]
    copy = pltpu.make_async_copy(ids, marked, sem)
    copy.start()
    core = lax.axis_index("ctx") % 2
    shape = (wt.shape[0], w_out.shape[0])
    same = lax.broadcasted_iota(jnp.int32, shape, 0) == lax.broadcasted_iota(jnp.int32, shape, 1)
    turned = jnp.dot(same.astype(F32).astype(BF16), w_out[...], preferred_element_type=F32).astype(BF16)
    wt[...] = turned
    half = wt_far.shape[0]
    wt_far[...] = jnp.where(core == 0, turned[0:half], turned[half:2 * half])
    for g in range(w_far.shape[0]):
        w_far[g] = w[core * w_far.shape[0] + g]
    gate = [jnp.dot(embed[...], w[g], preferred_element_type=F32) for g in range(3)]
    spread(tab, jax.nn.sigmoid(gate[1] + 3.0), 0, blocks, 0, 2)
    spread(tab, jax.nn.sigmoid(gate[0]) * jnp.tanh(gate[2]), 0, blocks, 1, 2)
    copy.wait()
    start = -block_of[lax.axis_index("ctx")] * toks
    for k in range(doc_lengths.shape[0]):
        inside = (start >= 0) & (start < toks)
        at = jnp.clip(start, 0, toks - 1)
        spot = jnp.where(inside, marked[at], 0)
        spots[k] = spot
        marked[at] = jnp.where(inside, vocab + k, marked[at])
        tile(tab, vocab + k, blocks, 0, 2)[...] = jnp.zeros((blocks, LANE), F32)
        tile(tab, vocab + k, blocks, 1, 2)[...] = tile(tab, spot, blocks, 1, 2)[...]
        start = start + doc_lengths[k]
    prod, total = segment_ends(marked, tab, toks, blocks, 2)
    p_all, s_all = prod[0], total[0]
    for s in range(CHAINS):
        seg[s, 0] = prod[s]
        seg[s, 1] = total[s]
        if s:
            s_all = prod[s] * s_all + total[s]
            p_all = prod[s] * p_all
    for d in range(ends.shape[0]):
        ends[d, 0] = p_all
        ends[d, 1] = s_all


def carry_kernel(block_of, ps_all, _, bias, carry, order):
    own = stream_order(order, block_of)

    def earlier(b, c):
        return ps_all[order[b], 0] * c + ps_all[order[b], 1]

    carry[...] = lax.fori_loop(0, own, earlier, jnp.zeros(carry.shape, F32))


def rest_table_kernel(spots, embed, w, o_tab, *, vocab, blocks):
    spread(o_tab, jax.nn.sigmoid(jnp.dot(embed[...], w[3], preferred_element_type=F32)), 0, blocks)
    for k in range(spots.shape[0]):
        tile(o_tab, vocab + k, blocks)[...] = tile(o_tab, spots[k], blocks)[...]


def other_table_kernel(spots, embed, direct, passed, tab, *, vocab, blocks):
    first = lax.axis_index("ctx") % 2 == 0

    def weights(g):
        mine, theirs = direct[g % 2], passed[g % 2]
        return jnp.where(first, mine, theirs) if g < 2 else jnp.where(first, theirs, mine)

    gate = [jnp.dot(embed[...], weights(g), preferred_element_type=F32) for g in range(4)]
    spread(tab, jax.nn.sigmoid(gate[1] + 3.0), 0, blocks, 0, 3)
    spread(tab, jax.nn.sigmoid(gate[0]) * jnp.tanh(gate[2]), 0, blocks, 1, 3)
    spread(tab, jax.nn.sigmoid(gate[3]), 0, blocks, 2, 3)
    for k in range(spots.shape[0]):
        tile(tab, vocab + k, blocks, 0, 3)[...] = jnp.zeros((blocks, LANE), F32)
        for kind in (1, 2):
            tile(tab, vocab + k, blocks, kind, 3)[...] = tile(tab, spots[k], blocks, kind, 3)[...]


def cell_kernel(*refs, others, total_tokens, blocks):
    ids, tab_o, o_tab, seg_o, wt_o, bias, tgt, ids_row = refs[:8]
    carries = refs[8:9 + others]
    refs = refs[9 + others:]
    tab_x, seg_x = refs[:others], refs[others:2 * others]
    halves = refs[2 * others:4 * others]
    refs = refs[4 * others:]
    hid, prev, src_out, keep_o, send_o, heads, head, o_sum, sums = refs[:9]
    src, hs, low, low_x, wt_x, logits, pcum, lgrad, sem, src_sems = refs[9:]
    toks = ids.shape[0]
    length = toks // CHAINS
    width = blocks * LANE
    vocab = wt_o.shape[0]
    nt = (((1,), (1,)), ((), ()))
    tn = (((0,), (0,)), ((), ()))

    def starts(piece, seg):
        c = carries[piece][...]
        out = []
        for s in range(CHAINS):
            out.append(c)
            c = seg[s, 0] * c + seg[s, 1]
        return tuple(out)

    def flatten(low):
        rows = 256

        def part(k, carry):
            at = pl.multiple_of(k * rows, rows)
            value = hs[pl.ds(at * blocks, rows * blocks), :]
            low[pl.ds(at, rows), :] = value.reshape(rows, width).astype(BF16)
            return carry

        lax.fori_loop(0, toks // rows, part, 0)

    def own_step(r, carry):
        cells, prods = list(carry[:CHAINS]), list(carry[CHAINS:])
        for s in range(CHAINS):
            t = s * length + r
            at = ids[t]
            d = tile(tab_o, at, blocks, 0, 2)[...]
            o = tile(o_tab, at, blocks)[...]
            tile(prev, t, blocks)[...] = cells[s]
            cells[s] = d * cells[s] + tile(tab_o, at, blocks, 1, 2)[...]
            prods[s] = prods[s] * d
            tile(pcum, t, blocks)[...] = prods[s]
            th = jnp.tanh(cells[s])
            h = o * th
            tile(hs, t, blocks)[...] = h
            tile(src, t, blocks)[...] = o - h * th
        return tuple(cells + prods)

    lax.fori_loop(0, length, own_step, starts(0, seg_o) + (jnp.ones((blocks, LANE), F32),) * CHAINS, unroll=4)
    flatten(low)
    save = pltpu.make_async_copy(low, hid, sem)
    save.start()
    logits[...] = lax.dot_general(wt_o[...], low[...], nt, preferred_element_type=F32) + bias[...]
    first = lax.axis_index("ctx") % 2 == 0
    half = vocab // 2
    for p in range(others):
        tab = tab_x[p]
        direct, passed = halves[2 * p:2 * p + 2]
        wt_x[0:half, :] = jnp.where(first, direct[...], passed[...])
        wt_x[half:vocab, :] = jnp.where(first, passed[...], direct[...])

        def other_step(r, carry):
            cells = list(carry)
            for s in range(CHAINS):
                t = s * length + r
                at = ids[t]
                cells[s] = tile(tab, at, blocks, 0, 3)[...] * cells[s] + tile(tab, at, blocks, 1, 3)[...]
                tile(hs, t, blocks)[...] = tile(tab, at, blocks, 2, 3)[...] * jnp.tanh(cells[s])
            return tuple(cells)

        lax.fori_loop(0, length, other_step, starts(p + 1, seg_x[p]), unroll=4)
        flatten(low_x)
        logits[...] += lax.dot_general(wt_x[...], low_x[...], nt, preferred_element_type=F32)

    rows = 1024

    def save_src(k):
        place = pl.ds(pl.multiple_of(k * rows * blocks, rows * blocks), rows * blocks)
        return pltpu.make_async_copy(src.at[place, :], src_out.at[place, :], src_sems.at[k])


    def back(k, carry):
        loss, b_grad = carry
        at = pl.multiple_of(k * rows, rows)
        part = logits[:, pl.ds(at, rows)]
        target = lax.broadcasted_iota(jnp.int32, (vocab, rows), 0) == tgt[:, pl.ds(at, rows)]
        top = jnp.max(part, axis=0, keepdims=True)
        power = jnp.exp(part - top)
        norm = jnp.sum(power, axis=0, keepdims=True)
        picked = jnp.sum(jnp.where(target, part, 0.0), axis=0, keepdims=True)
        loss = loss + (top + jnp.log(norm) - picked)
        share = power * ((1.0 / norm) * (1.0 / total_tokens))
        grad = (share - jnp.where(target, 1.0 / total_tokens, 0.0)).astype(BF16)
        lgrad[:, pl.ds(at, rows)] = grad
        b_grad = b_grad + jnp.sum(grad.astype(F32).reshape(vocab, rows // LANE, LANE), axis=1)
        hg = lax.dot_general(grad, wt_o[...], tn, preferred_element_type=F32)
        low_x[pl.ds(at, rows), :] = (hg * low[pl.ds(at, rows), :].astype(F32)).astype(BF16)
        for b in range(blocks):
            hs[pl.ds(at * blocks + b, rows, stride=blocks), :] = hg[:, b * LANE:(b + 1) * LANE]
        for q in range(rows // length):
            place = pl.ds((at + q * length) * blocks, length * blocks)
            grad_src = src[place, :] * hs[place, :]
            src[place, :] = grad_src
            ends = (pcum[place, :] * grad_src).reshape(length, blocks, LANE)
            tile(heads, k * (rows // length) + q, blocks)[...] = jnp.sum(ends, axis=0)
        save_src(k).start()
        return loss, b_grad

    loss, b_grad = lax.fori_loop(
        0, toks // rows, back, (jnp.zeros((1, rows), F32), jnp.zeros((vocab, LANE), F32))
    )
    lane = lax.broadcasted_iota(jnp.int32, (vocab, LANE), 1)
    row = lax.broadcasted_iota(jnp.int32, (vocab, LANE), 0)
    sums[...] = jnp.where(lane == LANE - 1, jnp.sum(b_grad, axis=1, keepdims=True), 0.0) + jnp.where(
        (lane == LANE - 2) & (row == 0), jnp.sum(loss, axis=1, keepdims=True), 0.0
    )
    grad_out = jnp.dot(lgrad[...], low[...], preferred_element_type=F32)
    part = keep_o.shape[1]
    count = head.shape[0]
    splits = count // blocks

    def piece(q):
        c, e = q // splits, q % splits
        size = max(0, min(part, vocab - e * part))
        return padded(grad_out, slice(e * part, e * part + size), slice(c * LANE, (c + 1) * LANE), part)

    store_pairs(keep_o, send_o, lax.axis_index("ctx"), piece, count, slice(0, part))
    chars = lax.broadcasted_iota(jnp.int32, (vocab, toks), 0) == ids_row[...]
    o_sum[...] = jnp.dot(chars.astype(F32).astype(BF16), low_x[...], preferred_element_type=F32)
    save.wait()
    for k in range(toks // rows):
        save_src(k).wait()
    total = tile(heads, CHAINS - 1, blocks)[...]
    for s in range(CHAINS - 2, -1, -1):
        total = tile(heads, s, blocks)[...] + seg_o[s, 0] * total
    for d in range(head.shape[0]):
        head[d] = total


def char_sum_kernel(
    ids, block_of, tab, seg, heads, h_all, ps_all, prev, src, sums, order, carry, *refs, copies, blocks
):
    number = pl.program_id(0)
    length = ids.shape[0] // CHAINS
    span = src.shape[1] // blocks
    sets = [refs[2 * k:2 * k + 2] for k in range(copies)]

    @pl.when(number == 0)
    def _():
        for ref in refs:
            ref[...] = jnp.zeros_like(ref)
        own = stream_order(order, block_of)
        count = block_of.shape[0]

        def from_later(i, g):
            slot = order[count - 1 - i]
            return h_all[slot] + ps_all[slot, 0] * g

        later = lax.fori_loop(0, count - 1 - own, from_later, jnp.zeros((blocks, LANE), F32))
        for s in range(CHAINS - 1, -1, -1):
            carry[s] = later
            later = tile(heads, s, blocks)[...] + seg[s, 0] * later

    def step(i, later):
        h = list(later)
        r = span - 1 - i
        for s in range(CHAINS):
            token = s * length + (pl.num_programs(0) - 1 - number) * span + r
            at = ids[token]
            here = pl.ds(pl.multiple_of(r * blocks, blocks), blocks)
            g = src[s, here, :] + h[s]
            h[s] = tile(tab, at, blocks, 0, 2)[...] * g
            cell, forget = sets[s % copies]
            tile(cell, at, blocks)[...] += g
            tile(forget, at, blocks)[...] += g * tile(prev, token, blocks)[...]
        return tuple(h)

    ends = lax.fori_loop(0, span, step, tuple(carry[s] for s in range(CHAINS)))
    for s in range(CHAINS):
        carry[s] = ends[s]

    @pl.when(number == pl.num_programs(0) - 1)
    def _():
        for k in range(2):
            value = refs[k][...]
            for more in sets[1:]:
                value = value + more[k][...]
            sums[k] = value


def gate_sum_kernel(spots, sums, o_sum, embed, w, extra, high, low, keep_e, send_e, merged, *, count, vocab, blocks):
    rows = high.shape[1]
    merged[...] = sums[...]
    for k in range(spots.shape[0]):
        tile(merged.at[0], spots[k], blocks)[...] += tile(merged.at[0], vocab + k, blocks)[...]
    pad = (rows - vocab) * blocks
    for q in range(2):
        merged[q, vocab * blocks:, :] = jnp.zeros((pad, LANE), F32)

    def units(value_of):
        return jnp.concatenate([value_of(b) for b in range(blocks)], axis=1)

    def column(q, b):
        return merged[q, pl.ds(b, rows, stride=blocks), :]

    def gate_of(g):
        return jnp.dot(embed[...], w[g], preferred_element_type=F32)

    both = (((1,), (1,)), ((), ()))
    in_gate, cand = jax.nn.sigmoid(gate_of(0)), jnp.tanh(gate_of(2))
    forget = jax.nn.sigmoid(gate_of(1) + 3.0)
    cell = units(lambda b: column(0, b))
    source = in_gate * cand
    parts = [
        lambda: cell * (source - source * in_gate),
        lambda: units(lambda b: column(1, b)) * (forget - forget * forget),
        lambda: cell * (in_gate - source * cand),
        lambda: o_sum[...] * (1.0 - jax.nn.sigmoid(gate_of(3))),
    ]
    part_e = jnp.zeros((rows, w.shape[1]), F32)
    for gate in range(4):
        total = parts[gate]()
        high[gate] = total.astype(BF16)
        low[gate] = (total - high[gate].astype(F32)).astype(BF16)
        part_e = part_e + lax.dot_general(high[gate], w[gate], both, preferred_element_type=F32)
        part_e = part_e + lax.dot_general(low[gate], w[gate], both, preferred_element_type=F32)
    per = keep_e.shape[1]
    wide_e = jnp.concatenate([part_e, jnp.zeros((rows, LANE - part_e.shape[1]), F32)], axis=1) + extra[...]
    wide_e = jnp.concatenate([wide_e, jnp.zeros((count * per - rows, LANE), F32)], axis=0)
    me = lax.axis_index("ctx")
    store_pairs(keep_e, send_e, me, lambda q: wide_e[q * per:(q + 1) * per, :], count, slice(0, per))


def input_grad_kernel(high, low, table, keep, send, *, count, part, blocks):
    tn = (((0,), (0,)), ((), ()))
    splits = count // blocks
    for gate in range(4):
        wide = lax.dot_general(table[...], high[gate], tn, preferred_element_type=F32)
        wide = wide + lax.dot_general(table[...], low[gate], tn, preferred_element_type=F32)

        def piece(q):
            c, e = q // splits, q % splits
            size = max(0, min(part, wide.shape[0] - e * part))
            return padded(wide, slice(e * part, e * part + size), slice(c * LANE, (c + 1) * LANE), part)

        store_pairs(keep, send, lax.axis_index("ctx"), piece, count, slice(gate * part, (gate + 1) * part))


def finish_kernel(mine_a, mine_b, theirs_a, theirs_b, w_grad, b_grad, out_grad, *, groups, part, emb):
    count = 2 * mine_a.shape[0]
    me = lax.axis_index("ctx")
    first = me % 2 == 0
    stages = gather_stages_of(count)
    pairs = {}
    top = mine_a.shape[1]
    rest = section_rows(groups) - top

    def chunk(q, rows):
        pair = q - q % 2
        if pair not in pairs:
            slot = slot_of(pair ^ (me - me % 2), count, stages)
            own, other = (
                jnp.concatenate([a[slot].astype(jnp.int32), b[slot, 0:rest].astype(jnp.int32)], axis=0)
                for a, b in ((mine_a, mine_b), (theirs_a, theirs_b))
            )
            pairs[pair] = [
                decode(jnp.where(first, own, other), groups), decode(jnp.where(first, other, own), groups)
            ]
        return pairs[pair][q % 2][rows]

    cols = w_grad.shape[2] // LANE
    splits = count // cols
    vpart = groups[-1]
    vocab = out_grad.shape[0]
    for c in range(cols):
        lanes = slice(c * LANE, (c + 1) * LANE)
        for e in range(splits):
            q = c * splits + e
            size = max(0, min(part, emb - e * part))
            for gate in range(4):
                if size:
                    w_grad[e * part:e * part + size, gate, lanes] = chunk(q, slice(gate * part, gate * part + size))
                if e * part <= emb < (e + 1) * part:
                    at = gate * part + emb - e * part
                    b_grad[gate:gate + 1, lanes] = chunk(q, slice(at, at + 1))
            size = max(0, min(vpart, vocab - e * vpart))
            if size:
                out_grad[e * vpart:e * vpart + size, lanes] = chunk(q, slice(4 * part, 4 * part + size))


def tree_sum(values):
    while len(values) > 1:
        values = [values[k] + values[k + 1] for k in range(0, len(values), 2)]
    return values[0]


def embed_finish_kernel(*refs, groups, shards, total_tokens):
    codes, theirs_b = refs[:2 * shards - 1], refs[2 * shards - 1]
    e_grad, o_grad, loss, eacc = refs[2 * shards:]
    count = 2 * codes[0].shape[0]
    me = lax.axis_index("ctx")
    first = me % 2 == 0
    stages = gather_stages_of(count)
    per, rows = sum(groups), codes[0].shape[1]
    for p in range(0, count, 2):
        slot = slot_of(p ^ (me - me % 2), count, stages)
        own = [codes[k if k == 0 else 2 * k - 1][slot] for k in range(shards)]
        other = [theirs_b[slot, theirs_b.shape[1] - rows:]] + [codes[2 * k][slot] for k in range(1, shards)]
        own, other = (tree_sum([decode(code, groups) for code in kind]) for kind in (own, other))
        eacc[p * per:(p + 1) * per, :] = jnp.where(first, own, other)
        eacc[(p + 1) * per:(p + 2) * per, :] = jnp.where(first, other, own)
    vocab, emb = e_grad.shape
    e_grad[...] = eacc[0:vocab, 0:emb]
    for k in range(eacc.shape[0] // LANE):
        size = max(0, min(LANE, vocab - k * LANE))
        if size:
            flipped = jnp.transpose(eacc[k * LANE:(k + 1) * LANE, :], (1, 0))
            o_grad[:, k * LANE:k * LANE + size] = flipped[LANE - 1:LANE, 0:size] * (1.0 / shards)
    loss[...] = eacc[0:1, LANE - 2:LANE - 1] * (1.0 / (shards * total_tokens))


def half_of(value, core):
    half = value.shape[0] // 2
    return lax.dynamic_slice_in_dim(value, core * half, half, 0)


def from_others(value, wa):
    return [lax.ppermute(value, "wa", [(k, (k - s) % wa) for k in range(wa)]) for s in range(1, wa)]


def after(value, earlier):
    return lax.optimization_barrier((value, earlier))[0]


def body(ids, targets, doc_lengths, block_of, embed, w_in, b_in, w_out, b_out):
    count = lax.axis_size("ctx")
    wa = lax.axis_size("wa")
    toks = ids.shape[0]
    emb, gates, width = w_in.shape
    blocks = width // LANE
    vocab = embed.shape[0]
    docs = doc_lengths.shape[0]
    vpad = ceil_to(vocab + docs, 32)
    kdim = ceil_to(emb + 3, 16)
    total_tokens = toks * count
    core = lax.axis_index("ctx") % 2

    b_hi = lax.reduce_precision(b_in, 8, 7)
    b_mid = lax.reduce_precision(b_in - b_hi, 8, 7)
    extra_rows = jnp.stack([b_hi, b_mid, b_in - b_hi - b_mid], axis=1).astype(BF16)
    fill = jnp.zeros((gates, kdim - emb - 3, width), BF16)
    w_own = jnp.concatenate([jnp.transpose(w_in, (1, 0, 2)), extra_rows, fill], axis=1)
    ones_col = (jnp.arange(kdim) >= emb) & (jnp.arange(kdim) < emb + 3)
    ones_row = jnp.arange(vpad) < vocab
    table = jnp.pad(embed, ((0, vpad - vocab), (0, kdim - emb)))
    table = jnp.where(ones_col[None, :] & ones_row[:, None], jnp.ones((), BF16), table)

    chip = lambda *shape: pltpu.VMEM(shape, F32)
    hbm = lambda shape, kind: jax.ShapeDtypeStruct(shape, kind)
    smem = lambda shape: jax.ShapeDtypeStruct(shape, jnp.int32)
    tokens = (toks * blocks, LANE)

    bf = lambda *shape: pltpu.HBM(shape, BF16)
    marked, spots, tab, seg, ends, w_far, wt_own, wt_far = call(
        functools.partial(own_table_kernel, vocab=vocab, blocks=blocks),
        "tables_own",
        [doc_lengths, block_of],
        [ids, table, w_own, w_out.T],
        [smem((toks,)), smem((docs,)), chip(vpad * 2 * blocks, LANE), pltpu.HBM((CHAINS, 2, blocks, LANE), F32),
         pltpu.HBM((count, 2, blocks, LANE), F32), bf(gates // 2, kdim, width), bf(vpad, width), bf(vpad // 2, width)],
        [pltpu.SemaphoreType.DMA],
        in_spaces=[pl.ANY, pltpu.VMEM, pltpu.VMEM, pltpu.VMEM],
        out_spaces=[pltpu.SMEM, pltpu.SMEM] + [pltpu.VMEM] * 6,
        micros=6,
    )
    tab = near(tab)
    w_far, seg_x, wt_far = from_others(w_far, wa), from_others(seg, wa), from_others(wt_far, wa)
    ps_all = exchange(ends, "ctx")
    bias_out = jnp.pad(b_out, (0, vpad - vocab), constant_values=-1e30)[:, None]
    (o_tab,) = call(
        functools.partial(rest_table_kernel, vocab=vocab, blocks=blocks),
        "tables_rest",
        [spots],
        [table, w_own],
        [chip(vpad * blocks, LANE)],
        micros=3,
    )
    o_tab = near(o_tab)
    (carry,) = call(
        carry_kernel, "carry", [block_of], [ps_all, o_tab, bias_out], [hbm((blocks, LANE), F32)],
        [pltpu.SMEM((count,), jnp.int32)], in_spaces=[pltpu.VMEM, pltpu.VMEM, pl.ANY],
    )
    carries = [carry] + from_others(carry, wa)
    w_far = [after(w, ps_all) for w in w_far]
    w_oth = [v for w in w_far for v in (w, swap(w, "ctx", 1))]
    wt_far = [after(w, carry) for w in wt_far]
    wt_oth = [v for w in wt_far for v in (w, swap(w, "ctx", 1))]
    others = wa - 1
    tab_x = [
        near(call(
            functools.partial(other_table_kernel, vocab=vocab, blocks=blocks),
            "tables_other",
            [spots],
            [table] + w_oth[2 * p:2 * p + 2],
            [chip(vpad * 3 * blocks, LANE)],
            micros=3,
        )[0])
        for p in range(others)
    ]

    splits = count // blocks
    vpart = ceil_to(-(-vpad // splits), 8)
    half_chunks = lambda rows: [hbm((count // 2, rows, LANE), F32)] * 2
    copies = 2
    hid, prev, src, keep_o, send_o, heads, head, o_sum, extra = call(
        functools.partial(cell_kernel, others=others, total_tokens=total_tokens, blocks=blocks),
        "cells",
        [marked],
        [tab, o_tab, seg, wt_own, bias_out, targets[None], ids[None]] + carries + tab_x + seg_x + wt_oth,
        [
            hbm((toks, width), BF16), chip(*tokens), hbm(tokens, F32),
            *half_chunks(vpart), chip(CHAINS * blocks, LANE), hbm((count, blocks, LANE), F32),
            chip(vpad, width), hbm((vpad, LANE), F32),
        ],
        [
            pltpu.VMEM(tokens, F32), pltpu.VMEM(tokens, F32), pltpu.VMEM((toks, width), BF16),
            pltpu.VMEM((toks, width), BF16), pltpu.VMEM((vpad, width), BF16), pltpu.VMEM((vpad, toks), F32), pltpu.VMEM(tokens, F32),
            pltpu.VMEM((vpad, toks), BF16), pltpu.SemaphoreType.DMA, pltpu.SemaphoreType.DMA((toks // 1024,)),
        ],
        limit=44,
        out_spaces=[pl.ANY, pltpu.VMEM, pl.ANY] + [pltpu.VMEM] * 6,
        micros=26,
    )
    prev, heads, o_sum = near(prev), near(heads), near(o_sum)
    part = ceil_to(-(-kdim // splits), 8)
    per = ceil_to(-(-vpad // count), 8)
    h_all = exchange(head, "ctx")
    got_o = swap(send_o, "ctx", 1)
    length = toks // CHAINS
    span = 32
    block = pl.BlockSpec((CHAINS, span * blocks, LANE), lambda i: (0, length // span - 1 - i, 0))
    (sums,) = call(
        functools.partial(char_sum_kernel, copies=copies, blocks=blocks),
        "char_sums",
        [marked, block_of],
        [tab, seg, heads, h_all, ps_all, prev, far(src.reshape(CHAINS, length * blocks, LANE))],
        [chip(2, vpad * blocks, LANE)],
        [pltpu.SMEM((count,), jnp.int32), pltpu.VMEM((CHAINS, blocks, LANE), F32)]
        + [pltpu.VMEM((vpad * blocks, LANE), F32)] * (2 * copies),
        limit=24,
        in_spaces=[pltpu.VMEM] * 6 + [block],
        micros=(9, length // span),
    )
    high, low, keep_e, send_e = call(
        functools.partial(gate_sum_kernel, count=count, vocab=vocab, blocks=blocks),
        "gate_sums",
        [spots],
        [near(sums), o_sum, table, w_own, extra],
        [pltpu.VMEM((gates, vpad, width), BF16)] * 2 + half_chunks(per),
        [pltpu.VMEM((2, vpad * blocks, LANE), F32)],
        limit=24,
        micros=3,
    )
    keep, send = call(
        functools.partial(input_grad_kernel, count=count, part=part, blocks=blocks),
        "input_grad",
        [],
        [near(high), near(low), table],
        half_chunks(4 * part),
        limit=24,
        micros=3,
    )
    sections = [[part] * gates + [vpart], [per]]
    apart = section_rows(sections[1])
    chunk = reduce_chunks(
        [keep, keep_o, keep_e], [swap(send, "ctx", 1), got_o, swap(send_e, "ctx", 1)], sections, "ctx"
    )
    halves, tail = gather_chunks(chunk, "ctx", apart)
    far_tails = [swap(tail, "wa", mask) for mask in range(1, wa)]
    w_grad, bi_grad, w_out_grad = call(
        functools.partial(finish_kernel, groups=sections[0], part=part, emb=emb),
        "finish",
        [],
        halves,
        [hbm((emb, gates, width), F32), hbm((gates, width), F32), hbm((vocab, width), F32)],
        micros=4,
    )
    far_tails = [after(v, bi_grad) for v in far_tails]
    tails = [tail] + [v for far_tail in far_tails for v in (far_tail, swap(far_tail, "ctx", 1))]
    e_grad, bo_grad, loss = call(
        functools.partial(embed_finish_kernel, groups=sections[1], shards=wa, total_tokens=total_tokens),
        "embed_finish",
        [],
        tails + [halves[3]],
        [hbm((vocab, emb), F32), hbm((1, vocab), F32), hbm((1, 1), F32)],
        [pltpu.VMEM((ceil_to(count * per, LANE), LANE), F32)],
    )
    return (
        hid,
        loss[0, 0],
        e_grad,
        w_grad,
        bi_grad,
        w_out_grad.T,
        bo_grad[0],
    )


def solution(mesh):
    placed = (
        P("ctx"),
        P("ctx"),
        P(),
        P(),
        P(),
        P(None, None, "wa"),
        P(None, "wa"),
        P("wa", None),
        P(),
    )
    return jax.shard_map(
        body,
        mesh=mesh,
        in_specs=placed,
        out_specs=(
            P("ctx", "wa"),
            P(),
            P(),
            P(None, None, "wa"),
            P(None, "wa"),
            P("wa", None),
            P(),
        ),
        check_vma=False,
    )
```

```python
import functools

import jax
import jax.numpy as jnp
from jax import lax
from jax.experimental import pallas as pl
from jax.experimental.pallas import tpu as pltpu
from jax.sharding import PartitionSpec as P

CHAINS = 16
LANE = 128
F32 = jnp.float32
BF16 = jnp.bfloat16


def ceil_to(value, step):
    return -(-value // step) * step


def call(kernel, name, scalars, arrays, outs, scratch=(), limit=16, in_spaces=None, out_spaces=None, micros=1):
    spec = lambda m: m if isinstance(m, pl.BlockSpec) else pl.BlockSpec(memory_space=m)
    blocked = [m for m in in_spaces or [] if isinstance(m, pl.BlockSpec)]
    steps = micros[1] if blocked else None
    return pl.pallas_call(
        kernel,
        grid=(steps,) if blocked else (),
        in_specs=[spec(pltpu.SMEM)] * len(scalars) + [spec(m) for m in in_spaces or [pltpu.VMEM] * len(arrays)],
        out_specs=[spec(m) for m in out_spaces or [pltpu.VMEM] * len(outs)],
        out_shape=list(outs),
        scratch_shapes=list(scratch),
        compiler_params=pltpu.CompilerParams(vmem_limit_bytes=limit * 1024 * 1024),
        cost_estimate=pl.CostEstimate(
            flops=0, transcendentals=0, bytes_accessed=3000000 * (micros[0] if blocked else micros)
        ),
        name=name,
    )(*scalars, *arrays)


def near(value):
    return pltpu.with_memory_space_constraint(value, pltpu.VMEM)


def far(value):
    return pltpu.with_memory_space_constraint(value, pltpu.HBM)


def stages_of(count):
    stages, bit = [[1]], 2
    while bit < count:
        ways = min(8 if bit == 2 else 4, count // bit)
        stages.append([k * bit for k in range(1, ways)])
        bit *= ways
    return stages


def gather_stages_of(count):
    stages, bit = [[1]], 2
    while bit < count:
        ways = min(2 if bit == 2 else 4, count // bit)
        stages.append([k * bit for k in range(1, ways)])
        bit *= ways
    return stages


def swap(value, axis, mask):
    count = lax.axis_size(axis)
    return lax.ppermute(value, axis, [(k, k ^ mask) for k in range(count)])


def exchange(copies, axis):
    return lax.all_to_all(copies, axis, 0, 0, tiled=True)


def slot_of(xor_index, count, stages=None):
    place, size, bit = 0, count, 1
    for masks in stages or stages_of(count):
        ways = len(masks) + 1
        size = size // ways
        place = place + ((xor_index // bit) % ways) * size
        bit = bit * ways
    return place


STEPS = 32766.0
BIAS = 90


def power_of_two(exponent):
    value = jnp.full(exponent.shape, 2.0 ** -BIAS, F32)
    for bit in range(7):
        on = ((exponent + BIAS) // (1 << bit)) % 2 == 1
        value = value * jnp.where(on, 2.0 ** (1 << bit), 1.0)
    return value


def section_rows(groups):
    return ceil_to(sum(groups) + len(groups), 16)


def coded_rows(sections):
    return sum(section_rows(groups) for groups in sections)


def encode_all(value, sections):
    parts, at = [], 0
    for groups in sections:
        parts.append(encode(value[at:at + sum(groups)], groups))
        at += sum(groups)
    return jnp.concatenate(parts, axis=0)


def decode_all(code, sections):
    parts, at = [], 0
    for groups in sections:
        parts.append(decode(code[at:at + section_rows(groups)], groups))
        at += section_rows(groups)
    return jnp.concatenate(parts, axis=0)


def encode(value, groups):
    parts, exponents, at = [], [], 0
    for size in groups:
        part = value[at:at + size]
        most = jnp.max(jnp.abs(part), axis=0, keepdims=True)
        exponent = jnp.ceil(jnp.log2(jnp.maximum(most, 2.0 ** (1 - BIAS)))).astype(jnp.int32)
        exponent = jnp.clip(exponent, -BIAS, 127 - BIAS)
        parts.append(jnp.round(part * (STEPS / power_of_two(exponent))).astype(jnp.int32))
        exponents.append(exponent)
        at += size
    fill = section_rows(groups) - at - len(groups)
    if fill:
        exponents.append(jnp.zeros((fill, value.shape[1]), jnp.int32))
    return jnp.concatenate(parts + exponents, axis=0).astype(jnp.int16)


def decode(code, groups):
    code = code.astype(jnp.int32)
    parts, at, total = [], 0, sum(groups)
    for k, size in enumerate(groups):
        unit = power_of_two(code[total + k:total + k + 1]) * (1.0 / STEPS)
        parts.append(code[at:at + size].astype(F32) * unit)
        at += size
    return jnp.concatenate(parts, axis=0)


def reduce_chunks(keeps, moved, sections, axis):
    stages = stages_of(lax.axis_size(axis))[1:]
    number = len(keeps)
    sizes = [k.shape[1] for k in keeps]
    rows, coded = sum(sizes), coded_rows(sections)
    half = keeps[0].shape[0]
    ways = len(stages[0]) + 1 if stages else 1
    code_shape = lambda size: jax.ShapeDtypeStruct((size, coded, LANE), jnp.int16)

    def first(*refs):
        ins, outs = refs[:2 * number], refs[2 * number:]
        for place in range(half):
            way, slot = place // (half // ways), place % (half // ways)
            parts = [ins[k][place] + ins[number + k][place] for k in range(number)]
            value = jnp.concatenate(parts, axis=0)
            outs[way][slot] = value if way == 0 else encode_all(value, sections)

    keep, *sends = call(
        first,
        "core_sum",
        [],
        list(keeps) + list(moved),
        [jax.ShapeDtypeStruct((half // ways, rows, LANE), F32)] + [code_shape(half // ways)] * (ways - 1),
        limit=24,
    )
    for k, masks in enumerate(stages):
        got = [swap(part, axis, mask) for part, mask in zip(sends, masks)]
        ways = len(stages[k + 1]) + 1 if k + 1 < len(stages) else 1
        size = keep.shape[0] // ways
        last = k + 1 == len(stages)

        def later(*refs):
            ins, outs = refs[:len(got) + 1], refs[len(got) + 1:]
            for way in range(ways):
                for slot in range(size):
                    value = ins[0][way * size + slot]
                    for ref in ins[1:]:
                        value = value + decode_all(ref[way * size + slot], sections)
                    outs[way][slot] = value if way == 0 and not last else encode_all(value, sections)

        kept = code_shape(size) if last else jax.ShapeDtypeStruct((size, rows, LANE), F32)
        keep, *sends = call(
            later, "chip_sum" + str(k), [], [keep] + got, [kept] + [code_shape(size)] * (ways - 1), limit=24
        )
    return keep


def gather_chunks(chunk, axis, apart):
    stages = gather_stages_of(lax.axis_size(axis))
    middle = ceil_to(chunk.shape[1] // 2, 16)
    halves, tail = [chunk[:, :middle], chunk[:, middle:]], None
    for number, masks in enumerate(reversed(stages[1:])):
        for h in range(2):
            value = halves[h]
            parts = [value] + [swap(value, axis, mask) for mask in masks]
            size, rows = value.shape[0], value.shape[1]
            outs = [jax.ShapeDtypeStruct((size * len(parts), rows, LANE), value.dtype)]
            if h == 1 and number == len(stages) - 2:
                outs.append(jax.ShapeDtypeStruct((size * len(parts), apart, LANE), value.dtype))

            def kernel(*refs):
                for k in range(len(parts)):
                    for out in refs[len(parts):]:
                        out[k * size:(k + 1) * size] = refs[k][:, rows - out.shape[1]:, :]

            got = call(kernel, "chunk_join" + str(number), [], parts, outs)
            halves[h], tail = got[0], got[-1]
    return halves + [swap(h, axis, 1) for h in halves], tail


def padded(value, rows, lanes, size):
    count = rows.stop - rows.start
    if count == 0:
        return jnp.zeros((size, LANE), F32)
    piece = value[rows, lanes]
    return piece if count == size else jnp.concatenate([piece, jnp.zeros((size - count, LANE), F32)], axis=0)


def store_pairs(keep, send, me, value_of, count, rows):
    first = me % 2 == 0
    for pair in range(count // 2):
        a, b = value_of(2 * pair), value_of(2 * pair + 1)
        slot = slot_of((2 * pair) ^ (me - me % 2), count)
        keep[slot, rows, :] = jnp.where(first, a, b)
        send[slot, rows, :] = jnp.where(first, b, a)


def tile(ref, index, blocks, kind=0, kinds=1):
    return ref.at[pl.ds(pl.multiple_of((index * kinds + kind) * blocks, blocks), blocks), :]


def spread(ref, value, first, blocks, kind=0, kinds=1):
    rows = value.shape[0]
    for b in range(blocks):
        place = pl.ds((first * kinds + kind) * blocks + b, rows, stride=kinds * blocks)
        ref[place, :] = value[:, b * LANE:(b + 1) * LANE]


def gathered(ref, first, rows, blocks, b, kind=0, kinds=1):
    return ref[pl.ds((first * kinds + kind) * blocks + b, rows, stride=kinds * blocks), :]


def stream_order(order, block_of):
    def place(d, carry):
        order[block_of[d]] = d
        return carry

    lax.fori_loop(0, block_of.shape[0], place, 0)
    return block_of[lax.axis_index("ctx")]


def segment_ends(ids, tab, toks, blocks, kinds):
    length = toks // CHAINS

    def step(r, carry):
        prod, total = list(carry[:CHAINS]), list(carry[CHAINS:])
        for s in range(CHAINS):
            at = ids[s * length + r]
            d = tile(tab, at, blocks, 0, kinds)[...]
            total[s] = d * total[s] + tile(tab, at, blocks, 1, kinds)[...]
            prod[s] = prod[s] * d
        return tuple(prod + total)

    first = [jnp.ones((blocks, LANE), F32)] * CHAINS + [jnp.zeros((blocks, LANE), F32)] * CHAINS
    carry = lax.fori_loop(0, length, step, tuple(first), unroll=2)
    return carry[:CHAINS], carry[CHAINS:]


def own_table_kernel(
    doc_lengths, block_of, ids, embed, w, w_out, marked, spots, tab_out, seg, ends, w_far, wt, wt_far, tab, sem, tab_sem,
    *, vocab, blocks,
):
    toks = ids.shape[0]
    copy = pltpu.make_async_copy(ids, marked, sem)
    copy.start()
    core = lax.axis_index("ctx") % 2
    shape = (wt.shape[0], w_out.shape[0])
    same = lax.broadcasted_iota(jnp.int32, shape, 0) == lax.broadcasted_iota(jnp.int32, shape, 1)
    turned = jnp.dot(same.astype(F32).astype(BF16), w_out[...], preferred_element_type=F32).astype(BF16)
    wt[...] = turned
    half = wt_far.shape[0]
    wt_far[...] = jnp.where(core == 0, turned[0:half], turned[half:2 * half])
    for g in range(w_far.shape[0]):
        w_far[g] = w[core * w_far.shape[0] + g]
    gate = [jnp.dot(embed[...], w[g], preferred_element_type=F32) for g in range(3)]
    spread(tab, jax.nn.sigmoid(gate[1] + 3.0), 0, blocks, 0, 2)
    spread(tab, jax.nn.sigmoid(gate[0]) * jnp.tanh(gate[2]), 0, blocks, 1, 2)
    copy.wait()
    start = -block_of[lax.axis_index("ctx")] * toks
    for k in range(doc_lengths.shape[0]):
        inside = (start >= 0) & (start < toks)
        at = jnp.clip(start, 0, toks - 1)
        spot = jnp.where(inside, marked[at], 0)
        spots[k] = spot
        marked[at] = jnp.where(inside, vocab + k, marked[at])
        tile(tab, vocab + k, blocks, 0, 2)[...] = jnp.zeros((blocks, LANE), F32)
        tile(tab, vocab + k, blocks, 1, 2)[...] = tile(tab, spot, blocks, 1, 2)[...]
        start = start + doc_lengths[k]
    save = pltpu.make_async_copy(tab, tab_out, tab_sem)
    save.start()
    prod, total = segment_ends(marked, tab, toks, blocks, 2)
    p_all, s_all = prod[0], total[0]
    for s in range(CHAINS):
        seg[s, 0] = prod[s]
        seg[s, 1] = total[s]
        if s:
            s_all = prod[s] * s_all + total[s]
            p_all = prod[s] * p_all
    for d in range(ends.shape[0]):
        ends[d, 0] = p_all
        ends[d, 1] = s_all
    save.wait()


def carry_kernel(block_of, ps_all, _, bias, carry, order):
    own = stream_order(order, block_of)

    def earlier(b, c):
        return ps_all[order[b], 0] * c + ps_all[order[b], 1]

    carry[...] = lax.fori_loop(0, own, earlier, jnp.zeros(carry.shape, F32))


def rest_table_kernel(spots, embed, w, o_tab, *, vocab, blocks):
    spread(o_tab, jax.nn.sigmoid(jnp.dot(embed[...], w[3], preferred_element_type=F32)), 0, blocks)
    for k in range(spots.shape[0]):
        tile(o_tab, vocab + k, blocks)[...] = tile(o_tab, spots[k], blocks)[...]


def other_table_kernel(spots, embed, direct, passed, tab, *, vocab, blocks):
    first = lax.axis_index("ctx") % 2 == 0

    def weights(g):
        mine, theirs = direct[g % 2], passed[g % 2]
        return jnp.where(first, mine, theirs) if g < 2 else jnp.where(first, theirs, mine)

    gate = [jnp.dot(embed[...], weights(g), preferred_element_type=F32) for g in range(4)]
    spread(tab, jax.nn.sigmoid(gate[1] + 3.0), 0, blocks, 0, 3)
    spread(tab, jax.nn.sigmoid(gate[0]) * jnp.tanh(gate[2]), 0, blocks, 1, 3)
    spread(tab, jax.nn.sigmoid(gate[3]), 0, blocks, 2, 3)
    for k in range(spots.shape[0]):
        tile(tab, vocab + k, blocks, 0, 3)[...] = jnp.zeros((blocks, LANE), F32)
        for kind in (1, 2):
            tile(tab, vocab + k, blocks, kind, 3)[...] = tile(tab, spots[k], blocks, kind, 3)[...]


def cell_kernel(*refs, others, total_tokens, blocks):
    ids, tab_o, o_tab, seg_o, wt_o, bias, tgt, ids_row = refs[:8]
    carries = refs[8:9 + others]
    refs = refs[9 + others:]
    tab_x, seg_x = refs[:others], refs[others:2 * others]
    halves = refs[2 * others:4 * others]
    refs = refs[4 * others:]
    hid, prev, src_out, keep_o, send_o, heads, head, o_sum, sums = refs[:9]
    src, hs, low, low_x, wt_x, logits, pcum, lgrad, sem, src_sems = refs[9:]
    toks = ids.shape[0]
    length = toks // CHAINS
    width = blocks * LANE
    vocab = wt_o.shape[0]
    nt = (((1,), (1,)), ((), ()))
    tn = (((0,), (0,)), ((), ()))

    def starts(piece, seg):
        c = carries[piece][...]
        out = []
        for s in range(CHAINS):
            out.append(c)
            c = seg[s, 0] * c + seg[s, 1]
        return tuple(out)

    def flatten(low):
        rows = 256

        def part(k, carry):
            at = pl.multiple_of(k * rows, rows)
            value = hs[pl.ds(at * blocks, rows * blocks), :]
            low[pl.ds(at, rows), :] = value.reshape(rows, width).astype(BF16)
            return carry

        lax.fori_loop(0, toks // rows, part, 0)

    def own_step(r, carry):
        cells, prods = list(carry[:CHAINS]), list(carry[CHAINS:])
        for s in range(CHAINS):
            t = s * length + r
            at = ids[t]
            d = tile(tab_o, at, blocks, 0, 2)[...]
            o = tile(o_tab, at, blocks)[...]
            tile(prev, t, blocks)[...] = cells[s]
            cells[s] = d * cells[s] + tile(tab_o, at, blocks, 1, 2)[...]
            prods[s] = prods[s] * d
            tile(pcum, t, blocks)[...] = prods[s]
            th = jnp.tanh(cells[s])
            h = o * th
            tile(hs, t, blocks)[...] = h
            tile(src, t, blocks)[...] = o - h * th
        return tuple(cells + prods)

    lax.fori_loop(0, length, own_step, starts(0, seg_o) + (jnp.ones((blocks, LANE), F32),) * CHAINS, unroll=4)
    flatten(low)
    save = pltpu.make_async_copy(low, hid, sem)
    save.start()
    logits[...] = lax.dot_general(wt_o[...], low[...], nt, preferred_element_type=F32) + bias[...]
    first = lax.axis_index("ctx") % 2 == 0
    half = vocab // 2
    for p in range(others):
        tab = tab_x[p]
        direct, passed = halves[2 * p:2 * p + 2]
        wt_x[0:half, :] = jnp.where(first, direct[...], passed[...])
        wt_x[half:vocab, :] = jnp.where(first, passed[...], direct[...])

        def other_step(r, carry):
            cells = list(carry)
            for s in range(CHAINS):
                t = s * length + r
                at = ids[t]
                cells[s] = tile(tab, at, blocks, 0, 3)[...] * cells[s] + tile(tab, at, blocks, 1, 3)[...]
                tile(hs, t, blocks)[...] = tile(tab, at, blocks, 2, 3)[...] * jnp.tanh(cells[s])
            return tuple(cells)

        lax.fori_loop(0, length, other_step, starts(p + 1, seg_x[p]), unroll=4)
        flatten(low_x)
        logits[...] += lax.dot_general(wt_x[...], low_x[...], nt, preferred_element_type=F32)

    rows = 1024

    def save_src(k):
        place = pl.ds(pl.multiple_of(k * rows * blocks, rows * blocks), rows * blocks)
        return pltpu.make_async_copy(src.at[place, :], src_out.at[place, :], src_sems.at[k])


    def back(k, carry):
        loss, b_grad = carry
        at = pl.multiple_of(k * rows, rows)
        part = logits[:, pl.ds(at, rows)]
        target = lax.broadcasted_iota(jnp.int32, (vocab, rows), 0) == tgt[:, pl.ds(at, rows)]
        top = jnp.max(part, axis=0, keepdims=True)
        power = jnp.exp(part - top)
        norm = jnp.sum(power, axis=0, keepdims=True)
        picked = jnp.sum(jnp.where(target, part, 0.0), axis=0, keepdims=True)
        loss = loss + (top + jnp.log(norm) - picked)
        share = power * ((1.0 / norm) * (1.0 / total_tokens))
        grad = (share - jnp.where(target, 1.0 / total_tokens, 0.0)).astype(BF16)
        lgrad[:, pl.ds(at, rows)] = grad
        b_grad = b_grad + jnp.sum(grad.astype(F32).reshape(vocab, rows // LANE, LANE), axis=1)
        hg = lax.dot_general(grad, wt_o[...], tn, preferred_element_type=F32)
        low_x[pl.ds(at, rows), :] = (hg * low[pl.ds(at, rows), :].astype(F32)).astype(BF16)
        for b in range(blocks):
            hs[pl.ds(at * blocks + b, rows, stride=blocks), :] = hg[:, b * LANE:(b + 1) * LANE]
        for q in range(rows // length):
            place = pl.ds((at + q * length) * blocks, length * blocks)
            grad_src = src[place, :] * hs[place, :]
            src[place, :] = grad_src
            ends = (pcum[place, :] * grad_src).reshape(length, blocks, LANE)
            tile(heads, k * (rows // length) + q, blocks)[...] = jnp.sum(ends, axis=0)
        save_src(k).start()
        return loss, b_grad

    loss, b_grad = lax.fori_loop(
        0, toks // rows, back, (jnp.zeros((1, rows), F32), jnp.zeros((vocab, LANE), F32))
    )
    lane = lax.broadcasted_iota(jnp.int32, (vocab, LANE), 1)
    row = lax.broadcasted_iota(jnp.int32, (vocab, LANE), 0)
    sums[...] = jnp.where(lane == LANE - 1, jnp.sum(b_grad, axis=1, keepdims=True), 0.0) + jnp.where(
        (lane == LANE - 2) & (row == 0), jnp.sum(loss, axis=1, keepdims=True), 0.0
    )
    grad_out = jnp.dot(lgrad[...], low[...], preferred_element_type=F32)
    part = keep_o.shape[1]
    count = head.shape[0]
    splits = count // blocks

    def piece(q):
        c, e = q // splits, q % splits
        size = max(0, min(part, vocab - e * part))
        return padded(grad_out, slice(e * part, e * part + size), slice(c * LANE, (c + 1) * LANE), part)

    store_pairs(keep_o, send_o, lax.axis_index("ctx"), piece, count, slice(0, part))
    chars = lax.broadcasted_iota(jnp.int32, (vocab, toks), 0) == ids_row[...]
    o_sum[...] = jnp.dot(chars.astype(F32).astype(BF16), low_x[...], preferred_element_type=F32)
    save.wait()
    for k in range(toks // rows):
        save_src(k).wait()
    total = tile(heads, CHAINS - 1, blocks)[...]
    for s in range(CHAINS - 2, -1, -1):
        total = tile(heads, s, blocks)[...] + seg_o[s, 0] * total
    for d in range(head.shape[0]):
        head[d] = total


def char_sum_kernel(
    ids, block_of, tab, seg, heads, h_all, ps_all, prev, src, sums, order, carry, *refs, copies, blocks
):
    number = pl.program_id(0)
    length = ids.shape[0] // CHAINS
    span = src.shape[1] // blocks
    sets = [refs[2 * k:2 * k + 2] for k in range(copies)]

    @pl.when(number == 0)
    def _():
        for ref in refs:
            ref[...] = jnp.zeros_like(ref)
        own = stream_order(order, block_of)
        count = block_of.shape[0]

        def from_later(i, g):
            slot = order[count - 1 - i]
            return h_all[slot] + ps_all[slot, 0] * g

        later = lax.fori_loop(0, count - 1 - own, from_later, jnp.zeros((blocks, LANE), F32))
        for s in range(CHAINS - 1, -1, -1):
            carry[s] = later
            later = tile(heads, s, blocks)[...] + seg[s, 0] * later

    def step(i, later):
        h = list(later)
        r = span - 1 - i
        for s in range(CHAINS):
            token = s * length + (pl.num_programs(0) - 1 - number) * span + r
            at = ids[token]
            here = pl.ds(pl.multiple_of(r * blocks, blocks), blocks)
            g = src[s, here, :] + h[s]
            h[s] = tile(tab, at, blocks, 0, 2)[...] * g
            cell, forget = sets[s % copies]
            tile(cell, at, blocks)[...] += g
            tile(forget, at, blocks)[...] += g * tile(prev, token, blocks)[...]
        return tuple(h)

    ends = lax.fori_loop(0, span, step, tuple(carry[s] for s in range(CHAINS)))
    for s in range(CHAINS):
        carry[s] = ends[s]

    @pl.when(number == pl.num_programs(0) - 1)
    def _():
        for k in range(2):
            value = refs[k][...]
            for more in sets[1:]:
                value = value + more[k][...]
            sums[k] = value


def gate_sum_kernel(spots, sums, o_sum, embed, w, extra, high, low, keep_e, send_e, merged, *, count, vocab, blocks):
    rows = high.shape[1]
    merged[...] = sums[...]
    for k in range(spots.shape[0]):
        tile(merged.at[0], spots[k], blocks)[...] += tile(merged.at[0], vocab + k, blocks)[...]
    pad = (rows - vocab) * blocks
    for q in range(2):
        merged[q, vocab * blocks:, :] = jnp.zeros((pad, LANE), F32)

    def units(value_of):
        return jnp.concatenate([value_of(b) for b in range(blocks)], axis=1)

    def column(q, b):
        return merged[q, pl.ds(b, rows, stride=blocks), :]

    def gate_of(g):
        return jnp.dot(embed[...], w[g], preferred_element_type=F32)

    both = (((1,), (1,)), ((), ()))
    in_gate, cand = jax.nn.sigmoid(gate_of(0)), jnp.tanh(gate_of(2))
    forget = jax.nn.sigmoid(gate_of(1) + 3.0)
    cell = units(lambda b: column(0, b))
    source = in_gate * cand
    parts = [
        lambda: cell * (source - source * in_gate),
        lambda: units(lambda b: column(1, b)) * (forget - forget * forget),
        lambda: cell * (in_gate - source * cand),
        lambda: o_sum[...] * (1.0 - jax.nn.sigmoid(gate_of(3))),
    ]
    part_e = jnp.zeros((rows, w.shape[1]), F32)
    for gate in range(4):
        total = parts[gate]()
        high[gate] = total.astype(BF16)
        low[gate] = (total - high[gate].astype(F32)).astype(BF16)
        part_e = part_e + lax.dot_general(high[gate], w[gate], both, preferred_element_type=F32)
        part_e = part_e + lax.dot_general(low[gate], w[gate], both, preferred_element_type=F32)
    per = keep_e.shape[1]
    wide_e = jnp.concatenate([part_e, jnp.zeros((rows, LANE - part_e.shape[1]), F32)], axis=1) + extra[...]
    wide_e = jnp.concatenate([wide_e, jnp.zeros((count * per - rows, LANE), F32)], axis=0)
    me = lax.axis_index("ctx")
    store_pairs(keep_e, send_e, me, lambda q: wide_e[q * per:(q + 1) * per, :], count, slice(0, per))


def input_grad_kernel(high, low, table, keep, send, *, count, part, blocks):
    tn = (((0,), (0,)), ((), ()))
    splits = count // blocks
    for gate in range(4):
        wide = lax.dot_general(table[...], high[gate], tn, preferred_element_type=F32)
        wide = wide + lax.dot_general(table[...], low[gate], tn, preferred_element_type=F32)

        def piece(q):
            c, e = q // splits, q % splits
            size = max(0, min(part, wide.shape[0] - e * part))
            return padded(wide, slice(e * part, e * part + size), slice(c * LANE, (c + 1) * LANE), part)

        store_pairs(keep, send, lax.axis_index("ctx"), piece, count, slice(gate * part, (gate + 1) * part))


def finish_kernel(mine_a, mine_b, theirs_a, theirs_b, w_grad, b_grad, out_grad, *, groups, part, emb):
    count = 2 * mine_a.shape[0]
    me = lax.axis_index("ctx")
    first = me % 2 == 0
    stages = gather_stages_of(count)
    pairs = {}
    top = mine_a.shape[1]
    rest = section_rows(groups) - top

    def chunk(q, rows):
        pair = q - q % 2
        if pair not in pairs:
            slot = slot_of(pair ^ (me - me % 2), count, stages)
            own, other = (
                jnp.concatenate([a[slot].astype(jnp.int32), b[slot, 0:rest].astype(jnp.int32)], axis=0)
                for a, b in ((mine_a, mine_b), (theirs_a, theirs_b))
            )
            pairs[pair] = [
                decode(jnp.where(first, own, other), groups), decode(jnp.where(first, other, own), groups)
            ]
        return pairs[pair][q % 2][rows]

    cols = w_grad.shape[2] // LANE
    splits = count // cols
    vpart = groups[-1]
    vocab = out_grad.shape[0]
    for c in range(cols):
        lanes = slice(c * LANE, (c + 1) * LANE)
        for e in range(splits):
            q = c * splits + e
            size = max(0, min(part, emb - e * part))
            for gate in range(4):
                if size:
                    w_grad[e * part:e * part + size, gate, lanes] = chunk(q, slice(gate * part, gate * part + size))
                if e * part <= emb < (e + 1) * part:
                    at = gate * part + emb - e * part
                    b_grad[gate:gate + 1, lanes] = chunk(q, slice(at, at + 1))
            size = max(0, min(vpart, vocab - e * vpart))
            if size:
                out_grad[e * vpart:e * vpart + size, lanes] = chunk(q, slice(4 * part, 4 * part + size))


def tree_sum(values):
    while len(values) > 1:
        values = [values[k] + values[k + 1] for k in range(0, len(values), 2)]
    return values[0]


def embed_finish_kernel(*refs, groups, shards, total_tokens):
    codes, theirs_b = refs[:2 * shards - 1], refs[2 * shards - 1]
    e_grad, o_grad, loss, eacc = refs[2 * shards:]
    count = 2 * codes[0].shape[0]
    me = lax.axis_index("ctx")
    first = me % 2 == 0
    stages = gather_stages_of(count)
    per, rows = sum(groups), codes[0].shape[1]
    for p in range(0, count, 2):
        slot = slot_of(p ^ (me - me % 2), count, stages)
        own = [codes[k if k == 0 else 2 * k - 1][slot] for k in range(shards)]
        other = [theirs_b[slot, theirs_b.shape[1] - rows:]] + [codes[2 * k][slot] for k in range(1, shards)]
        own, other = (tree_sum([decode(code, groups) for code in kind]) for kind in (own, other))
        eacc[p * per:(p + 1) * per, :] = jnp.where(first, own, other)
        eacc[(p + 1) * per:(p + 2) * per, :] = jnp.where(first, other, own)
    vocab, emb = e_grad.shape
    e_grad[...] = eacc[0:vocab, 0:emb]
    for k in range(eacc.shape[0] // LANE):
        size = max(0, min(LANE, vocab - k * LANE))
        if size:
            flipped = jnp.transpose(eacc[k * LANE:(k + 1) * LANE, :], (1, 0))
            o_grad[:, k * LANE:k * LANE + size] = flipped[LANE - 1:LANE, 0:size] * (1.0 / shards)
    loss[...] = eacc[0:1, LANE - 2:LANE - 1] * (1.0 / (shards * total_tokens))


def half_of(value, core):
    half = value.shape[0] // 2
    return lax.dynamic_slice_in_dim(value, core * half, half, 0)


def from_others(value, wa):
    return [lax.ppermute(value, "wa", [(k, (k - s) % wa) for k in range(wa)]) for s in range(1, wa)]


def after(value, earlier):
    return lax.optimization_barrier((value, earlier))[0]


def body(ids, targets, doc_lengths, block_of, embed, w_in, b_in, w_out, b_out):
    count = lax.axis_size("ctx")
    wa = lax.axis_size("wa")
    toks = ids.shape[0]
    emb, gates, width = w_in.shape
    blocks = width // LANE
    vocab = embed.shape[0]
    docs = doc_lengths.shape[0]
    vpad = ceil_to(vocab + docs, 32)
    kdim = ceil_to(emb + 3, 16)
    total_tokens = toks * count
    core = lax.axis_index("ctx") % 2

    b_hi = lax.reduce_precision(b_in, 8, 7)
    b_mid = lax.reduce_precision(b_in - b_hi, 8, 7)
    extra_rows = jnp.stack([b_hi, b_mid, b_in - b_hi - b_mid], axis=1).astype(BF16)
    fill = jnp.zeros((gates, kdim - emb - 3, width), BF16)
    w_own = jnp.concatenate([jnp.transpose(w_in, (1, 0, 2)), extra_rows, fill], axis=1)
    ones_col = (jnp.arange(kdim) >= emb) & (jnp.arange(kdim) < emb + 3)
    ones_row = jnp.arange(vpad) < vocab
    table = jnp.pad(embed, ((0, vpad - vocab), (0, kdim - emb)))
    table = jnp.where(ones_col[None, :] & ones_row[:, None], jnp.ones((), BF16), table)

    chip = lambda *shape: pltpu.VMEM(shape, F32)
    hbm = lambda shape, kind: jax.ShapeDtypeStruct(shape, kind)
    smem = lambda shape: jax.ShapeDtypeStruct(shape, jnp.int32)
    tokens = (toks * blocks, LANE)

    bf = lambda *shape: pltpu.HBM(shape, BF16)
    marked, spots, tab, seg, ends, w_far, wt_own, wt_far = call(
        functools.partial(own_table_kernel, vocab=vocab, blocks=blocks),
        "tables_own",
        [doc_lengths, block_of],
        [ids, table, w_own, w_out.T],
        [smem((toks,)), smem((docs,)), pltpu.HBM((vpad * 2 * blocks, LANE), F32), pltpu.HBM((CHAINS, 2, blocks, LANE), F32),
         pltpu.HBM((count, 2, blocks, LANE), F32), bf(gates // 2, kdim, width), bf(vpad, width), bf(vpad // 2, width)],
        [pltpu.VMEM((vpad * 2 * blocks, LANE), F32), pltpu.SemaphoreType.DMA, pltpu.SemaphoreType.DMA],
        in_spaces=[pl.ANY, pltpu.VMEM, pltpu.VMEM, pltpu.VMEM],
        out_spaces=[pltpu.SMEM, pltpu.SMEM, pl.ANY] + [pltpu.VMEM] * 5,
        micros=6,
    )
    tab = near(tab)
    w_far, seg_x, wt_far = from_others(w_far, wa), from_others(seg, wa), from_others(wt_far, wa)
    ps_all = exchange(ends, "ctx")
    bias_out = jnp.pad(b_out, (0, vpad - vocab), constant_values=-1e30)[:, None]
    (o_tab,) = call(
        functools.partial(rest_table_kernel, vocab=vocab, blocks=blocks),
        "tables_rest",
        [spots],
        [table, w_own],
        [chip(vpad * blocks, LANE)],
        micros=3,
    )
    o_tab = near(o_tab)
    (carry,) = call(
        carry_kernel, "carry", [block_of], [ps_all, o_tab, bias_out], [hbm((blocks, LANE), F32)],
        [pltpu.SMEM((count,), jnp.int32)], in_spaces=[pltpu.VMEM, pltpu.VMEM, pl.ANY],
    )
    carries = [carry] + from_others(carry, wa)
    w_far = [after(w, ps_all) for w in w_far]
    w_oth = [v for w in w_far for v in (w, swap(w, "ctx", 1))]
    wt_far = [after(w, carry) for w in wt_far]
    wt_oth = [v for w in wt_far for v in (w, swap(w, "ctx", 1))]
    others = wa - 1
    tab_x = [
        near(call(
            functools.partial(other_table_kernel, vocab=vocab, blocks=blocks),
            "tables_other",
            [spots],
            [table] + w_oth[2 * p:2 * p + 2],
            [chip(vpad * 3 * blocks, LANE)],
            micros=3,
        )[0])
        for p in range(others)
    ]

    splits = count // blocks
    vpart = ceil_to(-(-vpad // splits), 8)
    half_chunks = lambda rows: [hbm((count // 2, rows, LANE), F32)] * 2
    copies = 2
    hid, prev, src, keep_o, send_o, heads, head, o_sum, extra = call(
        functools.partial(cell_kernel, others=others, total_tokens=total_tokens, blocks=blocks),
        "cells",
        [marked],
        [tab, o_tab, seg, wt_own, bias_out, targets[None], ids[None]] + carries + tab_x + seg_x + wt_oth,
        [
            hbm((toks, width), BF16), chip(*tokens), hbm(tokens, F32),
            *half_chunks(vpart), chip(CHAINS * blocks, LANE), hbm((count, blocks, LANE), F32),
            chip(vpad, width), hbm((vpad, LANE), F32),
        ],
        [
            pltpu.VMEM(tokens, F32), pltpu.VMEM(tokens, F32), pltpu.VMEM((toks, width), BF16),
            pltpu.VMEM((toks, width), BF16), pltpu.VMEM((vpad, width), BF16), pltpu.VMEM((vpad, toks), F32), pltpu.VMEM(tokens, F32),
            pltpu.VMEM((vpad, toks), BF16), pltpu.SemaphoreType.DMA, pltpu.SemaphoreType.DMA((toks // 1024,)),
        ],
        limit=44,
        out_spaces=[pl.ANY, pltpu.VMEM, pl.ANY] + [pltpu.VMEM] * 6,
        micros=26,
    )
    prev, heads, o_sum = near(prev), near(heads), near(o_sum)
    part = ceil_to(-(-kdim // splits), 8)
    per = ceil_to(-(-vpad // count), 8)
    h_all = exchange(head, "ctx")
    got_o = swap(send_o, "ctx", 1)
    length = toks // CHAINS
    span = 32
    block = pl.BlockSpec((CHAINS, span * blocks, LANE), lambda i: (0, length // span - 1 - i, 0))
    (sums,) = call(
        functools.partial(char_sum_kernel, copies=copies, blocks=blocks),
        "char_sums",
        [marked, block_of],
        [tab, seg, heads, h_all, ps_all, prev, far(src.reshape(CHAINS, length * blocks, LANE))],
        [chip(2, vpad * blocks, LANE)],
        [pltpu.SMEM((count,), jnp.int32), pltpu.VMEM((CHAINS, blocks, LANE), F32)]
        + [pltpu.VMEM((vpad * blocks, LANE), F32)] * (2 * copies),
        limit=24,
        in_spaces=[pltpu.VMEM] * 6 + [block],
        micros=(9, length // span),
    )
    high, low, keep_e, send_e = call(
        functools.partial(gate_sum_kernel, count=count, vocab=vocab, blocks=blocks),
        "gate_sums",
        [spots],
        [near(sums), o_sum, table, w_own, extra],
        [pltpu.VMEM((gates, vpad, width), BF16)] * 2 + half_chunks(per),
        [pltpu.VMEM((2, vpad * blocks, LANE), F32)],
        limit=24,
        micros=3,
    )
    keep, send = call(
        functools.partial(input_grad_kernel, count=count, part=part, blocks=blocks),
        "input_grad",
        [],
        [near(high), near(low), table],
        half_chunks(4 * part),
        limit=24,
        micros=3,
    )
    sections = [[part] * gates + [vpart], [per]]
    apart = section_rows(sections[1])
    chunk = reduce_chunks(
        [keep, keep_o, keep_e], [swap(send, "ctx", 1), got_o, swap(send_e, "ctx", 1)], sections, "ctx"
    )
    halves, tail = gather_chunks(chunk, "ctx", apart)
    far_tails = [swap(tail, "wa", mask) for mask in range(1, wa)]
    w_grad, bi_grad, w_out_grad = call(
        functools.partial(finish_kernel, groups=sections[0], part=part, emb=emb),
        "finish",
        [],
        halves,
        [hbm((emb, gates, width), F32), hbm((gates, width), F32), hbm((vocab, width), F32)],
        micros=4,
    )
    far_tails = [after(v, bi_grad) for v in far_tails]
    tails = [tail] + [v for far_tail in far_tails for v in (far_tail, swap(far_tail, "ctx", 1))]
    e_grad, bo_grad, loss = call(
        functools.partial(embed_finish_kernel, groups=sections[1], shards=wa, total_tokens=total_tokens),
        "embed_finish",
        [],
        tails + [halves[3]],
        [hbm((vocab, emb), F32), hbm((1, vocab), F32), hbm((1, 1), F32)],
        [pltpu.VMEM((ceil_to(count * per, LANE), LANE), F32)],
    )
    return (
        hid,
        loss[0, 0],
        e_grad,
        w_grad,
        bi_grad,
        w_out_grad.T,
        bo_grad[0],
    )


def solution(mesh):
    placed = (
        P("ctx"),
        P("ctx"),
        P(),
        P(),
        P(),
        P(None, None, "wa"),
        P(None, "wa"),
        P("wa", None),
        P(),
    )
    return jax.shard_map(
        body,
        mesh=mesh,
        in_specs=placed,
        out_specs=(
            P("ctx", "wa"),
            P(),
            P(),
            P(None, None, "wa"),
            P(None, "wa"),
            P("wa", None),
            P(),
        ),
        check_vma=False,
    )
```

```python
import functools

import jax
import jax.numpy as jnp
from jax import lax
from jax.experimental import pallas as pl
from jax.experimental.pallas import tpu as pltpu
from jax.sharding import PartitionSpec as P

CHAINS = 16
LANE = 128
F32 = jnp.float32
BF16 = jnp.bfloat16


def ceil_to(value, step):
    return -(-value // step) * step


def call(kernel, name, scalars, arrays, outs, scratch=(), limit=16, in_spaces=None, out_spaces=None, micros=1):
    spec = lambda m: m if isinstance(m, pl.BlockSpec) else pl.BlockSpec(memory_space=m)
    blocked = [m for m in in_spaces or [] if isinstance(m, pl.BlockSpec)]
    steps = micros[1] if blocked else None
    return pl.pallas_call(
        kernel,
        grid=(steps,) if blocked else (),
        in_specs=[spec(pltpu.SMEM)] * len(scalars) + [spec(m) for m in in_spaces or [pltpu.VMEM] * len(arrays)],
        out_specs=[spec(m) for m in out_spaces or [pltpu.VMEM] * len(outs)],
        out_shape=list(outs),
        scratch_shapes=list(scratch),
        compiler_params=pltpu.CompilerParams(vmem_limit_bytes=limit * 1024 * 1024),
        cost_estimate=pl.CostEstimate(
            flops=0, transcendentals=0, bytes_accessed=3000000 * (micros[0] if blocked else micros)
        ),
        name=name,
    )(*scalars, *arrays)


def near(value):
    return pltpu.with_memory_space_constraint(value, pltpu.VMEM)


def far(value):
    return pltpu.with_memory_space_constraint(value, pltpu.HBM)


def stages_of(count):
    stages, bit = [[1]], 2
    while bit < count:
        ways = min(4 if bit == 2 else 2, count // bit)
        stages.append([k * bit for k in range(1, ways)])
        bit *= ways
    return stages


def gather_stages_of(count):
    stages, bit = [[1]], 2
    while bit < count:
        ways = min(2 if bit == 2 else 4, count // bit)
        stages.append([k * bit for k in range(1, ways)])
        bit *= ways
    return stages


def swap(value, axis, mask):
    count = lax.axis_size(axis)
    return lax.ppermute(value, axis, [(k, k ^ mask) for k in range(count)])


def exchange(copies, axis):
    return lax.all_to_all(copies, axis, 0, 0, tiled=True)


def slot_of(xor_index, count, stages=None):
    place, size, bit = 0, count, 1
    for masks in stages or stages_of(count):
        ways = len(masks) + 1
        size = size // ways
        place = place + ((xor_index // bit) % ways) * size
        bit = bit * ways
    return place


STEPS = 32766.0
BIAS = 90


def power_of_two(exponent):
    value = jnp.full(exponent.shape, 2.0 ** -BIAS, F32)
    for bit in range(7):
        on = ((exponent + BIAS) // (1 << bit)) % 2 == 1
        value = value * jnp.where(on, 2.0 ** (1 << bit), 1.0)
    return value


def section_rows(groups):
    return ceil_to(sum(groups) + len(groups), 16)


def coded_rows(sections):
    return sum(section_rows(groups) for groups in sections)


def encode_all(value, sections):
    parts, at = [], 0
    for groups in sections:
        parts.append(encode(value[at:at + sum(groups)], groups))
        at += sum(groups)
    return jnp.concatenate(parts, axis=0)


def decode_all(code, sections):
    parts, at = [], 0
    for groups in sections:
        parts.append(decode(code[at:at + section_rows(groups)], groups))
        at += section_rows(groups)
    return jnp.concatenate(parts, axis=0)


def encode(value, groups):
    parts, exponents, at = [], [], 0
    for size in groups:
        part = value[at:at + size]
        most = jnp.max(jnp.abs(part), axis=0, keepdims=True)
        exponent = jnp.ceil(jnp.log2(jnp.maximum(most, 2.0 ** (1 - BIAS)))).astype(jnp.int32)
        exponent = jnp.clip(exponent, -BIAS, 127 - BIAS)
        parts.append(jnp.round(part * (STEPS / power_of_two(exponent))).astype(jnp.int32))
        exponents.append(exponent)
        at += size
    fill = section_rows(groups) - at - len(groups)
    if fill:
        exponents.append(jnp.zeros((fill, value.shape[1]), jnp.int32))
    return jnp.concatenate(parts + exponents, axis=0).astype(jnp.int16)


def decode(code, groups):
    code = code.astype(jnp.int32)
    parts, at, total = [], 0, sum(groups)
    for k, size in enumerate(groups):
        unit = power_of_two(code[total + k:total + k + 1]) * (1.0 / STEPS)
        parts.append(code[at:at + size].astype(F32) * unit)
        at += size
    return jnp.concatenate(parts, axis=0)


def reduce_chunks(keeps, moved, sections, axis):
    stages = stages_of(lax.axis_size(axis))[1:]
    number = len(keeps)
    sizes = [k.shape[1] for k in keeps]
    rows, coded = sum(sizes), coded_rows(sections)
    half = keeps[0].shape[0]
    ways = len(stages[0]) + 1 if stages else 1
    code_shape = lambda size: jax.ShapeDtypeStruct((size, coded, LANE), jnp.int16)

    def first(*refs):
        ins, outs = refs[:2 * number], refs[2 * number:]
        for place in range(half):
            way, slot = place // (half // ways), place % (half // ways)
            parts = [ins[k][place] + ins[number + k][place] for k in range(number)]
            value = jnp.concatenate(parts, axis=0)
            outs[way][slot] = value if way == 0 else encode_all(value, sections)

    keep, *sends = call(
        first,
        "core_sum",
        [],
        list(keeps) + list(moved),
        [jax.ShapeDtypeStruct((half // ways, rows, LANE), F32)] + [code_shape(half // ways)] * (ways - 1),
        limit=24,
    )
    for k, masks in enumerate(stages):
        got = [swap(part, axis, mask) for part, mask in zip(sends, masks)]
        ways = len(stages[k + 1]) + 1 if k + 1 < len(stages) else 1
        size = keep.shape[0] // ways
        last = k + 1 == len(stages)

        def later(*refs):
            ins, outs = refs[:len(got) + 1], refs[len(got) + 1:]
            for way in range(ways):
                for slot in range(size):
                    value = ins[0][way * size + slot]
                    for ref in ins[1:]:
                        value = value + decode_all(ref[way * size + slot], sections)
                    outs[way][slot] = value if way == 0 and not last else encode_all(value, sections)

        kept = code_shape(size) if last else jax.ShapeDtypeStruct((size, rows, LANE), F32)
        keep, *sends = call(
            later, "chip_sum" + str(k), [], [keep] + got, [kept] + [code_shape(size)] * (ways - 1), limit=24
        )
    return keep


def gather_chunks(chunk, axis, apart):
    stages = gather_stages_of(lax.axis_size(axis))
    middle = ceil_to(chunk.shape[1] // 2, 16)
    halves, tail = [chunk[:, :middle], chunk[:, middle:]], None
    for number, masks in enumerate(reversed(stages[1:])):
        for h in range(2):
            value = halves[h]
            parts = [value] + [swap(value, axis, mask) for mask in masks]
            size, rows = value.shape[0], value.shape[1]
            outs = [jax.ShapeDtypeStruct((size * len(parts), rows, LANE), value.dtype)]
            if h == 1 and number == len(stages) - 2:
                outs.append(jax.ShapeDtypeStruct((size * len(parts), apart, LANE), value.dtype))

            def kernel(*refs):
                for k in range(len(parts)):
                    for out in refs[len(parts):]:
                        out[k * size:(k + 1) * size] = refs[k][:, rows - out.shape[1]:, :]

            got = call(kernel, "chunk_join" + str(number), [], parts, outs)
            halves[h], tail = got[0], got[-1]
    return halves + [swap(h, axis, 1) for h in halves], tail


def padded(value, rows, lanes, size):
    count = rows.stop - rows.start
    if count == 0:
        return jnp.zeros((size, LANE), F32)
    piece = value[rows, lanes]
    return piece if count == size else jnp.concatenate([piece, jnp.zeros((size - count, LANE), F32)], axis=0)


def store_pairs(keep, send, me, value_of, count, rows):
    first = me % 2 == 0
    for pair in range(count // 2):
        a, b = value_of(2 * pair), value_of(2 * pair + 1)
        slot = slot_of((2 * pair) ^ (me - me % 2), count)
        keep[slot, rows, :] = jnp.where(first, a, b)
        send[slot, rows, :] = jnp.where(first, b, a)


def tile(ref, index, blocks, kind=0, kinds=1):
    return ref.at[pl.ds(pl.multiple_of((index * kinds + kind) * blocks, blocks), blocks), :]


def spread(ref, value, first, blocks, kind=0, kinds=1):
    rows = value.shape[0]
    for b in range(blocks):
        place = pl.ds((first * kinds + kind) * blocks + b, rows, stride=kinds * blocks)
        ref[place, :] = value[:, b * LANE:(b + 1) * LANE]


def gathered(ref, first, rows, blocks, b, kind=0, kinds=1):
    return ref[pl.ds((first * kinds + kind) * blocks + b, rows, stride=kinds * blocks), :]


def stream_order(order, block_of):
    def place(d, carry):
        order[block_of[d]] = d
        return carry

    lax.fori_loop(0, block_of.shape[0], place, 0)
    return block_of[lax.axis_index("ctx")]


def segment_ends(ids, tab, toks, blocks, kinds):
    length = toks // CHAINS

    def step(r, carry):
        prod, total = list(carry[:CHAINS]), list(carry[CHAINS:])
        for s in range(CHAINS):
            at = ids[s * length + r]
            d = tile(tab, at, blocks, 0, kinds)[...]
            total[s] = d * total[s] + tile(tab, at, blocks, 1, kinds)[...]
            prod[s] = prod[s] * d
        return tuple(prod + total)

    first = [jnp.ones((blocks, LANE), F32)] * CHAINS + [jnp.zeros((blocks, LANE), F32)] * CHAINS
    carry = lax.fori_loop(0, length, step, tuple(first), unroll=2)
    return carry[:CHAINS], carry[CHAINS:]


def own_table_kernel(
    doc_lengths, block_of, ids, embed, w, w_out, marked, spots, tab_out, seg, ends, w_far, wt, wt_far, tab, sem, tab_sem,
    *, vocab, blocks,
):
    toks = ids.shape[0]
    copy = pltpu.make_async_copy(ids, marked, sem)
    copy.start()
    core = lax.axis_index("ctx") % 2
    shape = (wt.shape[0], w_out.shape[0])
    same = lax.broadcasted_iota(jnp.int32, shape, 0) == lax.broadcasted_iota(jnp.int32, shape, 1)
    turned = jnp.dot(same.astype(F32).astype(BF16), w_out[...], preferred_element_type=F32).astype(BF16)
    wt[...] = turned
    half = wt_far.shape[0]
    wt_far[...] = jnp.where(core == 0, turned[0:half], turned[half:2 * half])
    for g in range(w_far.shape[0]):
        w_far[g] = w[core * w_far.shape[0] + g]
    gate = [jnp.dot(embed[...], w[g], preferred_element_type=F32) for g in range(3)]
    spread(tab, jax.nn.sigmoid(gate[1] + 3.0), 0, blocks, 0, 2)
    spread(tab, jax.nn.sigmoid(gate[0]) * jnp.tanh(gate[2]), 0, blocks, 1, 2)
    copy.wait()
    start = -block_of[lax.axis_index("ctx")] * toks
    for k in range(doc_lengths.shape[0]):
        inside = (start >= 0) & (start < toks)
        at = jnp.clip(start, 0, toks - 1)
        spot = jnp.where(inside, marked[at], 0)
        spots[k] = spot
        marked[at] = jnp.where(inside, vocab + k, marked[at])
        tile(tab, vocab + k, blocks, 0, 2)[...] = jnp.zeros((blocks, LANE), F32)
        tile(tab, vocab + k, blocks, 1, 2)[...] = tile(tab, spot, blocks, 1, 2)[...]
        start = start + doc_lengths[k]
    save = pltpu.make_async_copy(tab, tab_out, tab_sem)
    save.start()
    prod, total = segment_ends(marked, tab, toks, blocks, 2)
    p_all, s_all = prod[0], total[0]
    for s in range(CHAINS):
        seg[s, 0] = prod[s]
        seg[s, 1] = total[s]
        if s:
            s_all = prod[s] * s_all + total[s]
            p_all = prod[s] * p_all
    for d in range(ends.shape[0]):
        ends[d, 0] = p_all
        ends[d, 1] = s_all
    save.wait()


def carry_kernel(block_of, ps_all, _, bias, carry, order):
    own = stream_order(order, block_of)

    def earlier(b, c):
        return ps_all[order[b], 0] * c + ps_all[order[b], 1]

    carry[...] = lax.fori_loop(0, own, earlier, jnp.zeros(carry.shape, F32))


def rest_table_kernel(spots, embed, w, o_tab, *, vocab, blocks):
    spread(o_tab, jax.nn.sigmoid(jnp.dot(embed[...], w[3], preferred_element_type=F32)), 0, blocks)
    for k in range(spots.shape[0]):
        tile(o_tab, vocab + k, blocks)[...] = tile(o_tab, spots[k], blocks)[...]


def other_table_kernel(spots, embed, direct, passed, tab, *, vocab, blocks):
    first = lax.axis_index("ctx") % 2 == 0

    def weights(g):
        mine, theirs = direct[g % 2], passed[g % 2]
        return jnp.where(first, mine, theirs) if g < 2 else jnp.where(first, theirs, mine)

    gate = [jnp.dot(embed[...], weights(g), preferred_element_type=F32) for g in range(4)]
    spread(tab, jax.nn.sigmoid(gate[1] + 3.0), 0, blocks, 0, 3)
    spread(tab, jax.nn.sigmoid(gate[0]) * jnp.tanh(gate[2]), 0, blocks, 1, 3)
    spread(tab, jax.nn.sigmoid(gate[3]), 0, blocks, 2, 3)
    for k in range(spots.shape[0]):
        tile(tab, vocab + k, blocks, 0, 3)[...] = jnp.zeros((blocks, LANE), F32)
        for kind in (1, 2):
            tile(tab, vocab + k, blocks, kind, 3)[...] = tile(tab, spots[k], blocks, kind, 3)[...]


def cell_kernel(*refs, others, total_tokens, blocks):
    ids, tab_o, o_tab, seg_o, wt_o, bias, tgt, ids_row = refs[:8]
    carries = refs[8:9 + others]
    refs = refs[9 + others:]
    tab_x, seg_x = refs[:others], refs[others:2 * others]
    halves = refs[2 * others:4 * others]
    refs = refs[4 * others:]
    hid, prev, src_out, keep_o, send_o, heads, head, o_sum, sums = refs[:9]
    src, hs, low, low_x, wt_x, logits, pcum, lgrad, sem, src_sems = refs[9:]
    toks = ids.shape[0]
    length = toks // CHAINS
    width = blocks * LANE
    vocab = wt_o.shape[0]
    nt = (((1,), (1,)), ((), ()))
    tn = (((0,), (0,)), ((), ()))

    def starts(piece, seg):
        c = carries[piece][...]
        out = []
        for s in range(CHAINS):
            out.append(c)
            c = seg[s, 0] * c + seg[s, 1]
        return tuple(out)

    def flatten(low):
        rows = 256

        def part(k, carry):
            at = pl.multiple_of(k * rows, rows)
            value = hs[pl.ds(at * blocks, rows * blocks), :]
            low[pl.ds(at, rows), :] = value.reshape(rows, width).astype(BF16)
            return carry

        lax.fori_loop(0, toks // rows, part, 0)

    def own_step(r, carry):
        cells, prods = list(carry[:CHAINS]), list(carry[CHAINS:])
        for s in range(CHAINS):
            t = s * length + r
            at = ids[t]
            d = tile(tab_o, at, blocks, 0, 2)[...]
            o = tile(o_tab, at, blocks)[...]
            tile(prev, t, blocks)[...] = cells[s]
            cells[s] = d * cells[s] + tile(tab_o, at, blocks, 1, 2)[...]
            prods[s] = prods[s] * d
            tile(pcum, t, blocks)[...] = prods[s]
            th = jnp.tanh(cells[s])
            h = o * th
            tile(hs, t, blocks)[...] = h
            tile(src, t, blocks)[...] = o - h * th
        return tuple(cells + prods)

    lax.fori_loop(0, length, own_step, starts(0, seg_o) + (jnp.ones((blocks, LANE), F32),) * CHAINS, unroll=4)
    flatten(low)
    save = pltpu.make_async_copy(low, hid, sem)
    save.start()
    logits[...] = lax.dot_general(wt_o[...], low[...], nt, preferred_element_type=F32) + bias[...]
    first = lax.axis_index("ctx") % 2 == 0
    half = vocab // 2
    for p in range(others):
        tab = tab_x[p]
        direct, passed = halves[2 * p:2 * p + 2]
        wt_x[0:half, :] = jnp.where(first, direct[...], passed[...])
        wt_x[half:vocab, :] = jnp.where(first, passed[...], direct[...])

        def other_step(r, carry):
            cells = list(carry)
            for s in range(CHAINS):
                t = s * length + r
                at = ids[t]
                cells[s] = tile(tab, at, blocks, 0, 3)[...] * cells[s] + tile(tab, at, blocks, 1, 3)[...]
                tile(hs, t, blocks)[...] = tile(tab, at, blocks, 2, 3)[...] * jnp.tanh(cells[s])
            return tuple(cells)

        lax.fori_loop(0, length, other_step, starts(p + 1, seg_x[p]), unroll=4)
        flatten(low_x)
        logits[...] += lax.dot_general(wt_x[...], low_x[...], nt, preferred_element_type=F32)

    rows = 1024

    def save_src(k):
        place = pl.ds(pl.multiple_of(k * rows * blocks, rows * blocks), rows * blocks)
        return pltpu.make_async_copy(src.at[place, :], src_out.at[place, :], src_sems.at[k])


    def back(k, carry):
        loss, b_grad = carry
        at = pl.multiple_of(k * rows, rows)
        part = logits[:, pl.ds(at, rows)]
        target = lax.broadcasted_iota(jnp.int32, (vocab, rows), 0) == tgt[:, pl.ds(at, rows)]
        top = jnp.max(part, axis=0, keepdims=True)
        power = jnp.exp(part - top)
        norm = jnp.sum(power, axis=0, keepdims=True)
        picked = jnp.sum(jnp.where(target, part, 0.0), axis=0, keepdims=True)
        loss = loss + (top + jnp.log(norm) - picked)
        share = power * ((1.0 / norm) * (1.0 / total_tokens))
        grad = (share - jnp.where(target, 1.0 / total_tokens, 0.0)).astype(BF16)
        lgrad[:, pl.ds(at, rows)] = grad
        b_grad = b_grad + jnp.sum(grad.astype(F32).reshape(vocab, rows // LANE, LANE), axis=1)
        hg = lax.dot_general(grad, wt_o[...], tn, preferred_element_type=F32)
        low_x[pl.ds(at, rows), :] = (hg * low[pl.ds(at, rows), :].astype(F32)).astype(BF16)
        for b in range(blocks):
            hs[pl.ds(at * blocks + b, rows, stride=blocks), :] = hg[:, b * LANE:(b + 1) * LANE]
        for q in range(rows // length):
            place = pl.ds((at + q * length) * blocks, length * blocks)
            grad_src = src[place, :] * hs[place, :]
            src[place, :] = grad_src
            ends = (pcum[place, :] * grad_src).reshape(length, blocks, LANE)
            tile(heads, k * (rows // length) + q, blocks)[...] = jnp.sum(ends, axis=0)
        save_src(k).start()
        return loss, b_grad

    loss, b_grad = lax.fori_loop(
        0, toks // rows, back, (jnp.zeros((1, rows), F32), jnp.zeros((vocab, LANE), F32))
    )
    lane = lax.broadcasted_iota(jnp.int32, (vocab, LANE), 1)
    row = lax.broadcasted_iota(jnp.int32, (vocab, LANE), 0)
    sums[...] = jnp.where(lane == LANE - 1, jnp.sum(b_grad, axis=1, keepdims=True), 0.0) + jnp.where(
        (lane == LANE - 2) & (row == 0), jnp.sum(loss, axis=1, keepdims=True), 0.0
    )
    grad_out = jnp.dot(lgrad[...], low[...], preferred_element_type=F32)
    part = keep_o.shape[1]
    count = head.shape[0]
    splits = count // blocks

    def piece(q):
        c, e = q // splits, q % splits
        size = max(0, min(part, vocab - e * part))
        return padded(grad_out, slice(e * part, e * part + size), slice(c * LANE, (c + 1) * LANE), part)

    store_pairs(keep_o, send_o, lax.axis_index("ctx"), piece, count, slice(0, part))
    chars = lax.broadcasted_iota(jnp.int32, (vocab, toks), 0) == ids_row[...]
    o_sum[...] = jnp.dot(chars.astype(F32).astype(BF16), low_x[...], preferred_element_type=F32)
    save.wait()
    for k in range(toks // rows):
        save_src(k).wait()
    total = tile(heads, CHAINS - 1, blocks)[...]
    for s in range(CHAINS - 2, -1, -1):
        total = tile(heads, s, blocks)[...] + seg_o[s, 0] * total
    for d in range(head.shape[0]):
        head[d] = total


def char_sum_kernel(
    ids, block_of, tab, seg, heads, h_all, ps_all, prev, src, sums, order, carry, *refs, copies, blocks
):
    number = pl.program_id(0)
    length = ids.shape[0] // CHAINS
    span = src.shape[1] // blocks
    sets = [refs[2 * k:2 * k + 2] for k in range(copies)]

    @pl.when(number == 0)
    def _():
        for ref in refs:
            ref[...] = jnp.zeros_like(ref)
        own = stream_order(order, block_of)
        count = block_of.shape[0]

        def from_later(i, g):
            slot = order[count - 1 - i]
            return h_all[slot] + ps_all[slot, 0] * g

        later = lax.fori_loop(0, count - 1 - own, from_later, jnp.zeros((blocks, LANE), F32))
        for s in range(CHAINS - 1, -1, -1):
            carry[s] = later
            later = tile(heads, s, blocks)[...] + seg[s, 0] * later

    def step(i, later):
        h = list(later)
        r = span - 1 - i
        for s in range(CHAINS):
            token = s * length + (pl.num_programs(0) - 1 - number) * span + r
            at = ids[token]
            here = pl.ds(pl.multiple_of(r * blocks, blocks), blocks)
            g = src[s, here, :] + h[s]
            h[s] = tile(tab, at, blocks, 0, 2)[...] * g
            cell, forget = sets[s % copies]
            tile(cell, at, blocks)[...] += g
            tile(forget, at, blocks)[...] += g * tile(prev, token, blocks)[...]
        return tuple(h)

    ends = lax.fori_loop(0, span, step, tuple(carry[s] for s in range(CHAINS)))
    for s in range(CHAINS):
        carry[s] = ends[s]

    @pl.when(number == pl.num_programs(0) - 1)
    def _():
        for k in range(2):
            value = refs[k][...]
            for more in sets[1:]:
                value = value + more[k][...]
            sums[k] = value


def gate_sum_kernel(spots, sums, o_sum, embed, w, extra, high, low, keep_e, send_e, merged, *, count, vocab, blocks):
    rows = high.shape[1]
    merged[...] = sums[...]
    for k in range(spots.shape[0]):
        tile(merged.at[0], spots[k], blocks)[...] += tile(merged.at[0], vocab + k, blocks)[...]
    pad = (rows - vocab) * blocks
    for q in range(2):
        merged[q, vocab * blocks:, :] = jnp.zeros((pad, LANE), F32)

    def units(value_of):
        return jnp.concatenate([value_of(b) for b in range(blocks)], axis=1)

    def column(q, b):
        return merged[q, pl.ds(b, rows, stride=blocks), :]

    def gate_of(g):
        return jnp.dot(embed[...], w[g], preferred_element_type=F32)

    both = (((1,), (1,)), ((), ()))
    in_gate, cand = jax.nn.sigmoid(gate_of(0)), jnp.tanh(gate_of(2))
    forget = jax.nn.sigmoid(gate_of(1) + 3.0)
    cell = units(lambda b: column(0, b))
    source = in_gate * cand
    parts = [
        lambda: cell * (source - source * in_gate),
        lambda: units(lambda b: column(1, b)) * (forget - forget * forget),
        lambda: cell * (in_gate - source * cand),
        lambda: o_sum[...] * (1.0 - jax.nn.sigmoid(gate_of(3))),
    ]
    part_e = jnp.zeros((rows, w.shape[1]), F32)
    for gate in range(4):
        total = parts[gate]()
        high[gate] = total.astype(BF16)
        low[gate] = (total - high[gate].astype(F32)).astype(BF16)
        part_e = part_e + lax.dot_general(high[gate], w[gate], both, preferred_element_type=F32)
        part_e = part_e + lax.dot_general(low[gate], w[gate], both, preferred_element_type=F32)
    per = keep_e.shape[1]
    wide_e = jnp.concatenate([part_e, jnp.zeros((rows, LANE - part_e.shape[1]), F32)], axis=1) + extra[...]
    wide_e = jnp.concatenate([wide_e, jnp.zeros((count * per - rows, LANE), F32)], axis=0)
    me = lax.axis_index("ctx")
    store_pairs(keep_e, send_e, me, lambda q: wide_e[q * per:(q + 1) * per, :], count, slice(0, per))


def input_grad_kernel(high, low, table, keep, send, *, count, part, blocks):
    tn = (((0,), (0,)), ((), ()))
    splits = count // blocks
    for gate in range(4):
        wide = lax.dot_general(table[...], high[gate], tn, preferred_element_type=F32)
        wide = wide + lax.dot_general(table[...], low[gate], tn, preferred_element_type=F32)

        def piece(q):
            c, e = q // splits, q % splits
            size = max(0, min(part, wide.shape[0] - e * part))
            return padded(wide, slice(e * part, e * part + size), slice(c * LANE, (c + 1) * LANE), part)

        store_pairs(keep, send, lax.axis_index("ctx"), piece, count, slice(gate * part, (gate + 1) * part))


def finish_kernel(mine_a, mine_b, theirs_a, theirs_b, w_grad, b_grad, out_grad, *, groups, part, emb):
    count = 2 * mine_a.shape[0]
    me = lax.axis_index("ctx")
    first = me % 2 == 0
    stages = gather_stages_of(count)
    pairs = {}
    top = mine_a.shape[1]
    rest = section_rows(groups) - top

    def chunk(q, rows):
        pair = q - q % 2
        if pair not in pairs:
            slot = slot_of(pair ^ (me - me % 2), count, stages)
            own, other = (
                jnp.concatenate([a[slot].astype(jnp.int32), b[slot, 0:rest].astype(jnp.int32)], axis=0)
                for a, b in ((mine_a, mine_b), (theirs_a, theirs_b))
            )
            pairs[pair] = [
                decode(jnp.where(first, own, other), groups), decode(jnp.where(first, other, own), groups)
            ]
        return pairs[pair][q % 2][rows]

    cols = w_grad.shape[2] // LANE
    splits = count // cols
    vpart = groups[-1]
    vocab = out_grad.shape[0]
    for c in range(cols):
        lanes = slice(c * LANE, (c + 1) * LANE)
        for e in range(splits):
            q = c * splits + e
            size = max(0, min(part, emb - e * part))
            for gate in range(4):
                if size:
                    w_grad[e * part:e * part + size, gate, lanes] = chunk(q, slice(gate * part, gate * part + size))
                if e * part <= emb < (e + 1) * part:
                    at = gate * part + emb - e * part
                    b_grad[gate:gate + 1, lanes] = chunk(q, slice(at, at + 1))
            size = max(0, min(vpart, vocab - e * vpart))
            if size:
                out_grad[e * vpart:e * vpart + size, lanes] = chunk(q, slice(4 * part, 4 * part + size))


def tree_sum(values):
    while len(values) > 1:
        values = [values[k] + values[k + 1] for k in range(0, len(values), 2)]
    return values[0]


def embed_finish_kernel(*refs, groups, shards, total_tokens):
    codes, theirs_b = refs[:2 * shards - 1], refs[2 * shards - 1]
    e_grad, o_grad, loss, eacc = refs[2 * shards:]
    count = 2 * codes[0].shape[0]
    me = lax.axis_index("ctx")
    first = me % 2 == 0
    stages = gather_stages_of(count)
    per, rows = sum(groups), codes[0].shape[1]
    for p in range(0, count, 2):
        slot = slot_of(p ^ (me - me % 2), count, stages)
        own = [codes[k if k == 0 else 2 * k - 1][slot] for k in range(shards)]
        other = [theirs_b[slot, theirs_b.shape[1] - rows:]] + [codes[2 * k][slot] for k in range(1, shards)]
        own, other = (tree_sum([decode(code, groups) for code in kind]) for kind in (own, other))
        eacc[p * per:(p + 1) * per, :] = jnp.where(first, own, other)
        eacc[(p + 1) * per:(p + 2) * per, :] = jnp.where(first, other, own)
    vocab, emb = e_grad.shape
    e_grad[...] = eacc[0:vocab, 0:emb]
    for k in range(eacc.shape[0] // LANE):
        size = max(0, min(LANE, vocab - k * LANE))
        if size:
            flipped = jnp.transpose(eacc[k * LANE:(k + 1) * LANE, :], (1, 0))
            o_grad[:, k * LANE:k * LANE + size] = flipped[LANE - 1:LANE, 0:size] * (1.0 / shards)
    loss[...] = eacc[0:1, LANE - 2:LANE - 1] * (1.0 / (shards * total_tokens))


def half_of(value, core):
    half = value.shape[0] // 2
    return lax.dynamic_slice_in_dim(value, core * half, half, 0)


def from_others(value, wa):
    return [lax.ppermute(value, "wa", [(k, (k - s) % wa) for k in range(wa)]) for s in range(1, wa)]


def after(value, earlier):
    return lax.optimization_barrier((value, earlier))[0]


def body(ids, targets, doc_lengths, block_of, embed, w_in, b_in, w_out, b_out):
    count = lax.axis_size("ctx")
    wa = lax.axis_size("wa")
    toks = ids.shape[0]
    emb, gates, width = w_in.shape
    blocks = width // LANE
    vocab = embed.shape[0]
    docs = doc_lengths.shape[0]
    vpad = ceil_to(vocab + docs, 32)
    kdim = ceil_to(emb + 3, 16)
    total_tokens = toks * count
    core = lax.axis_index("ctx") % 2

    b_hi = lax.reduce_precision(b_in, 8, 7)
    b_mid = lax.reduce_precision(b_in - b_hi, 8, 7)
    extra_rows = jnp.stack([b_hi, b_mid, b_in - b_hi - b_mid], axis=1).astype(BF16)
    fill = jnp.zeros((gates, kdim - emb - 3, width), BF16)
    w_own = jnp.concatenate([jnp.transpose(w_in, (1, 0, 2)), extra_rows, fill], axis=1)
    ones_col = (jnp.arange(kdim) >= emb) & (jnp.arange(kdim) < emb + 3)
    ones_row = jnp.arange(vpad) < vocab
    table = jnp.pad(embed, ((0, vpad - vocab), (0, kdim - emb)))
    table = jnp.where(ones_col[None, :] & ones_row[:, None], jnp.ones((), BF16), table)

    chip = lambda *shape: pltpu.VMEM(shape, F32)
    hbm = lambda shape, kind: jax.ShapeDtypeStruct(shape, kind)
    smem = lambda shape: jax.ShapeDtypeStruct(shape, jnp.int32)
    tokens = (toks * blocks, LANE)

    bf = lambda *shape: pltpu.HBM(shape, BF16)
    marked, spots, tab, seg, ends, w_far, wt_own, wt_far = call(
        functools.partial(own_table_kernel, vocab=vocab, blocks=blocks),
        "tables_own",
        [doc_lengths, block_of],
        [ids, table, w_own, w_out.T],
        [smem((toks,)), smem((docs,)), pltpu.HBM((vpad * 2 * blocks, LANE), F32), pltpu.HBM((CHAINS, 2, blocks, LANE), F32),
         pltpu.HBM((count, 2, blocks, LANE), F32), bf(gates // 2, kdim, width), bf(vpad, width), bf(vpad // 2, width)],
        [pltpu.VMEM((vpad * 2 * blocks, LANE), F32), pltpu.SemaphoreType.DMA, pltpu.SemaphoreType.DMA],
        in_spaces=[pl.ANY, pltpu.VMEM, pltpu.VMEM, pltpu.VMEM],
        out_spaces=[pltpu.SMEM, pltpu.SMEM, pl.ANY] + [pltpu.VMEM] * 5,
        micros=6,
    )
    tab = near(tab)
    w_far, seg_x, wt_far = from_others(w_far, wa), from_others(seg, wa), from_others(wt_far, wa)
    ps_all = exchange(ends, "ctx")
    bias_out = jnp.pad(b_out, (0, vpad - vocab), constant_values=-1e30)[:, None]
    (o_tab,) = call(
        functools.partial(rest_table_kernel, vocab=vocab, blocks=blocks),
        "tables_rest",
        [spots],
        [table, w_own],
        [chip(vpad * blocks, LANE)],
        micros=3,
    )
    o_tab = near(o_tab)
    (carry,) = call(
        carry_kernel, "carry", [block_of], [ps_all, o_tab, bias_out], [hbm((blocks, LANE), F32)],
        [pltpu.SMEM((count,), jnp.int32)], in_spaces=[pltpu.VMEM, pltpu.VMEM, pl.ANY],
    )
    carries = [carry] + from_others(carry, wa)
    w_far = [after(w, ps_all) for w in w_far]
    w_oth = [v for w in w_far for v in (w, swap(w, "ctx", 1))]
    wt_far = [after(w, carry) for w in wt_far]
    wt_oth = [v for w in wt_far for v in (w, swap(w, "ctx", 1))]
    others = wa - 1
    tab_x = [
        near(call(
            functools.partial(other_table_kernel, vocab=vocab, blocks=blocks),
            "tables_other",
            [spots],
            [table] + w_oth[2 * p:2 * p + 2],
            [chip(vpad * 3 * blocks, LANE)],
            micros=3,
        )[0])
        for p in range(others)
    ]

    splits = count // blocks
    vpart = ceil_to(-(-vpad // splits), 8)
    half_chunks = lambda rows: [hbm((count // 2, rows, LANE), F32)] * 2
    copies = 2
    hid, prev, src, keep_o, send_o, heads, head, o_sum, extra = call(
        functools.partial(cell_kernel, others=others, total_tokens=total_tokens, blocks=blocks),
        "cells",
        [marked],
        [tab, o_tab, seg, wt_own, bias_out, targets[None], ids[None]] + carries + tab_x + seg_x + wt_oth,
        [
            hbm((toks, width), BF16), chip(*tokens), hbm(tokens, F32),
            *half_chunks(vpart), chip(CHAINS * blocks, LANE), hbm((count, blocks, LANE), F32),
            chip(vpad, width), hbm((vpad, LANE), F32),
        ],
        [
            pltpu.VMEM(tokens, F32), pltpu.VMEM(tokens, F32), pltpu.VMEM((toks, width), BF16),
            pltpu.VMEM((toks, width), BF16), pltpu.VMEM((vpad, width), BF16), pltpu.VMEM((vpad, toks), F32), pltpu.VMEM(tokens, F32),
            pltpu.VMEM((vpad, toks), BF16), pltpu.SemaphoreType.DMA, pltpu.SemaphoreType.DMA((toks // 1024,)),
        ],
        limit=44,
        out_spaces=[pl.ANY, pltpu.VMEM, pl.ANY] + [pltpu.VMEM] * 6,
        micros=26,
    )
    prev, heads, o_sum = near(prev), near(heads), near(o_sum)
    part = ceil_to(-(-kdim // splits), 8)
    per = ceil_to(-(-vpad // count), 8)
    h_all = exchange(head, "ctx")
    got_o = swap(send_o, "ctx", 1)
    length = toks // CHAINS
    span = 32
    block = pl.BlockSpec((CHAINS, span * blocks, LANE), lambda i: (0, length // span - 1 - i, 0))
    (sums,) = call(
        functools.partial(char_sum_kernel, copies=copies, blocks=blocks),
        "char_sums",
        [marked, block_of],
        [tab, seg, heads, h_all, ps_all, prev, far(src.reshape(CHAINS, length * blocks, LANE))],
        [chip(2, vpad * blocks, LANE)],
        [pltpu.SMEM((count,), jnp.int32), pltpu.VMEM((CHAINS, blocks, LANE), F32)]
        + [pltpu.VMEM((vpad * blocks, LANE), F32)] * (2 * copies),
        limit=24,
        in_spaces=[pltpu.VMEM] * 6 + [block],
        micros=(9, length // span),
    )
    high, low, keep_e, send_e = call(
        functools.partial(gate_sum_kernel, count=count, vocab=vocab, blocks=blocks),
        "gate_sums",
        [spots],
        [near(sums), o_sum, table, w_own, extra],
        [pltpu.VMEM((gates, vpad, width), BF16)] * 2 + half_chunks(per),
        [pltpu.VMEM((2, vpad * blocks, LANE), F32)],
        limit=24,
        micros=3,
    )
    keep, send = call(
        functools.partial(input_grad_kernel, count=count, part=part, blocks=blocks),
        "input_grad",
        [],
        [near(high), near(low), table],
        half_chunks(4 * part),
        limit=24,
        micros=3,
    )
    sections = [[part] * gates + [vpart], [per]]
    apart = section_rows(sections[1])
    chunk = reduce_chunks(
        [keep, keep_o, keep_e], [swap(send, "ctx", 1), got_o, swap(send_e, "ctx", 1)], sections, "ctx"
    )
    halves, tail = gather_chunks(chunk, "ctx", apart)
    far_tails = [swap(tail, "wa", mask) for mask in range(1, wa)]
    w_grad, bi_grad, w_out_grad = call(
        functools.partial(finish_kernel, groups=sections[0], part=part, emb=emb),
        "finish",
        [],
        halves,
        [hbm((emb, gates, width), F32), hbm((gates, width), F32), hbm((vocab, width), F32)],
        micros=4,
    )
    far_tails = [after(v, bi_grad) for v in far_tails]
    tails = [tail] + [v for far_tail in far_tails for v in (far_tail, swap(far_tail, "ctx", 1))]
    e_grad, bo_grad, loss = call(
        functools.partial(embed_finish_kernel, groups=sections[1], shards=wa, total_tokens=total_tokens),
        "embed_finish",
        [],
        tails + [halves[3]],
        [hbm((vocab, emb), F32), hbm((1, vocab), F32), hbm((1, 1), F32)],
        [pltpu.VMEM((ceil_to(count * per, LANE), LANE), F32)],
    )
    return (
        hid,
        loss[0, 0],
        e_grad,
        w_grad,
        bi_grad,
        w_out_grad.T,
        bo_grad[0],
    )


def solution(mesh):
    placed = (
        P("ctx"),
        P("ctx"),
        P(),
        P(),
        P(),
        P(None, None, "wa"),
        P(None, "wa"),
        P("wa", None),
        P(),
    )
    return jax.shard_map(
        body,
        mesh=mesh,
        in_specs=placed,
        out_specs=(
            P("ctx", "wa"),
            P(),
            P(),
            P(None, None, "wa"),
            P(None, "wa"),
            P("wa", None),
            P(),
        ),
        check_vma=False,
    )
```
